256 devices in a mesh: ctx: 32 (over y, x, core), mp: 8 (over z).
Axes of the slice: x: 4, y: 4, z: 8, core: 2. Of those that a mesh axis runs over, the one named last changes fastest.
Arguments:
- tokens: bfloat16 [8192, 4096], P(('ctx', 'mp')), may hold values from -6 to 6
- branch: bfloat16 [8192, 4096], P('ctx', 'mp'), may hold values from -4 to 4
- out_grad: bfloat16 [8192, 4096], P(('ctx', 'mp')), may hold values from -24 to 24
- w_in: bfloat16 [4096, 4096], P(None, 'mp'), may hold values from -0.09375 to 0.09375
- conv_w: bfloat16 [4, 4096], P(None, 'mp'), may hold values from -3 to 3
- gate_a_w: bfloat16 [16, 256, 256], P('mp'), may hold values from -0.375 to 0.375
- gate_a_b: float32 [4096], P('mp'), may hold values from -4 to 4
- gate_i_w: bfloat16 [16, 256, 256], P('mp'), may hold values from -0.375 to 0.375
- gate_i_b: float32 [4096], P('mp'), may hold values from -4 to 4
- decay_param: float32 [4096], P('mp')
- w_out: bfloat16 [4096, 4096], P('mp'), may hold values from -0.09375 to 0.09375
- state_init: float32 [4096], P('mp'), may hold values from -5 to 5
- conv_history: bfloat16 [3, 4096], P(None, 'mp'), may hold values from -5 to 5
Outputs:
- tokens_grad: bfloat16 [8192, 4096], P(('ctx', 'mp'))
- branch_grad: bfloat16 [8192, 4096], P('ctx', 'mp')
- w_in_grad: float32 [4096, 4096], P('ctx', 'mp')
- w_out_grad: float32 [4096, 4096], P('mp', 'ctx')
- conv_w_grad: float32 [4, 4096], P(None, 'mp')
- gate_a_w_grad: float32 [16, 256, 256], P('mp')
- gate_a_b_grad: float32 [4096], P('mp')
- gate_i_w_grad: float32 [16, 256, 256], P('mp')
- gate_i_b_grad: float32 [4096], P('mp')
- decay_grad: float32 [4096], P('mp')
The draws below stay inside these ranges and needn't reach their ends.
All inputs are finite; a program needn't handle non-finite values.
Results may differ from the reference program's by a relative error of at most 0.02.
Values may be sent and summed in bfloat16 or wider, within the bound.
A program may use at most 128 MiB of HBM per device.

```python
import jax
import jax.numpy as jnp
from jax import lax

D = 4096
DR = 4096
H = 16
CONV = 4
TOK_DEV = 256
TOKENS = 8192
BLOCK = 256
N_CTX = 32
N_MP = 8


def draw_decay_param(key, part):
    key_kind, key_slow, key_fast = jax.random.split(key, 3)
    slow_share = 0.5
    slow = jax.random.uniform(key_kind, (DR,), jnp.float32) < slow_share
    fraction = jnp.exp(jax.random.uniform(key_slow, (DR,), jnp.float32, jnp.log(0.1), 0.0))
    slow_rate = fraction * (2.302585 / (8.0 * TOKENS))
    fast_rate = jnp.exp(jax.random.uniform(key_fast, (DR,), jnp.float32, jnp.log(0.005), jnp.log(0.1)))
    rate = jnp.where(slow, slow_rate, fast_rate)
    return (-jnp.log(jnp.expm1(rate))).astype(jnp.float32)


def with_spikes(values, key, source, target, shards_of, factor):
    owner, partner = [(jnp.arange(values.shape[dim]) // (values.shape[dim] // shards_of)).reshape([-1 if axis == dim else 1 for axis in range(values.ndim)]) for dim in (source, target)]
    chosen = jax.random.permutation(key, shards_of)[partner]
    strong = (owner == chosen) | (owner == (partner + shards_of // 2) % shards_of)
    return jnp.where(strong, factor * values, values)


def block_levels(rng, dims, cuts, smallest, top_value):
    level = 1.0
    for axis_at, parts in cuts:
        steps = jax.random.uniform(jax.random.fold_in(jax.random.fold_in(rng, 6), axis_at), (parts,), jnp.float32, smallest / len(cuts), top_value / len(cuts))
        level = level * jnp.repeat(jnp.exp(steps), dims[axis_at] // parts).reshape((-1,) + (1,) * (len(dims) - 1 - axis_at))
    return level


def bell_draw(own_key, shape, spread, most, shards=(), dtype=jnp.bfloat16):
    result = jax.random.normal(own_key, shape, jnp.float32) * spread
    if len(shards) > 0:
        result = block_levels(own_key, shape, shards, -0.22, 0.18) * result
    return jnp.clip(result, min=-most, max=most).astype(dtype)


def bell_draw_with(stream_key, extent, deviation, limit, cuts, heavy, dtype=jnp.bfloat16):
    array = deviation * jax.random.normal(stream_key, extent, jnp.float32)
    if cuts:
        array = array * block_levels(stream_key, extent, cuts, -0.22, 0.18)
    return jnp.clip(with_spikes(array, jax.random.fold_in(stream_key, 3), *heavy), -limit, limit).astype(dtype)


def setup_inputs(seed: int = 0) -> dict:
    key_list = jax.random.split(jax.random.key(seed), 14)
    tokens = bell_draw(key_list[0], (TOKENS, D), 1.0, 6.0, ((0, 256),))
    branch = bell_draw(key_list[1], (TOKENS, DR), 0.7, 4.0, ((0, 32), (1, 8)))
    out_grad = bell_draw_with(key_list[2], (TOKENS, D), 1.0, 24.0, ((0, 256),), (0, 1, 256, 6.0))
    w_in = bell_draw(key_list[3], (D, DR), D ** -0.5, 0.09375, ((1, 8),))
    conv_w = bell_draw(key_list[4], (CONV, DR), CONV ** -0.5, 3.0, ((1, 8),))
    gate_a_w = bell_draw(key_list[5], (H, BLOCK, BLOCK), BLOCK ** -0.5, 0.375, ((0, 8),))
    gate_a_b = bell_draw(key_list[6], (DR,), 1.0, 4.0, ((0, 8),), jnp.float32)
    gate_i_w = bell_draw(key_list[7], (H, BLOCK, BLOCK), BLOCK ** -0.5, 0.375, ((0, 8),))
    gate_i_b = bell_draw(key_list[8], (DR,), 1.0, 4.0, ((0, 8),), jnp.float32)
    decay_param = draw_decay_param(jax.random.fold_in(key_list[13], 71), 0)
    w_out = bell_draw(key_list[10], (DR, D), DR ** -0.5, 0.09375, ((0, 8),))
    state_init = bell_draw(key_list[11], (DR,), 1.0, 5.0, ((0, 8),), jnp.float32)
    conv_history = bell_draw(key_list[12], (CONV - 1, DR), 1.0, 5.0, ((1, 8),))
    return {"tokens": tokens, "branch": branch, "out_grad": out_grad, "w_in": w_in, "conv_w": conv_w, "gate_a_w": gate_a_w, "gate_a_b": gate_a_b, "gate_i_w": gate_i_w, "gate_i_b": gate_i_b, "decay_param": decay_param, "w_out": w_out, "state_init": state_init, "conv_history": conv_history}


def linear_step(state, pair):
    state = pair[0] * state + pair[1]
    return (state, state)

def adjoint_step(carry, pair):
    adjoint = pair[1] + carry
    return (pair[0] * adjoint, adjoint)

def rounded(value):
    return lax.optimization_barrier(value.astype(jnp.bfloat16)).astype(jnp.float32)

def run_sum(left, right):

    def add_run(total, pair):
        term = jnp.dot(pair[0].T, pair[1], preferred_element_type=jnp.float32)
        return (total + rounded(term), None)
    start = jnp.zeros((left.shape[2], right.shape[2]), jnp.float32)
    total, unused = lax.scan(add_run, start, (left, right))
    return total

def group_backward(tokens, branch, out_grad, w_in, conv_w, gate_a_w, gate_a_b, gate_i_w, gate_i_b, decay_param, w_out, state_init, conv_history):
    length = tokens.shape[0]
    channels = w_in.shape[1]
    blocks = gate_a_w.shape[0]
    block = gate_a_w.shape[1]
    taps = conv_w.shape[0]
    projected = jnp.dot(tokens, w_in, preferred_element_type=jnp.float32).astype(jnp.bfloat16)
    extended = jnp.concatenate([conv_history, projected], 0).astype(jnp.float32)
    kernel = conv_w.astype(jnp.float32)
    conv_sum = jnp.zeros((length, channels), jnp.float32)
    for shift_by in range(taps):
        conv_sum = conv_sum + kernel[shift_by] * extended[taps - 1 - shift_by:taps - 1 - shift_by + length]
    conv_out = conv_sum.astype(jnp.bfloat16)
    conv_wide = conv_out.astype(jnp.float32)
    conv_blocks = conv_wide.reshape(length, blocks, block)
    gate_a = gate_a_w.astype(jnp.float32)
    gate_i = gate_i_w.astype(jnp.float32)
    recur_gate = jax.nn.sigmoid(jnp.einsum('thb,hbc->thc', conv_blocks, gate_a).reshape(length, channels) + gate_a_b)
    input_gate = jax.nn.sigmoid(jnp.einsum('thb,hbc->thc', conv_blocks, gate_i).reshape(length, channels) + gate_i_b)
    softrate = jax.nn.softplus(-decay_param)
    log_decay = -8.0 * recur_gate * softrate
    decay = jnp.exp(log_decay)
    remain = -jnp.expm1(2.0 * log_decay)
    scaler = jnp.sqrt(remain)
    driven = scaler * input_gate * conv_wide
    final_state, states = lax.scan(linear_step, state_init, (decay, driven))
    branch_wide = branch.astype(jnp.float32)
    gated_out = (states * branch_wide).astype(jnp.bfloat16)
    grad_gated = jnp.dot(out_grad, w_out.T, preferred_element_type=jnp.float32)
    branch_grad = (grad_gated * states).astype(jnp.bfloat16)
    state_grad = grad_gated * branch_wide
    last_carry, adjoint = lax.scan(adjoint_step, jnp.zeros((channels,), jnp.float32), (decay, state_grad), reverse=True)
    previous = jnp.concatenate([state_init[None], states[:-1]], 0)
    scaler_grad = adjoint * input_gate * conv_wide
    log_grad = adjoint * previous * decay - 2.0 * decay * decay * scaler_grad / jnp.sqrt(jnp.maximum(4.0 * remain, 1e-06))
    recur_pre = (log_grad * (-8.0 * softrate) * recur_gate * (1.0 - recur_gate)).astype(jnp.bfloat16)
    input_pre = (adjoint * scaler * conv_wide * input_gate * (1.0 - input_gate)).astype(jnp.bfloat16)
    recur_blocks = recur_pre.astype(jnp.float32).reshape(length, blocks, block)
    input_blocks = input_pre.astype(jnp.float32).reshape(length, blocks, block)
    gate_a_w_grad = jnp.einsum('thb,thc->hbc', conv_blocks, recur_blocks)
    gate_i_w_grad = jnp.einsum('thb,thc->hbc', conv_blocks, input_blocks)
    gate_a_b_grad = lax.optimization_barrier(jnp.sum(recur_pre.astype(jnp.float32), 0))
    gate_i_b_grad = lax.optimization_barrier(jnp.sum(input_pre.astype(jnp.float32), 0))
    decay_grad = lax.optimization_barrier(jnp.sum(log_grad * (-8.0 * recur_gate), 0)) * -jax.nn.sigmoid(-decay_param)
    conv_grad = adjoint * scaler * input_gate
    conv_grad = conv_grad + jnp.einsum('thc,hbc->thb', recur_blocks, gate_a).reshape(length, channels)
    conv_grad = conv_grad + jnp.einsum('thc,hbc->thb', input_blocks, gate_i).reshape(length, channels)
    padded = jnp.concatenate([conv_grad, jnp.zeros((taps - 1, channels), jnp.float32)], 0)
    proj_sum = jnp.zeros((length, channels), jnp.float32)
    tap_grads = []
    for shift_by in range(taps):
        proj_sum = proj_sum + kernel[shift_by] * padded[shift_by:shift_by + length]
        tap_grads.append(lax.optimization_barrier(jnp.sum(conv_grad * extended[taps - 1 - shift_by:taps - 1 - shift_by + length], 0)))
    proj_grad = proj_sum.astype(jnp.bfloat16)
    conv_w_grad = jnp.stack(tap_grads, 0)
    return (branch_grad, proj_grad, gated_out, conv_w_grad, gate_a_w_grad, gate_a_b_grad, gate_i_w_grad, gate_i_b_grad, decay_grad)

def reference(tokens, branch, out_grad, w_in, conv_w, gate_a_w, gate_a_b, gate_i_w, gate_i_b, decay_param, w_out, state_init, conv_history):
    channels = DR // N_MP
    blocks = H // N_MP
    token_runs = tokens.reshape(N_CTX, TOK_DEV, D)
    grad_runs = out_grad.reshape(N_CTX, TOK_DEV, D)
    tokens_total = jnp.zeros((TOKENS, D), jnp.float32)
    collected = []
    for group in range(N_MP):
        low = group * channels
        high = low + channels
        w_in_group = w_in[:, low:high]
        results = group_backward(tokens, branch[:, low:high], out_grad, w_in_group, conv_w[:, low:high], gate_a_w[group * blocks:(group + 1) * blocks], gate_a_b[low:high], gate_i_w[group * blocks:(group + 1) * blocks], gate_i_b[low:high], decay_param[low:high], w_out[low:high], state_init[low:high], conv_history[:, low:high])
        proj_grad = results[1]
        gated_out = results[2]
        tokens_total = tokens_total + rounded(jnp.dot(proj_grad, w_in_group.T, preferred_element_type=jnp.float32))
        w_in_grad = run_sum(token_runs, proj_grad.reshape(N_CTX, TOK_DEV, channels))
        w_out_grad = run_sum(gated_out.reshape(N_CTX, TOK_DEV, channels), grad_runs)
        collected.append((results[0], w_in_grad, w_out_grad) + results[3:])
    branch_grad = jnp.concatenate([item[0] for item in collected], 1)
    w_in_grad = jnp.concatenate([item[1] for item in collected], 1)
    w_out_grad = jnp.concatenate([item[2] for item in collected], 0)
    conv_w_grad = jnp.concatenate([item[3] for item in collected], 1)
    gate_a_w_grad = jnp.concatenate([item[4] for item in collected], 0)
    gate_a_b_grad = jnp.concatenate([item[5] for item in collected], 0)
    gate_i_w_grad = jnp.concatenate([item[6] for item in collected], 0)
    gate_i_b_grad = jnp.concatenate([item[7] for item in collected], 0)
    decay_grad = jnp.concatenate([item[8] for item in collected], 0)
    tokens_grad = tokens_total.astype(jnp.bfloat16)
    return (tokens_grad, branch_grad, w_in_grad, w_out_grad, conv_w_grad, gate_a_w_grad, gate_a_b_grad, gate_i_w_grad, gate_i_b_grad, decay_grad)
```

```python
import jax
import jax.numpy as jnp
from jax import lax
from jax.experimental import pallas as pl
from jax.experimental.pallas import tpu as pltpu
from jax.sharding import PartitionSpec as P

MESH = pl.DeviceIdType.MESH
F32 = jnp.float32
BF16 = jnp.bfloat16
NMP = 8
SEG = 32
CH = 512
DM = 4096
HALF = DM // 2


def matmul_tn(left, right):
    return lax.dot_general(left, right, (((0,), (0,)), ((), ())), preferred_element_type=F32)


def matmul_nt(left, right):
    return lax.dot_general(left, right, (((1,), (1,)), ((), ())), preferred_element_type=F32)


def to_segments(value):
    return jnp.transpose(value.reshape(NMP, SEG, CH), (1, 0, 2))


def from_segments(value):
    return jnp.transpose(value, (1, 0, 2)).reshape(NMP * SEG, CH)


def remote(src, dst, send_sem, recv_sem, device):
    return pltpu.make_async_remote_copy(
        src_ref=src,
        dst_ref=dst,
        send_sem=send_sem,
        recv_sem=recv_sem,
        device_id=device,
        device_id_type=MESH,
    )


class Place:
    def __init__(self):
        self.c = lax.axis_index("ctx")
        self.m = lax.axis_index("mp")
        self.k = lax.rem(self.c, 2)
        self.x = lax.rem(lax.div(self.c, 2), 4)
        self.y = lax.div(self.c, 8)

    def chip(self, y, x, k):
        return (y * 8 + x * 2 + k, self.m)

    def other_core(self):
        return self.chip(self.y, self.x, 1 - self.k)

    def along_x(self, step):
        return self.chip(self.y, lax.rem(self.x + step, 4), self.k)

    def along_y(self, step):
        return self.chip(lax.rem(self.y + step, 4), self.x, self.k)

    def along_z(self, step):
        return (self.c, lax.rem(self.m + step, NMP))

    def along_ctx(self, step):
        return (lax.rem(self.c + step, 32), self.m)


class Gather:
    def __init__(self, place, buf, send_sem, recv_sem):
        self.p, self.buf, self.ss, self.rs = place, buf, send_sem, recv_sem

    def view(self, d, s, part):
        step = (NMP - s) if d == 0 else s
        return self.buf.at[lax.rem(self.p.m + step, NMP), :, pl.ds(part * HALF, HALF)]

    def copy(self, d, s, part, at):
        view = self.view(d, at, part)
        to = self.p.along_z(1 if d == 0 else NMP - 1)
        return remote(view, view, self.ss.at[d, s, part], self.rs.at[d, s, part], to)

    def present(self, d, s, part):
        return s < 3 or part == d

    def send(self, s):
        for part in (0, 1):
            for d in (0, 1):
                if self.present(d, s, part):
                    self.copy(d, s, part, s).start()

    def arrive(self, s):
        for part in (0, 1):
            for d in (0, 1):
                if self.present(d, s, part):
                    self.copy(d, s, part, s + 1).wait_recv()
                    if s < 3 and self.present(d, s + 1, part):
                        self.copy(d, s + 1, part, s + 1).start()

    def sent(self):
        for s in range(4):
            for part in (0, 1):
                for d in (0, 1):
                    if self.present(d, s, part):
                        self.copy(d, s, part, s).wait_send()


class Fold:
    def __init__(self, place, core, row, col, send_sem, recv_sem):
        self.p = place
        self.slots = (core, row, col)
        self.ss, self.rs = send_sem, recv_sem

    def stage(self, which, value):
        p, slots = self.p, self.slots[which]
        mine = (p.k, p.x, p.y)[which]
        slots[mine] = value
        size = 2 if which == 0 else 4
        base = (0, 1, 4)[which]
        out = []
        for o in range(1, size):
            to = p.other_core() if which == 0 else (p.along_x(o) if which == 1 else p.along_y(o))
            send = remote(
                slots.at[mine], slots.at[mine], self.ss.at[base + o - 1], self.rs.at[base + o - 1], to
            )
            send.start()
            out.append((o, to))
        for o, to in out:
            came = lax.rem(mine + size - o, size)
            remote(
                slots.at[came], slots.at[came], self.ss.at[base + o - 1], self.rs.at[base + o - 1], to
            ).wait_recv()
        return out, mine, base

    def done(self, started):
        out, mine, base, which = started
        slots = self.slots[which]
        for o, to in out:
            remote(
                slots.at[mine], slots.at[mine], self.ss.at[base + o - 1], self.rs.at[base + o - 1], to
            ).wait_send()


def minus_expm1(v):
    series = 1.0 + v * (1.0 / 8.0)
    for n in (7, 6, 5, 4, 3, 2):
        series = 1.0 + v * (1.0 / n) * series
    return jnp.where(v > -0.35, -v * series, 1.0 - jnp.exp(v))


def enter(place, partners):
    barrier = pltpu.get_barrier_semaphore()
    for device in partners:
        pl.semaphore_signal(barrier, inc=1, device_id=device, device_id_type=MESH)
    pl.semaphore_wait(barrier, len(partners))


def first_kernel(
    tokens, branch, out_grad, w_in, conv_w, gate_a, gate_a_b, gate_i, gate_i_b, decay_param, w_out,
    state_init, conv_history,
    branch_grad, tok, og, proj_out, gated, conv_b, recur_b, input_b, small,
    w_in_v, w_out_v, acc, px, cv, rg, ig, dk, rem, hs, cp, ep, br, gp, cg, kv, edge_s, edge_r, edge_c,
    core_s, row_s, col_s, core_b, row_b, col_b,
    w_sem, ts, tr, gs, gr, fs, fr, bs, brs, es, er,
):
    p = Place()
    loads = [
        pltpu.make_async_copy(w_in, w_in_v, w_sem.at[0]),
        pltpu.make_async_copy(w_out, w_out_v, w_sem.at[1]),
    ]
    for load in loads:
        load.start()
    tok[p.m] = tokens[...]
    og[p.m] = out_grad[...]
    enter(
        p,
        [p.along_z(1), p.along_z(NMP - 1), p.along_ctx(1), p.along_ctx(31), p.other_core()]
        + [p.along_x(o) for o in (1, 2, 3)]
        + [p.along_y(o) for o in (1, 2, 3)],
    )
    tokens_in = Gather(p, tok, ts, tr)
    grads_in = Gather(p, og, gs, gr)
    tokens_in.send(0)

    def wide(row):
        return jnp.broadcast_to(row.reshape(1, CH), (8, CH))

    taps = conv_w[...].astype(F32)
    for j in range(4):
        kv[j] = wide(taps[j : j + 1])
    kv[4] = wide(gate_a_b[...])
    kv[5] = wide(gate_i_b[...])
    negative = wide(-decay_param[...])
    small_exp = jnp.exp(-jnp.abs(negative))
    one_more = 1.0 + small_exp
    gap = one_more - 1.0
    log_part = jnp.where(
        gap == 0.0, small_exp, jnp.log(one_more) * (small_exp / jnp.where(gap == 0.0, 1.0, gap))
    )
    kv[6] = jnp.maximum(negative, 0.0) + log_part
    br[...] = to_segments(branch[...].astype(F32))

    for s in (0, 1, 2):
        tokens_in.arrive(s)
    grads_in.send(0)
    loads[0].wait()
    tokens_in.arrive(3)

    acc[...] = jnp.zeros_like(acc)

    def project(n, carry):
        at = pl.ds(pl.multiple_of(n * 512, 512), 512)
        acc[...] += jnp.dot(
            tok[:, :, at].reshape(256, 512), w_in_v[at, :], preferred_element_type=F32
        )
        return carry

    lax.fori_loop(0, 8, project, 0)
    edge_s[...] = acc[pl.ds(240, 16), :].astype(BF16)
    forward_edge = remote(edge_s, edge_r, es.at[0], er.at[0], p.along_ctx(1))
    forward_edge.start()
    px[pl.ds(3, 32)] = to_segments(acc[...].astype(BF16).astype(F32))
    grads_in.arrive(0)

    lane8 = lax.broadcasted_iota(jnp.int32, (8, CH), 0)
    forward_edge.wait_recv()
    first = p.c == 0
    before = edge_r[...].astype(F32)[13:16]
    before = jnp.where(first, conv_history[...].astype(F32), before)
    for j in range(3):
        turned = pltpu.roll(px[32 + j], 1, 0)
        px[j] = jnp.where(lane8 == 0, wide(before[j : j + 1]), turned)

    def convolve(n, carry):
        total = kv[0] * px[pl.ds(2 * n + 3, 2)]
        for j in (1, 2, 3):
            total = total + kv[j] * px[pl.ds(2 * n + 3 - j, 2)]
        rounded = total.astype(BF16)
        cv[pl.ds(2 * n, 2)] = rounded.astype(F32)
        conv_b[pl.ds(pl.multiple_of(16 * n, 16), 16), :] = rounded.reshape(16, CH)
        return carry

    lax.fori_loop(0, 16, convolve, 0)
    for b in (0, 1):
        cols = pl.ds(b * 256, 256)
        rg[:, :, cols] = jnp.dot(
            conv_b[:, cols], gate_a[b], preferred_element_type=F32
        ).reshape(32, 8, 256)
        ig[:, :, cols] = jnp.dot(
            conv_b[:, cols], gate_i[b], preferred_element_type=F32
        ).reshape(32, 8, 256)

    def gates(n, carry):
        h, c = carry
        at = pl.ds(2 * n, 2)
        recur = jax.nn.sigmoid(rg[at] + kv[4])
        inp = jax.nn.sigmoid(ig[at] + kv[5])
        log_decay = -8.0 * recur * kv[6]
        decay = jnp.exp(log_decay)
        remain = minus_expm1(2.0 * log_decay)
        rg[at] = recur
        ig[at] = inp
        dk[at] = decay
        rem[at] = remain
        driven = jnp.sqrt(remain) * inp * cv[at]
        for t in (0, 1):
            h = decay[t] * h + driven[t]
            c = decay[t] * c
            hs[2 * n + 1 + t] = h
            cp[2 * n + t] = c
        return h, c

    h, c = lax.fori_loop(0, 16, gates, (jnp.zeros((8, CH), F32), jnp.ones((8, CH), F32)))
    c_seg = c
    for sh in (1, 2, 4):
        ok = lane8 >= sh
        h, c = (
            jnp.where(ok, h + c * pltpu.roll(h, sh, 0), h),
            jnp.where(ok, c * pltpu.roll(c, sh, 0), c),
        )
    c_before = jnp.where(lane8 == 0, 1.0, pltpu.roll(c, 1, 0))
    h_before = jnp.where(lane8 == 0, 0.0, pltpu.roll(h, 1, 0))
    states = Fold(p, core_s, row_s, col_s, fs, fr)
    pair = jnp.where(lane8 < 4, wide(c[7:8]), wide(h[7:8]))

    def both(slot):
        value = slot
        return wide(value[0:1]), wide(value[4:5])

    held = [states.stage(0, pair) + (0,)]
    grads_in.arrive(1)

    def suffix(n, e):
        ep[31 - n] = e
        return e * dk[31 - n]

    lax.fori_loop(0, 32, suffix, jnp.ones((8, CH), F32))
    c0, h0 = both(core_s[0])
    c1, h1 = both(core_s[1])
    held.append(states.stage(1, jnp.where(lane8 < 4, c0 * c1, c1 * h0 + h1)) + (1,))
    cr, hr = jnp.ones((8, CH), F32), jnp.zeros((8, CH), F32)
    for o in range(4):
        co, ho = both(row_s[o])
        cr, hr = cr * co, co * hr + ho
    held.append(states.stage(2, jnp.where(lane8 < 4, cr, hr)) + (2,))
    state = wide(state_init[...])
    for o in range(4):
        co, ho = both(col_s[o])
        state = jnp.where(o < p.y, co * state + ho, state)
    for o in range(4):
        co, ho = both(row_s[o])
        state = jnp.where(o < p.x, co * state + ho, state)
    state = jnp.where(p.k == 1, c0 * state + h0, state)
    seg_state = h_before + c_before * state
    hs[0] = seg_state

    def finish_states(n, carry):
        at = pl.ds(2 * n, 2)
        value = hs[pl.ds(2 * n + 1, 2)] + cp[at] * seg_state
        hs[pl.ds(2 * n + 1, 2)] = value
        cp[at] = value * br[at]
        return carry

    lax.fori_loop(0, 16, finish_states, 0)
    gated[...] = from_segments(cp[...]).astype(BF16)

    grads_in.arrive(2)
    loads[1].wait()
    grads_in.arrive(3)
    acc[...] = jnp.zeros_like(acc)

    def grad_product(n, carry):
        at = pl.ds(pl.multiple_of(n * 512, 512), 512)
        acc[...] += matmul_nt(og[:, :, at].reshape(256, 512), w_out_v[:, at])
        return carry

    lax.fori_loop(0, 8, grad_product, 0)
    gp[...] = to_segments(acc[...])

    def backward(n, b):
        i = 31 - n
        g = gp[i]
        cp[i] = g * hs[i + 1]
        a = g * br[i] + b
        gp[i] = a
        return dk[i] * a

    b = lax.fori_loop(0, 32, backward, jnp.zeros((8, CH), F32))
    c = c_seg
    for sh in (1, 2, 4):
        ok = lane8 < 8 - sh
        b, c = (
            jnp.where(ok, b + c * pltpu.roll(b, 8 - sh, 0), b),
            jnp.where(ok, c * pltpu.roll(c, 8 - sh, 0), c),
        )
    c_after = jnp.where(lane8 == 7, 1.0, pltpu.roll(c, 7, 0))
    b_after = jnp.where(lane8 == 7, 0.0, pltpu.roll(b, 7, 0))
    adjoints = Fold(p, core_b, row_b, col_b, bs, brs)
    held_b = [adjoints.stage(0, wide(b[0:1])) + (0,)]
    b0, b1 = core_b[0], core_b[1]
    held_b.append(adjoints.stage(1, b0 + c0 * b1) + (1,))
    row = jnp.zeros((8, CH), F32)
    for o in (3, 2, 1, 0):
        row = row_b[o] + both(row_s[o])[0] * row
    held_b.append(adjoints.stage(2, row) + (2,))
    branch_grad[...] = from_segments(cp[...]).astype(BF16)
    later = jnp.zeros((8, CH), F32)
    for o in (3, 2, 1, 0):
        later = jnp.where(o > p.y, col_b[o] + both(col_s[o])[0] * later, later)
    for o in (3, 2, 1, 0):
        later = jnp.where(o > p.x, row_b[o] + both(row_s[o])[0] * later, later)
    later = jnp.where(p.k == 0, b1 + c1 * later, later)
    seg_later = b_after + c_after * later

    def gate_grads(n, carry):
        sum_a, sum_i, sum_r = carry
        at = pl.ds(2 * n, 2)
        adjoint = gp[at] + ep[at] * seg_later
        decay, remain, inp, recur, wide_conv = dk[at], rem[at], ig[at], rg[at], cv[at]
        scaler = jnp.sqrt(remain)
        scaler_grad = adjoint * inp * wide_conv
        log_grad = adjoint * hs[at] * decay - 2.0 * decay * decay * scaler_grad / jnp.sqrt(
            jnp.maximum(4.0 * remain, 1e-06)
        )
        recur_pre = (log_grad * (-8.0 * kv[6]) * recur * (1.0 - recur)).astype(BF16)
        input_pre = (scaler_grad * scaler * (1.0 - inp)).astype(BF16)
        flat = pl.ds(pl.multiple_of(16 * n, 16), 16)
        recur_b[flat, :] = recur_pre.reshape(16, CH)
        input_b[flat, :] = input_pre.reshape(16, CH)
        cg[at] = adjoint * scaler * inp
        return (
            sum_a + jnp.sum(recur_pre.astype(F32), 0),
            sum_i + jnp.sum(input_pre.astype(F32), 0),
            sum_r + jnp.sum(log_grad * (-8.0 * recur), 0),
        )

    zero = jnp.zeros((8, CH), F32)
    sum_a, sum_i, sum_r = lax.fori_loop(0, 16, gate_grads, (zero, zero, zero))
    for b in (0, 1):
        cols = pl.ds(b * 256, 256)
        cg[pl.ds(0, 32), :, cols] += (
            matmul_nt(recur_b[:, cols], gate_a[b]) + matmul_nt(input_b[:, cols], gate_i[b])
        ).reshape(32, 8, 256)
    backward_edge = remote(cg.at[pl.ds(0, 3)], edge_c, es.at[1], er.at[1], p.along_ctx(31))
    backward_edge.start()
    backward_edge.wait_recv()
    for j in range(3):
        turned = pltpu.roll(cg[j], 7, 0)
        came = jnp.where(p.c == 31, 0.0, wide(edge_c[j][0:1]))
        cg[32 + j] = jnp.where(lane8 == 7, came, turned)

    def proj_grads(n, carry):
        at = pl.ds(2 * n, 2)
        own = cg[at]
        total = kv[0] * own
        for j in (1, 2, 3):
            total = total + kv[j] * cg[pl.ds(2 * n + j, 2)]
        cp[at] = total
        return tuple(
            carry[j] + jnp.sum(own * px[pl.ds(2 * n + 3 - j, 2)], 0) for j in range(4)
        )

    tap_sums = lax.fori_loop(0, 16, proj_grads, (zero, zero, zero, zero))
    proj_out[...] = from_segments(cp[...]).astype(BF16)
    rows = [jnp.sum(v, 0, keepdims=True) for v in (*tap_sums, sum_r, sum_a, sum_i)]
    small[...] = jnp.concatenate(rows + [jnp.zeros((1, CH), F32)], 0)

    tokens_in.sent()
    grads_in.sent()
    for started in held:
        states.done(started)
    for started in held_b:
        adjoints.done(started)
    forward_edge.wait_send()
    backward_edge.wait_send()


def call_first(*args):
    def vm(shape, dtype):
        return pltpu.VMEM(shape, dtype)

    seg = (32, 8, CH)
    tile = (8, CH)
    dma = pltpu.SemaphoreType.DMA
    S = jax.ShapeDtypeStruct
    outs = (
        S((256, CH), BF16),
        S((8, 32, DM), BF16),
        S((8, 32, DM), BF16),
        S((256, CH), BF16),
        S((256, CH), BF16),
        S((256, CH), BF16),
        S((256, CH), BF16),
        S((256, CH), BF16),
        S((8, CH), F32),
    )
    big = {3, 10}
    return pl.pallas_call(
        first_kernel,
        out_shape=outs,
        in_specs=[
            pl.BlockSpec(memory_space=pl.ANY if n in big else pltpu.VMEM) for n in range(13)
        ],
        out_specs=tuple(pl.BlockSpec(memory_space=pltpu.VMEM) for _ in outs),
        scratch_shapes=[
            vm((DM, CH), BF16),
            vm((CH, DM), BF16),
            vm((256, CH), F32),
            vm((35, 8, CH), F32),
            *[vm(seg, F32) for _ in range(5)],
            vm((33, 8, CH), F32),
            *[vm(seg, F32) for _ in range(4)],
            vm((35, 8, CH), F32),
            vm((7, 8, CH), F32),
            vm((16, CH), BF16),
            vm((16, CH), BF16),
            vm((3, 8, CH), F32),
            vm((2, *tile), F32),
            vm((4, *tile), F32),
            vm((4, *tile), F32),
            vm((2, *tile), F32),
            vm((4, *tile), F32),
            vm((4, *tile), F32),
            dma((2,)),
            dma((2, 4, 2)),
            dma((2, 4, 2)),
            dma((2, 4, 2)),
            dma((2, 4, 2)),
            dma((7,)),
            dma((7,)),
            dma((7,)),
            dma((7,)),
            dma((2,)),
            dma((2,)),
        ],
        compiler_params=pltpu.CompilerParams(
            collective_id=0, has_side_effects=True, vmem_limit_bytes=56 << 20
        ),
    )(*args)


def cut_along(value, dim, peers):
    lengths = value.shape
    parts = value.reshape(*lengths[:dim], peers, lengths[dim] // peers, *lengths[dim + 1 :])
    return jnp.moveaxis(parts, dim, 0)


def sum_at_owner(value, axis, dim):
    peers = lax.axis_size(axis)
    parts = lax.all_to_all(cut_along(value, dim, peers), axis, 0, 0, tiled=True)
    return jnp.sum(parts.astype(jnp.float32), axis=0)


def one_scatter(arrays, axis, dims):
    peers = lax.axis_size(axis)
    parts = [cut_along(a, dim, peers) for a, dim in zip(arrays, dims)]
    lines = jnp.concatenate([b.reshape(peers, -1) for b in parts], axis=1)
    rows = max(16, -(-lines.shape[1] // 1024) * 8)
    lines = jnp.pad(lines, ((0, 0), (0, rows * 128 - lines.shape[1]))).reshape(-1, 128)
    ravelled, at, gathered = (lax.psum_scatter(lines, axis, tiled=True).reshape(-1), 0, [])
    for b in parts:
        part = b[0]
        gathered.append(ravelled[at : at + part.size].reshape(part.shape))
        at += part.size
    return tuple(gathered)


def shards(tokens, branch, out_grad, w_in, conv_w, gate_a_w, gate_a_b, gate_i_w, gate_i_b, decay_param, w_out, state_init, conv_history):
    branch_grad, tok, og, proj_grad, gated_out, conv_out, recur_pre, input_pre, small = call_first(
        tokens, branch, out_grad, w_in, conv_w, gate_a_w, gate_a_b, gate_i_w, gate_i_b, decay_param,
        w_out, state_init, conv_history,
    )
    token_block, grad_block = tok.reshape(256, DM), og.reshape(256, DM)
    conv_blocks = conv_out.reshape(256, 2, 256)
    recur_blocks = recur_pre.reshape(256, 2, 256)
    input_blocks = input_pre.reshape(256, 2, 256)
    gate_a_local = jnp.einsum("thb,thc->hbc", conv_blocks, recur_blocks, preferred_element_type=F32)
    gate_i_local = jnp.einsum("thb,thc->hbc", conv_blocks, input_blocks, preferred_element_type=F32)
    sums = lax.psum(small, "ctx")
    gate_a_w_grad = lax.psum(gate_a_local.astype(BF16), "ctx").astype(F32)
    gate_i_w_grad = lax.psum(gate_i_local.astype(BF16), "ctx").astype(F32)
    conv_w_grad, rate_total, gate_a_b_grad, gate_i_b_grad = sums[:4], sums[4], sums[5], sums[6]
    decay_grad = rate_total * -jax.nn.sigmoid(-decay_param)
    tokens_grad = sum_at_owner(matmul_nt(proj_grad, w_in).astype(jnp.bfloat16), "mp", 0).astype(
        jnp.bfloat16
    )
    w_in_grad, w_out_grad = tuple(
        (
            part.astype(jnp.float32)
            for part in one_scatter(
                (
                    matmul_tn(token_block, proj_grad).astype(jnp.bfloat16),
                    matmul_tn(gated_out, grad_block).astype(jnp.bfloat16),
                ),
                "ctx",
                (0, 1),
            )
        )
    )
    return (
        tokens_grad,
        branch_grad,
        w_in_grad,
        w_out_grad,
        conv_w_grad,
        gate_a_w_grad,
        gate_a_b_grad,
        gate_i_w_grad,
        gate_i_b_grad,
        decay_grad,
    )


def solution(mesh):
    placed = (
        P(("ctx", "mp"), None),
        P("ctx", "mp"),
        P(("ctx", "mp"), None),
        P(None, "mp"),
        P(None, "mp"),
        P("mp", None, None),
        P("mp"),
        P("mp", None, None),
        P("mp"),
        P("mp"),
        P("mp", None),
        P("mp"),
        P(None, "mp"),
    )
    return jax.shard_map(
        shards,
        mesh=mesh,
        in_specs=placed,
        out_specs=(
            P(("ctx", "mp"), None),
            P("ctx", "mp"),
            P("ctx", "mp"),
            P("mp", "ctx"),
            P(None, "mp"),
            P("mp", None, None),
            P("mp"),
            P("mp", None, None),
            P("mp"),
            P("mp"),
        ),
        check_vma=False,
    )
```

```python
import jax
import jax.numpy as jnp
from jax import lax
from jax.experimental import pallas as pl
from jax.experimental.pallas import tpu as pltpu
from jax.sharding import PartitionSpec as P

MESH = pl.DeviceIdType.MESH
F32 = jnp.float32
BF16 = jnp.bfloat16
NMP = 8
SEG = 32
CH = 512
DM = 4096
HALF = DM // 2


def matmul_tn(left, right):
    return lax.dot_general(left, right, (((0,), (0,)), ((), ())), preferred_element_type=F32)


def matmul_nt(left, right):
    return lax.dot_general(left, right, (((1,), (1,)), ((), ())), preferred_element_type=F32)


def to_segments(value):
    return jnp.transpose(value.reshape(NMP, SEG, CH), (1, 0, 2))


def from_segments(value):
    return jnp.transpose(value, (1, 0, 2)).reshape(NMP * SEG, CH)


def remote(src, dst, send_sem, recv_sem, device):
    return pltpu.make_async_remote_copy(
        src_ref=src,
        dst_ref=dst,
        send_sem=send_sem,
        recv_sem=recv_sem,
        device_id=device,
        device_id_type=MESH,
    )


class Place:
    def __init__(self):
        self.c = lax.axis_index("ctx")
        self.m = lax.axis_index("mp")
        self.k = lax.rem(self.c, 2)
        self.x = lax.rem(lax.div(self.c, 2), 4)
        self.y = lax.div(self.c, 8)

    def chip(self, y, x, k):
        return (y * 8 + x * 2 + k, self.m)

    def other_core(self):
        return self.chip(self.y, self.x, 1 - self.k)

    def along_x(self, step):
        return self.chip(self.y, lax.rem(self.x + step, 4), self.k)

    def along_y(self, step):
        return self.chip(lax.rem(self.y + step, 4), self.x, self.k)

    def along_z(self, step):
        return (self.c, lax.rem(self.m + step, NMP))

    def along_ctx(self, step):
        return (lax.rem(self.c + step, 32), self.m)


class Gather:
    def __init__(self, place, buf, send_sem, recv_sem):
        self.p, self.buf, self.ss, self.rs = place, buf, send_sem, recv_sem

    def view(self, d, s, part):
        step = (NMP - s) if d == 0 else s
        return self.buf.at[lax.rem(self.p.m + step, NMP), :, pl.ds(part * HALF, HALF)]

    def copy(self, d, s, part, at):
        view = self.view(d, at, part)
        to = self.p.along_z(1 if d == 0 else NMP - 1)
        return remote(view, view, self.ss.at[d, s, part], self.rs.at[d, s, part], to)

    def present(self, d, s, part):
        return s < 3 or part == d

    def send(self, s):
        for part in (0, 1):
            for d in (0, 1):
                if self.present(d, s, part):
                    self.copy(d, s, part, s).start()

    def arrive(self, s):
        for part in (0, 1):
            for d in (0, 1):
                if self.present(d, s, part):
                    self.copy(d, s, part, s + 1).wait_recv()
                    if s < 3 and self.present(d, s + 1, part):
                        self.copy(d, s + 1, part, s + 1).start()

    def sent(self):
        for s in range(4):
            for part in (0, 1):
                for d in (0, 1):
                    if self.present(d, s, part):
                        self.copy(d, s, part, s).wait_send()


class Fold:
    def __init__(self, place, core, row, col, send_sem, recv_sem):
        self.p = place
        self.slots = (core, row, col)
        self.ss, self.rs = send_sem, recv_sem

    def copies(self, which, arriving):
        p, slots = self.p, self.slots[which]
        mine = (p.k, p.x, p.y)[which]
        size = 2 if which == 0 else 4
        base = (0, 1, 4)[which]
        found = []
        for o in range(1, size):
            to = p.other_core() if which == 0 else (p.along_x(o) if which == 1 else p.along_y(o))
            slot = slots.at[lax.rem(mine + size - o, size) if arriving else mine]
            sems = self.ss.at[base + o - 1], self.rs.at[base + o - 1]
            found.append(remote(slot, slot, *sems, to))
        return found

    def start(self, which, value):
        self.slots[which][(self.p.k, self.p.x, self.p.y)[which]] = value
        for copy in self.copies(which, False):
            copy.start()

    def finish(self, which):
        for copy in self.copies(which, True):
            copy.wait_recv()

    def drain(self):
        for which in range(3):
            for copy in self.copies(which, False):
                copy.wait_send()


class CorePair:
    def __init__(self, place, src, dst, send_sem, recv_sem):
        self.copy = remote(src, dst, send_sem, recv_sem, place.other_core())
        self.start, self.finish, self.drain = (
            self.copy.start, self.copy.wait_recv, self.copy.wait_send
        )


class CoreColumns:
    def __init__(self, place, own, other, send_sem, recv_sem):
        self.p, self.own, self.other = place, own, other
        self.ss, self.rs = send_sem, recv_sem
        self.whole = remote(other, other, send_sem, recv_sem, place.other_core())

    def start(self):
        def one(j, carry):
            src = pl.ds(pl.multiple_of((2 * j + 1 - self.p.k) * 128, 128), 128)
            dst = pl.ds(pl.multiple_of(j * 128, 128), 128)
            remote(
                self.own.at[:, :, src], self.other.at[:, :, dst], self.ss, self.rs,
                self.p.other_core(),
            ).start()
            return carry

        lax.fori_loop(0, 16, one, 0)

    def finish(self):
        self.whole.wait_recv()

    def drain(self):
        self.whole.wait_send()


class WeightSum:
    def __init__(self, place, first_x, lhs, own, other, refs):
        self.p, self.first_x = place, first_x
        self.lhs, self.own, self.other = lhs, own, other
        (self.out, self.mine, self.relay, self.ring, self.q, self.relay2, self.ring2,
         self.ss, self.rrs, self.rs, self.ss2, self.rs2) = refs
        self.ia, self.ib = (place.x, place.y) if first_x else (place.y, place.x)

    def along(self, first, step):
        return self.p.along_x(step) if first == self.first_x else self.p.along_y(step)

    def product(self, pa, pb):
        j = pb * 4 + pa if self.first_x else pa * 4 + pb
        here = pl.ds(pl.multiple_of((2 * j + self.p.k) * 128, 128), 128)
        there = pl.ds(pl.multiple_of(j * 128, 128), 128)
        return jnp.dot(
            self.lhs[0], self.own[:, :, here].reshape(256, 128), preferred_element_type=F32
        ) + jnp.dot(
            self.lhs[1], self.other[:, :, there].reshape(256, 128), preferred_element_type=F32
        )

    def relay_copy(self, pb):
        step = jnp.where(pb < 2, 1, 3)
        return remote(
            self.out.at[0, pb], self.relay.at[pb], self.ss.at[0, pb], self.rrs.at[pb],
            self.along(True, step),
        )

    def ring_copy(self, d, pb):
        return remote(
            self.out.at[1 + d, pb], self.ring.at[d, pb], self.ss.at[1 + d, pb], self.rs.at[d, pb],
            self.along(True, 1 + 2 * d),
        )

    def send_relay(self):
        def one(pb, carry):
            self.out[0, pb] = self.product(lax.rem(self.ia + 2, 4), pb).astype(BF16)
            self.relay_copy(pb).start()
            return carry

        lax.fori_loop(0, 4, one, 0)

    def send_fresh(self):
        def one(t, carry):
            d = lax.div(t, 2)
            pb = lax.rem(t + 2, 4)
            self.out[1 + d, pb] = self.product(lax.rem(self.ia + 1 + 2 * d, 4), pb).astype(BF16)
            self.ring_copy(d, pb).start()
            return carry

        lax.fori_loop(0, 4, one, 0)

    def send_joined(self):
        def one(pb, carry):
            d = lax.div(pb, 2)
            value = self.product(lax.rem(self.ia + 1 + 2 * d, 4), pb)
            self.relay_copy(pb).wait_recv()
            self.out[1 + d, pb] = (value + self.relay[pb].astype(F32)).astype(BF16)
            self.ring_copy(d, pb).start()
            return carry

        lax.fori_loop(0, 4, one, 0)

    def keep(self):
        def one(pb, carry):
            self.mine[pb] = self.product(self.ia, pb)
            return carry

        lax.fori_loop(0, 4, one, 0)

    def halves(self, which):
        place = lax.rem(self.ib + 2, 4)
        rows = pl.ds(256 * which, 256)
        return remote(
            self.q.at[place, rows, :], self.relay2.at[which], self.ss2.at[which],
            self.rs2.at[which], self.along(False, 1 + 2 * which),
        )

    def ends(self, which):
        return remote(
            self.q.at[lax.rem(self.ib + 1 + 2 * which, 4)], self.ring2.at[which],
            self.ss2.at[2 + which], self.rs2.at[2 + which], self.along(False, 1 + 2 * which),
        )

    def turn(self):
        def one(t, carry):
            pb = lax.rem(self.ib + 2 + t, 4)
            for d in (0, 1):
                self.ring_copy(d, pb).wait_recv()
            total = self.mine[pb] + self.ring[0, pb].astype(F32) + self.ring[1, pb].astype(F32)
            self.mine[pb] = total
            self.q[pb] = total.astype(BF16)
            return carry

        one(0, 0)
        for which in (0, 1):
            self.halves(which).start()
        lax.fori_loop(1, 4, one, 0)

    def join(self):
        for which in (0, 1):
            self.halves(which).wait_recv()
            place = lax.rem(self.ib + 1 + 2 * which, 4)
            rows = pl.ds(256 * which, 256)
            self.q[place, rows, :] = (
                self.mine[place, rows, :] + self.relay2[which].astype(F32)
            ).astype(BF16)
            self.ends(which).start()

    def finish(self, result):
        for which in (0, 1):
            self.ends(which).wait_recv()
        result[...] = self.mine[self.ib] + self.ring2[0].astype(F32) + self.ring2[1].astype(F32)

    def drain(self):
        def one(pb, carry):
            self.relay_copy(pb).wait_send()
            for d in (0, 1):
                self.ring_copy(d, pb).wait_send()
            return carry

        lax.fori_loop(0, 4, one, 0)
        for which in (0, 1):
            self.halves(which).wait_send()
            self.ends(which).wait_send()


class RowSum:
    def __init__(self, place, parts, came, send_sem, recv_sem):
        self.p, self.parts, self.came = place, parts, came
        self.ss, self.rs = send_sem, recv_sem

    def block(self, d, s):
        return lax.rem(self.p.m + (4 - s if d == 0 else 4 + s), NMP)

    def copy(self, d, s, part):
        cols = pl.ds(part * HALF, HALF)
        return remote(
            self.parts.at[self.block(d, s), :, cols], self.came.at[d, s, :, cols],
            self.ss.at[d, s, part], self.rs.at[d, s, part], self.p.along_z(1 if d == 0 else NMP - 1),
        )

    def begin(self, part):
        self.copy(part, 0, part).start()
        self.copy(1 - part, 1, part).start()

    def step(self, s):
        for fresh in (True, False):
            for d in (0, 1):
                part = 1 - d if fresh else d
                if fresh and s == 1:
                    continue
                self.copy(d, s - 1, part).wait_recv()
                cols = pl.ds(part * HALF, HALF)
                to = self.block(d, s)
                self.parts[to, :, cols] = (
                    self.parts[to, :, cols].astype(F32) + self.came[d, s - 1, :, cols].astype(F32)
                ).astype(BF16)
                self.copy(d, s, part).start()

    def finish(self, result):
        for d in (0, 1):
            for part in (0, 1):
                self.copy(d, 3, part).wait_recv()
        result[...] = (
            self.parts[self.p.m].astype(F32)
            + self.came[0, 3].astype(F32)
            + self.came[1, 3].astype(F32)
        ).astype(BF16)

    def drain(self):
        for d in (0, 1):
            for s in range(4):
                for part in (0, 1):
                    if s > 0 or part == d:
                        self.copy(d, s, part).wait_send()


class GateSum:
    def __init__(self, place, parts, row, mid, col, total, send_sem, recv_sem):
        self.p = place
        self.parts, self.row, self.mid, self.col, self.total = parts, row, mid, col, total
        self.ss, self.rs = send_sem, recv_sem

    def copies(self, which, arriving):
        p = self.p
        if which == 4:
            view = self.total.at[1 - p.k if arriving else p.k]
            return [remote(view, view, self.ss.at[4, 0], self.rs.at[4, 0], p.other_core())]
        found = []
        for o in (1, 2, 3):
            x, y = lax.rem(p.x + o, 4), lax.rem(p.y + o, 4)
            back_x, back_y = lax.rem(p.x + 4 - o, 4), lax.rem(p.y + 4 - o, 4)
            sems = self.ss.at[which, o - 1], self.rs.at[which, o - 1]
            if which == 0:
                src = self.parts.at[:, pl.ds(pl.multiple_of(x * 64, 64), 64), :]
                dst = self.row.at[back_x if arriving else p.x]
                found.append(remote(src, dst, *sems, p.along_x(o)))
            elif which == 1:
                src = self.mid.at[:, pl.ds(pl.multiple_of(y * 16, 16), 16), :]
                dst = self.col.at[back_y if arriving else p.y]
                found.append(remote(src, dst, *sems, p.along_y(o)))
            elif which == 2:
                at = p.x * 64 + (back_y if arriving else p.y) * 16
                view = self.total.at[p.k, :, pl.ds(pl.multiple_of(at, 16), 16), :]
                found.append(remote(view, view, *sems, p.along_y(o)))
            else:
                at = (back_x if arriving else p.x) * 64
                view = self.total.at[p.k, :, pl.ds(pl.multiple_of(at, 64), 64), :]
                found.append(remote(view, view, *sems, p.along_x(o)))
        return found

    def start(self, which):
        p = self.p
        if which == 0:
            mine = pl.ds(pl.multiple_of(p.x * 64, 64), 64)
            self.row[p.x] = self.parts[:, mine, :]
        if which == 1:
            total = self.row[0].astype(F32)
            for o in (1, 2, 3):
                total = total + self.row[o].astype(F32)
            self.mid[...] = total.astype(BF16)
            self.col[p.y] = self.mid[:, pl.ds(pl.multiple_of(p.y * 16, 16), 16), :]
        if which == 2:
            total = self.col[0].astype(F32)
            for o in (1, 2, 3):
                total = total + self.col[o].astype(F32)
            at = pl.ds(pl.multiple_of(p.x * 64 + p.y * 16, 16), 16)
            self.total[p.k, :, at, :] = total.astype(BF16)
        for copy in self.copies(which, False):
            copy.start()

    def finish(self, which):
        for copy in self.copies(which, True):
            copy.wait_recv()

    def drain(self):
        for which in range(5):
            for copy in self.copies(which, False):
                copy.wait_send()


def minus_expm1(v):
    series = 1.0 + v * (1.0 / 8.0)
    for n in (7, 6, 5, 4, 3, 2):
        series = 1.0 + v * (1.0 / n) * series
    return jnp.where(v > -0.35, -v * series, 1.0 - jnp.exp(v))


def enter(place, partners):
    barrier = pltpu.get_barrier_semaphore()
    for device in partners:
        pl.semaphore_signal(barrier, inc=1, device_id=device, device_id_type=MESH)
    pl.semaphore_wait(barrier, len(partners))


def first_kernel(
    tokens, branch, out_grad, w_in, conv_w, gate_a, gate_a_b, gate_i, gate_i_b, decay_param, w_out,
    state_init, conv_history,
    tokens_grad, branch_grad, w_in_t, w_out_grad, small, gate_total,
    tok, og, proj, gated, conv_b, ri, tok_o, og_o, conv_o, ri_o, gate_p, gate_row, gate_mid, gate_col,
    lhs_g, lhs_p, parts, came,
    w_in_v, w_out_v, acc, px, cv, rg, ig, dk, rem, hs, cp, ep, br, gp, cg, kv, edge_s, edge_r, edge_c,
    core_s, row_s, col_s, core_b, row_b, col_b,
    core_m, row_m, col_m,
    w_sem, ts, tr, gs, gr, fs, fr, bs, brs, es, er, ms, mr, zs, zr, ps, pr, qs, qr,
    *sums,
):
    p = Place()
    loads = [
        pltpu.make_async_copy(w_in, w_in_v, w_sem.at[0]),
        pltpu.make_async_copy(w_out, w_out_v, w_sem.at[1]),
    ]
    for load in loads:
        load.start()
    tok[p.m] = tokens[...]
    og[p.m] = out_grad[...]
    enter(
        p,
        [p.along_z(1), p.along_z(NMP - 1), p.along_ctx(1), p.along_ctx(31), p.other_core()]
        + [p.along_x(o) for o in (1, 2, 3)]
        + [p.along_y(o) for o in (1, 2, 3)],
    )
    tokens_in = Gather(p, tok, ts, tr)
    grads_in = Gather(p, og, gs, gr)
    tokens_in.send(0)

    def wide(row):
        return jnp.broadcast_to(row.reshape(1, CH), (8, CH))

    taps = conv_w[...].astype(F32)
    for j in range(4):
        kv[j] = wide(taps[j : j + 1])
    kv[4] = wide(gate_a_b[...])
    kv[5] = wide(gate_i_b[...])
    negative = wide(-decay_param[...])
    small_exp = jnp.exp(-jnp.abs(negative))
    one_more = 1.0 + small_exp
    gap = one_more - 1.0
    log_part = jnp.where(
        gap == 0.0, small_exp, jnp.log(one_more) * (small_exp / jnp.where(gap == 0.0, 1.0, gap))
    )
    kv[6] = jnp.maximum(negative, 0.0) + log_part
    br[...] = to_segments(branch[...].astype(F32))

    for s in (0, 1, 2):
        tokens_in.arrive(s)
    grads_in.send(0)
    loads[0].wait()
    tokens_in.arrive(3)
    other_tokens = CoreColumns(p, tok, tok_o, ps.at[0], pr.at[0])
    other_grads = CoreColumns(p, og, og_o, ps.at[1], pr.at[1])
    other_conv = CorePair(p, conv_b, conv_o, ps.at[2], pr.at[2])
    other_gated = CorePair(p, lhs_g.at[0], lhs_g.at[1], ps.at[3], pr.at[3])
    other_proj = CorePair(p, lhs_p.at[0], lhs_p.at[1], ps.at[4], pr.at[4])
    other_gate = CorePair(p, ri.at[1 - p.k], ri_o, ps.at[5], pr.at[5])
    pairs = [other_tokens, other_grads, other_conv, other_gated, other_proj, other_gate]
    w_out_sum = WeightSum(p, False, lhs_g, og, og_o, sums[:12])
    w_in_sum = WeightSum(p, True, lhs_p, tok, tok_o, sums[12:])
    row_sum = RowSum(p, parts, came, zs, zr)
    gate_sum = GateSum(p, gate_p, gate_row, gate_mid, gate_col, gate_total, qs, qr)
    total_sum = Fold(p, core_m, row_m, col_m, ms, mr)
    other_tokens.start()

    acc[...] = jnp.zeros_like(acc)

    def project(n, carry):
        at = pl.ds(pl.multiple_of(n * 512, 512), 512)
        acc[...] += jnp.dot(
            tok[:, :, at].reshape(256, 512), w_in_v[at, :], preferred_element_type=F32
        )
        return carry

    lax.fori_loop(0, 8, project, 0)
    edge_s[...] = acc[pl.ds(240, 16), :].astype(BF16)
    forward_edge = remote(edge_s, edge_r, es.at[0], er.at[0], p.along_ctx(1))
    forward_edge.start()
    px[pl.ds(3, 32)] = to_segments(acc[...].astype(BF16).astype(F32))
    grads_in.arrive(0)

    lane8 = lax.broadcasted_iota(jnp.int32, (8, CH), 0)
    forward_edge.wait_recv()
    first = p.c == 0
    before = edge_r[...].astype(F32)[13:16]
    before = jnp.where(first, conv_history[...].astype(F32), before)
    for j in range(3):
        turned = pltpu.roll(px[32 + j], 1, 0)
        px[j] = jnp.where(lane8 == 0, wide(before[j : j + 1]), turned)

    def convolve(n, carry):
        total = kv[0] * px[pl.ds(2 * n + 3, 2)]
        for j in (1, 2, 3):
            total = total + kv[j] * px[pl.ds(2 * n + 3 - j, 2)]
        rounded = total.astype(BF16)
        cv[pl.ds(2 * n, 2)] = rounded.astype(F32)
        conv_b[pl.ds(pl.multiple_of(16 * n, 16), 16), :] = rounded.reshape(16, CH)
        return carry

    lax.fori_loop(0, 16, convolve, 0)
    other_conv.start()
    for b in (0, 1):
        cols = pl.ds(b * 256, 256)
        rg[:, :, cols] = jnp.dot(
            conv_b[:, cols], gate_a[b], preferred_element_type=F32
        ).reshape(32, 8, 256)
        ig[:, :, cols] = jnp.dot(
            conv_b[:, cols], gate_i[b], preferred_element_type=F32
        ).reshape(32, 8, 256)

    def gates(n, carry):
        h, c = carry
        at = pl.ds(2 * n, 2)
        recur = jax.nn.sigmoid(rg[at] + kv[4])
        inp = jax.nn.sigmoid(ig[at] + kv[5])
        log_decay = -8.0 * recur * kv[6]
        decay = jnp.exp(log_decay)
        remain = minus_expm1(2.0 * log_decay)
        rg[at] = recur
        ig[at] = inp
        dk[at] = decay
        rem[at] = remain
        driven = jnp.sqrt(remain) * inp * cv[at]
        for t in (0, 1):
            h = decay[t] * h + driven[t]
            c = decay[t] * c
            hs[2 * n + 1 + t] = h
            cp[2 * n + t] = c
        return h, c

    h, c = lax.fori_loop(0, 16, gates, (jnp.zeros((8, CH), F32), jnp.ones((8, CH), F32)))
    c_seg = c
    for sh in (1, 2, 4):
        ok = lane8 >= sh
        h, c = (
            jnp.where(ok, h + c * pltpu.roll(h, sh, 0), h),
            jnp.where(ok, c * pltpu.roll(c, sh, 0), c),
        )
    c_before = jnp.where(lane8 == 0, 1.0, pltpu.roll(c, 1, 0))
    h_before = jnp.where(lane8 == 0, 0.0, pltpu.roll(h, 1, 0))
    states = Fold(p, core_s, row_s, col_s, fs, fr)
    pair = jnp.where(lane8 < 4, wide(c[7:8]), wide(h[7:8]))

    def both(slot):
        value = slot
        return wide(value[0:1]), wide(value[4:5])

    states.start(0, pair)
    grads_in.arrive(1)

    def suffix(n, e):
        ep[31 - n] = e
        return e * dk[31 - n]

    lax.fori_loop(0, 32, suffix, jnp.ones((8, CH), F32))
    states.finish(0)
    c0, h0 = both(core_s[0])
    c1, h1 = both(core_s[1])
    states.start(1, jnp.where(lane8 < 4, c0 * c1, c1 * h0 + h1))
    states.finish(1)
    cr, hr = jnp.ones((8, CH), F32), jnp.zeros((8, CH), F32)
    for o in range(4):
        co, ho = both(row_s[o])
        cr, hr = cr * co, co * hr + ho
    states.start(2, jnp.where(lane8 < 4, cr, hr))
    states.finish(2)
    state = wide(state_init[...])
    for o in range(4):
        co, ho = both(col_s[o])
        state = jnp.where(o < p.y, co * state + ho, state)
    for o in range(4):
        co, ho = both(row_s[o])
        state = jnp.where(o < p.x, co * state + ho, state)
    state = jnp.where(p.k == 1, c0 * state + h0, state)
    seg_state = h_before + c_before * state
    hs[0] = seg_state

    def finish_states(n, carry):
        at = pl.ds(2 * n, 2)
        value = hs[pl.ds(2 * n + 1, 2)] + cp[at] * seg_state
        hs[pl.ds(2 * n + 1, 2)] = value
        cp[at] = value * br[at]
        return carry

    lax.fori_loop(0, 16, finish_states, 0)
    gated[...] = from_segments(cp[...]).astype(BF16)
    lhs_g[0] = gated[...].T
    other_gated.start()

    grads_in.arrive(2)
    loads[1].wait()
    grads_in.arrive(3)
    other_grads.start()
    acc[...] = jnp.zeros_like(acc)

    def grad_product(n, carry):
        at = pl.ds(pl.multiple_of(n * 512, 512), 512)
        acc[...] += matmul_nt(og[:, :, at].reshape(256, 512), w_out_v[:, at])
        return carry

    lax.fori_loop(0, 8, grad_product, 0)
    gp[...] = to_segments(acc[...])

    def backward(n, b):
        i = 31 - n
        g = gp[i]
        cp[i] = g * hs[i + 1]
        a = g * br[i] + b
        gp[i] = a
        return dk[i] * a

    b = lax.fori_loop(0, 32, backward, jnp.zeros((8, CH), F32))
    c = c_seg
    for sh in (1, 2, 4):
        ok = lane8 < 8 - sh
        b, c = (
            jnp.where(ok, b + c * pltpu.roll(b, 8 - sh, 0), b),
            jnp.where(ok, c * pltpu.roll(c, 8 - sh, 0), c),
        )
    c_after = jnp.where(lane8 == 7, 1.0, pltpu.roll(c, 7, 0))
    b_after = jnp.where(lane8 == 7, 0.0, pltpu.roll(b, 7, 0))
    adjoints = Fold(p, core_b, row_b, col_b, bs, brs)
    adjoints.start(0, wide(b[0:1]))
    other_gated.finish()
    other_grads.finish()
    w_out_sum.send_relay()
    adjoints.finish(0)
    b0, b1 = core_b[0], core_b[1]
    adjoints.start(1, b0 + c0 * b1)
    w_out_sum.send_fresh()
    adjoints.finish(1)
    row = jnp.zeros((8, CH), F32)
    for o in (3, 2, 1, 0):
        row = row_b[o] + both(row_s[o])[0] * row
    adjoints.start(2, row)
    branch_grad[...] = from_segments(cp[...]).astype(BF16)
    adjoints.finish(2)
    later = jnp.zeros((8, CH), F32)
    for o in (3, 2, 1, 0):
        later = jnp.where(o > p.y, col_b[o] + both(col_s[o])[0] * later, later)
    for o in (3, 2, 1, 0):
        later = jnp.where(o > p.x, row_b[o] + both(row_s[o])[0] * later, later)
    later = jnp.where(p.k == 0, b1 + c1 * later, later)
    seg_later = b_after + c_after * later

    def gate_grads(n, carry):
        sum_a, sum_i, sum_r = carry
        at = pl.ds(2 * n, 2)
        adjoint = gp[at] + ep[at] * seg_later
        decay, remain, inp, recur, wide_conv = dk[at], rem[at], ig[at], rg[at], cv[at]
        scaler = jnp.sqrt(remain)
        scaler_grad = adjoint * inp * wide_conv
        log_grad = adjoint * hs[at] * decay - 2.0 * decay * decay * scaler_grad / jnp.sqrt(
            jnp.maximum(4.0 * remain, 1e-06)
        )
        recur_pre = (log_grad * (-8.0 * kv[6]) * recur * (1.0 - recur)).astype(BF16)
        input_pre = (scaler_grad * scaler * (1.0 - inp)).astype(BF16)
        flat = pl.ds(pl.multiple_of(16 * n, 16), 16)
        ri[0, flat, :] = recur_pre.reshape(16, CH)
        ri[1, flat, :] = input_pre.reshape(16, CH)
        cg[at] = adjoint * scaler * inp
        return (
            sum_a + jnp.sum(recur_pre.astype(F32), 0),
            sum_i + jnp.sum(input_pre.astype(F32), 0),
            sum_r + jnp.sum(log_grad * (-8.0 * recur), 0),
        )

    zero = jnp.zeros((8, CH), F32)
    sum_a, sum_i, sum_r = lax.fori_loop(0, 16, gate_grads, (zero, zero, zero))
    other_gate.start()
    for b in (0, 1):
        cols = pl.ds(b * 256, 256)
        cg[pl.ds(0, 32), :, cols] += (
            matmul_nt(ri[0, :, cols], gate_a[b]) + matmul_nt(ri[1, :, cols], gate_i[b])
        ).reshape(32, 8, 256)
    backward_edge = remote(cg.at[pl.ds(0, 3)], edge_c, es.at[1], er.at[1], p.along_ctx(31))
    backward_edge.start()
    w_out_sum.send_joined()
    backward_edge.wait_recv()
    for j in range(3):
        turned = pltpu.roll(cg[j], 7, 0)
        came = jnp.where(p.c == 31, 0.0, wide(edge_c[j][0:1]))
        cg[32 + j] = jnp.where(lane8 == 7, came, turned)

    def proj_grads(n, carry):
        at = pl.ds(2 * n, 2)
        own = cg[at]
        total = kv[0] * own
        for j in (1, 2, 3):
            total = total + kv[j] * cg[pl.ds(2 * n + j, 2)]
        cp[at] = total
        return tuple(
            carry[j] + jnp.sum(own * px[pl.ds(2 * n + 3 - j, 2)], 0) for j in range(4)
        )

    tap_sums = lax.fori_loop(0, 16, proj_grads, (zero, zero, zero, zero))
    proj[...] = from_segments(cp[...]).astype(BF16)
    lhs_p[0] = proj[...].T
    other_proj.start()
    for part in (0, 1):

        def spread(n, carry):
            at = pl.ds(pl.multiple_of(n * 512, 512), 512)
            parts[:, :, at] = matmul_nt(proj[...], w_in_v[at, :]).astype(BF16).reshape(8, 32, 512)
            return carry

        lax.fori_loop(part * 4, part * 4 + 4, spread, 0)
        row_sum.begin(part)
    rows = [jnp.sum(v, 0, keepdims=True) for v in (*tap_sums, sum_r, sum_a, sum_i)]
    total_sum.start(0, jnp.concatenate(rows + [jnp.zeros((1, CH), F32)], 0))
    other_tokens.finish()
    other_proj.finish()
    w_in_sum.send_relay()
    w_in_sum.send_fresh()
    row_sum.step(1)
    other_conv.finish()
    other_gate.finish()
    for b in (0, 1):
        cols = pl.ds(b * 256, 256)
        gate_p[b] = (
            matmul_tn(conv_b[:, cols], ri[p.k, :, cols]) + matmul_tn(conv_o[:, cols], ri_o[:, cols])
        ).astype(BF16)
    gate_sum.start(0)
    w_out_sum.keep()
    w_out_sum.turn()
    w_in_sum.send_joined()
    row_sum.step(2)
    total_sum.finish(0)
    total_sum.start(1, core_m[0] + core_m[1])
    gate_sum.finish(0)
    gate_sum.start(1)
    w_out_sum.join()
    w_in_sum.keep()
    row_sum.step(3)
    total_sum.finish(1)
    total_sum.start(2, row_m[0] + row_m[1] + row_m[2] + row_m[3])
    w_in_sum.turn()
    gate_sum.finish(1)
    gate_sum.start(2)
    w_out_sum.finish(w_out_grad)
    gate_sum.finish(2)
    gate_sum.start(3)
    w_in_sum.join()
    total_sum.finish(2)
    small[...] = col_m[0] + col_m[1] + col_m[2] + col_m[3]
    gate_sum.finish(3)
    gate_sum.start(4)
    row_sum.finish(tokens_grad)
    w_in_sum.finish(w_in_t)
    gate_sum.finish(4)
    for used in (states, adjoints, total_sum, w_out_sum, w_in_sum, row_sum, gate_sum, *pairs):
        used.drain()
    tokens_in.sent()
    grads_in.sent()
    forward_edge.wait_send()
    backward_edge.wait_send()


def call_first(*args):
    def vm(shape, dtype):
        return pltpu.VMEM(shape, dtype)

    seg = (32, 8, CH)
    tile = (8, CH)
    dma = pltpu.SemaphoreType.DMA
    S = jax.ShapeDtypeStruct
    outs = (
        S((32, DM), BF16),
        S((256, CH), BF16),
        S((CH, 128), F32),
        S((CH, 128), F32),
        S((8, CH), F32),
        S((2, 2, 256, 256), BF16),
    )
    weight = [
        vm((3, 4, CH, 128), BF16),
        vm((4, CH, 128), F32),
        vm((4, CH, 128), BF16),
        vm((2, 4, CH, 128), BF16),
        vm((4, CH, 128), BF16),
        vm((2, 256, 128), BF16),
        vm((2, CH, 128), BF16),
        dma((3, 4)),
        dma((4,)),
        dma((2, 4)),
        dma((4,)),
        dma((4,)),
    ]
    big = {3, 10}
    return pl.pallas_call(
        first_kernel,
        out_shape=outs,
        in_specs=[
            pl.BlockSpec(memory_space=pl.ANY if n in big else pltpu.VMEM) for n in range(13)
        ],
        out_specs=tuple(pl.BlockSpec(memory_space=pltpu.VMEM) for _ in outs),
        scratch_shapes=[
            vm((8, 32, DM), BF16),
            vm((8, 32, DM), BF16),
            vm((256, CH), BF16),
            vm((256, CH), BF16),
            vm((256, CH), BF16),
            vm((2, 256, CH), BF16),
            vm((8, 32, HALF), BF16),
            vm((8, 32, HALF), BF16),
            vm((256, CH), BF16),
            vm((256, CH), BF16),
            vm((2, 256, 256), BF16),
            vm((4, 2, 64, 256), BF16),
            vm((2, 64, 256), BF16),
            vm((4, 2, 16, 256), BF16),
            vm((2, CH, 256), BF16),
            vm((2, CH, 256), BF16),
            vm((8, 32, DM), BF16),
            vm((2, 4, 32, DM), BF16),
            vm((DM, CH), BF16),
            vm((CH, DM), BF16),
            vm((256, CH), F32),
            vm((35, 8, CH), F32),
            *[vm(seg, F32) for _ in range(5)],
            vm((33, 8, CH), F32),
            *[vm(seg, F32) for _ in range(4)],
            vm((35, 8, CH), F32),
            vm((7, 8, CH), F32),
            vm((16, CH), BF16),
            vm((16, CH), BF16),
            vm((3, 8, CH), F32),
            vm((2, *tile), F32),
            vm((4, *tile), F32),
            vm((4, *tile), F32),
            vm((2, *tile), F32),
            vm((4, *tile), F32),
            vm((4, *tile), F32),
            vm((2, *tile), F32),
            vm((4, *tile), F32),
            vm((4, *tile), F32),
            dma((2,)),
            dma((2, 4, 2)),
            dma((2, 4, 2)),
            dma((2, 4, 2)),
            dma((2, 4, 2)),
            dma((7,)),
            dma((7,)),
            dma((7,)),
            dma((7,)),
            dma((2,)),
            dma((2,)),
            dma((7,)),
            dma((7,)),
            dma((2, 4, 2)),
            dma((2, 4, 2)),
            dma((6,)),
            dma((6,)),
            dma((5, 3)),
            dma((5, 3)),
            *weight,
            *weight,
        ],
        compiler_params=pltpu.CompilerParams(
            collective_id=0, has_side_effects=True, vmem_limit_bytes=56 << 20
        ),
    )(*args)


def last_kernel(
    tokens_grad, branch_grad, w_in_t, w_out_grad, small, gates, decay_param,
    o_tokens, o_branch, o_w_in, o_w_out, o_conv, o_ga, o_gab, o_gi, o_gib, o_decay,
):
    o_tokens[...] = tokens_grad[...]
    o_branch[...] = branch_grad[...]
    o_w_in[...] = w_in_t[...].T
    o_w_out[...] = w_out_grad[...]
    o_conv[...] = small[pl.ds(0, 4), :]
    rows = small[...]
    o_gab[...] = rows[5]
    o_gib[...] = rows[6]
    o_decay[...] = rows[4] * -jax.nn.sigmoid(-decay_param[...])
    o_ga[...] = gates[0].astype(F32)
    o_gi[...] = gates[1].astype(F32)


def shards(*args):
    results = call_first(*args)
    S = jax.ShapeDtypeStruct
    outs = (
        S((32, DM), BF16),
        S((256, CH), BF16),
        S((128, CH), F32),
        S((CH, 128), F32),
        S((4, CH), F32),
        S((2, 256, 256), F32),
        S((CH,), F32),
        S((2, 256, 256), F32),
        S((CH,), F32),
        S((CH,), F32),
    )
    return pl.pallas_call(
        last_kernel,
        out_shape=outs,
        in_specs=[pl.BlockSpec(memory_space=pltpu.VMEM)] * 7,
        out_specs=tuple(pl.BlockSpec(memory_space=pltpu.VMEM) for _ in outs),
    )(*results, args[9])


def solution(mesh):
    placed = (
        P(("ctx", "mp"), None),
        P("ctx", "mp"),
        P(("ctx", "mp"), None),
        P(None, "mp"),
        P(None, "mp"),
        P("mp", None, None),
        P("mp"),
        P("mp", None, None),
        P("mp"),
        P("mp"),
        P("mp", None),
        P("mp"),
        P(None, "mp"),
    )
    return jax.shard_map(
        shards,
        mesh=mesh,
        in_specs=placed,
        out_specs=(
            P(("ctx", "mp"), None),
            P("ctx", "mp"),
            P("ctx", "mp"),
            P("mp", "ctx"),
            P(None, "mp"),
            P("mp", None, None),
            P("mp"),
            P("mp", None, None),
            P("mp"),
            P("mp"),
        ),
        check_vma=False,
    )
```

```python
import jax
import jax.numpy as jnp
from jax import lax
from jax.experimental import pallas as pl
from jax.experimental.pallas import tpu as pltpu
from jax.sharding import PartitionSpec as P

MESH = pl.DeviceIdType.MESH
F32 = jnp.float32
BF16 = jnp.bfloat16
NMP = 8
SEG = 32
CH = 512
DM = 4096
HALF = DM // 2


def matmul_tn(left, right):
    return lax.dot_general(left, right, (((0,), (0,)), ((), ())), preferred_element_type=F32)


def matmul_nt(left, right):
    return lax.dot_general(left, right, (((1,), (1,)), ((), ())), preferred_element_type=F32)


def to_segments(value):
    return jnp.transpose(value.reshape(NMP, SEG, CH), (1, 0, 2))


def from_segments(value):
    return jnp.transpose(value, (1, 0, 2)).reshape(NMP * SEG, CH)


def remote(src, dst, send_sem, recv_sem, device):
    return pltpu.make_async_remote_copy(
        src_ref=src,
        dst_ref=dst,
        send_sem=send_sem,
        recv_sem=recv_sem,
        device_id=device,
        device_id_type=MESH,
    )


class Place:
    def __init__(self):
        self.c = lax.axis_index("ctx")
        self.m = lax.axis_index("mp")
        self.k = lax.rem(self.c, 2)
        self.x = lax.rem(lax.div(self.c, 2), 4)
        self.y = lax.div(self.c, 8)

    def chip(self, y, x, k):
        return (y * 8 + x * 2 + k, self.m)

    def other_core(self):
        return self.chip(self.y, self.x, 1 - self.k)

    def along_x(self, step):
        return self.chip(self.y, lax.rem(self.x + step, 4), self.k)

    def along_y(self, step):
        return self.chip(lax.rem(self.y + step, 4), self.x, self.k)

    def along_z(self, step):
        return (self.c, lax.rem(self.m + step, NMP))

    def along_ctx(self, step):
        return (lax.rem(self.c + step, 32), self.m)


class Gather:
    def __init__(self, place, buf, send_sem, recv_sem):
        self.p, self.buf, self.ss, self.rs = place, buf, send_sem, recv_sem

    def view(self, d, s, part):
        step = (NMP - s) if d == 0 else s
        return self.buf.at[lax.rem(self.p.m + step, NMP), :, pl.ds(part * HALF, HALF)]

    def copy(self, d, s, part, at):
        view = self.view(d, at, part)
        to = self.p.along_z(1 if d == 0 else NMP - 1)
        return remote(view, view, self.ss.at[d, s, part], self.rs.at[d, s, part], to)

    def present(self, d, s, part):
        return s < 3 or part == d

    def send(self, s):
        for part in (0, 1):
            for d in (0, 1):
                if self.present(d, s, part):
                    self.copy(d, s, part, s).start()

    def arrive(self, s):
        for part in (0, 1):
            for d in (0, 1):
                if self.present(d, s, part):
                    self.copy(d, s, part, s + 1).wait_recv()
                    if s < 3 and self.present(d, s + 1, part):
                        self.copy(d, s + 1, part, s + 1).start()

    def sent(self):
        for s in range(4):
            for part in (0, 1):
                for d in (0, 1):
                    if self.present(d, s, part):
                        self.copy(d, s, part, s).wait_send()


class Fold:
    def __init__(self, place, core, row, col, send_sem, recv_sem):
        self.p = place
        self.slots = (core, row, col)
        self.ss, self.rs = send_sem, recv_sem

    def copies(self, which, arriving):
        p, slots = self.p, self.slots[which]
        mine = (p.k, p.x, p.y)[which]
        size = 2 if which == 0 else 4
        base = (0, 1, 4)[which]
        found = []
        for o in range(1, size):
            to = p.other_core() if which == 0 else (p.along_x(o) if which == 1 else p.along_y(o))
            slot = slots.at[lax.rem(mine + size - o, size) if arriving else mine]
            sems = self.ss.at[base + o - 1], self.rs.at[base + o - 1]
            found.append(remote(slot, slot, *sems, to))
        return found

    def start(self, which, value):
        self.slots[which][(self.p.k, self.p.x, self.p.y)[which]] = value
        for copy in self.copies(which, False):
            copy.start()

    def finish(self, which):
        for copy in self.copies(which, True):
            copy.wait_recv()

    def drain(self):
        for which in range(3):
            for copy in self.copies(which, False):
                copy.wait_send()


class Everyone:
    def __init__(self, place, slots, send_sem, recv_sem):
        self.p, self.slots, self.ss, self.rs = place, slots, send_sem, recv_sem

    def copy(self, o, owner):
        slot = self.slots.at[owner]
        return remote(slot, slot, self.ss.at[o], self.rs.at[o], self.p.along_ctx(o))

    def start(self, value):
        self.slots[self.p.c] = value

        def one(o, carry):
            self.copy(o, self.p.c).start()
            return carry

        lax.fori_loop(1, 32, one, 0)

    def finish(self):
        def one(o, carry):
            self.copy(o, lax.rem(self.p.c + 32 - o, 32)).wait_recv()
            return carry

        lax.fori_loop(1, 32, one, 0)

    def drain(self):
        def one(o, carry):
            self.copy(o, self.p.c).wait_send()
            return carry

        lax.fori_loop(1, 32, one, 0)


class CorePair:
    def __init__(self, place, src, dst, send_sem, recv_sem):
        self.copy = remote(src, dst, send_sem, recv_sem, place.other_core())
        self.start, self.finish, self.drain = (
            self.copy.start, self.copy.wait_recv, self.copy.wait_send
        )


class CoreColumns:
    def __init__(self, place, own, other, send_sem, recv_sem):
        self.p, self.own, self.other = place, own, other
        self.ss, self.rs = send_sem, recv_sem
        self.whole = remote(other, other, send_sem, recv_sem, place.other_core())

    def start(self):
        def one(j, carry):
            src = pl.ds(pl.multiple_of((2 * j + 1 - self.p.k) * 128, 128), 128)
            dst = pl.ds(pl.multiple_of(j * 128, 128), 128)
            remote(
                self.own.at[:, :, src], self.other.at[:, :, dst], self.ss, self.rs,
                self.p.other_core(),
            ).start()
            return carry

        lax.fori_loop(0, 16, one, 0)

    def finish(self):
        self.whole.wait_recv()

    def drain(self):
        self.whole.wait_send()


class WeightSum:
    def __init__(self, place, first_x, lhs, own, other, refs):
        self.p, self.first_x = place, first_x
        self.lhs, self.own, self.other = lhs, own, other
        (self.out, self.mine, self.relay, self.ring, self.q, self.relay2, self.ring2,
         self.ss, self.rs, self.ss2, self.rs2) = refs
        self.ia, self.ib = (place.x, place.y) if first_x else (place.y, place.x)
        self.rows = pl.ds(0 if first_x else 256, 256)

    def along(self, first, step):
        return self.p.along_x(step) if first == self.first_x else self.p.along_y(step)

    def product(self, distance, o):
        pa, pb = lax.rem(self.ia + distance, 4), lax.rem(self.ib + o, 4)
        j = pb * 4 + pa if self.first_x else pa * 4 + pb
        here = pl.ds(pl.multiple_of((2 * j + self.p.k) * 128, 128), 128)
        there = pl.ds(pl.multiple_of(j * 128, 128), 128)
        return jnp.dot(
            self.lhs[0, self.rows, :], self.own[:, :, here].reshape(256, 128),
            preferred_element_type=F32,
        ) + jnp.dot(
            self.lhs[1, self.rows, :], self.other[:, :, there].reshape(256, 128),
            preferred_element_type=F32,
        )

    def copy(self, kind, o):
        side = lax.rem(o, 2) if kind != 1 else 1 - lax.rem(o, 2)
        target = self.relay.at[o] if kind == 0 else self.ring.at[kind - 1, o]
        return remote(
            self.out.at[kind, o], target, self.ss.at[kind, o], self.rs.at[kind, o],
            self.along(True, 1 + 2 * side),
        )

    def send_relay(self, o):
        self.out[0, o] = self.product(2, o).astype(BF16)
        self.copy(0, o).start()

    def send_fresh(self, o):
        self.out[1, o] = self.product(3 - 2 * lax.rem(o, 2), o).astype(BF16)
        self.copy(1, o).start()

    def send_joined(self, o):
        value = self.product(1 + 2 * lax.rem(o, 2), o)
        self.copy(0, o).wait_recv()
        self.out[2, o] = (value + self.relay[o].astype(F32)).astype(BF16)
        self.copy(2, o).start()

    def keep(self, o):
        self.mine[o] = self.product(0, o)

    def total(self, o):
        for kind in (1, 2):
            self.copy(kind, o).wait_recv()
        return self.mine[o] + self.ring[0, o].astype(F32) + self.ring[1, o].astype(F32)

    def halves(self, which):
        return remote(
            self.q.at[1, pl.ds(128 * which, 128), :], self.relay2.at[which], self.ss2.at[which],
            self.rs2.at[which], self.along(False, 1 + 2 * which),
        )

    def ends(self, which):
        return remote(
            self.q.at[2 * which], self.ring2.at[which],
            self.ss2.at[2 + which], self.rs2.at[2 + which], self.along(False, 1 + 2 * which),
        )

    def turn(self):
        self.q[1] = self.total(2).astype(BF16)
        for which in (0, 1):
            self.halves(which).start()

    def join(self):
        for which in (0, 1):
            value = self.total(1 + 2 * which)
            self.halves(which).wait_recv()
            met = pl.ds(128 * which, 128)
            rest = slice(128, 256) if which == 0 else slice(0, 128)
            same = slice(0, 128) if which == 0 else slice(128, 256)
            self.q[2 * which, met, :] = (value[same] + self.relay2[which].astype(F32)).astype(BF16)
            self.q[2 * which, pl.ds(128 - 128 * which, 128), :] = value[rest].astype(BF16)
            self.ends(which).start()

    def finish(self, result):
        value = self.total(0)
        for which in (0, 1):
            self.ends(which).wait_recv()
        result[self.rows, :] = value + self.ring2[0].astype(F32) + self.ring2[1].astype(F32)

    def drain(self):
        def one(o, carry):
            for kind in range(3):
                self.copy(kind, o).wait_send()
            return carry

        lax.fori_loop(0, 4, one, 0)
        for which in (0, 1):
            self.halves(which).wait_send()
            self.ends(which).wait_send()


class WeightSums:
    def __init__(self, *sums):
        self.sums = sums

    def over(self, low, high, distance_of, names):
        def one(t, carry):
            for name in names:
                for one_sum in self.sums:
                    getattr(one_sum, name)(distance_of(t))
            return carry

        lax.fori_loop(low, high, one, 0)

    def relay(self):
        self.over(2, 6, lambda t: lax.rem(t, 4), ("send_relay",))

    def fresh(self):
        self.over(2, 4, lambda t: t, ("send_fresh",))

    def joined(self):
        self.over(2, 4, lambda t: t, ("send_joined",))

    def others(self):
        self.over(0, 2, lambda t: 1 - t, ("send_fresh", "send_joined"))

    def keep(self):
        self.over(0, 4, lambda t: t, ("keep",))

    def turn(self):
        for one_sum in self.sums:
            one_sum.turn()

    def join(self):
        for one_sum in self.sums:
            one_sum.join()

    def finish(self, result):
        for one_sum in self.sums:
            one_sum.finish(result)

    def drain(self):
        for one_sum in self.sums:
            one_sum.drain()


class RowSum:
    def __init__(self, place, parts, came, send_sem, recv_sem):
        self.p, self.parts, self.came = place, parts, came
        self.ss, self.rs = send_sem, recv_sem

    def block(self, d, s):
        return lax.rem(self.p.m + (4 - s if d == 0 else 4 + s), NMP)

    def copy(self, d, s, part):
        cols = pl.ds(part * HALF, HALF)
        return remote(
            self.parts.at[self.block(d, s), :, cols], self.came.at[d, s, :, cols],
            self.ss.at[d, s, part], self.rs.at[d, s, part], self.p.along_z(1 if d == 0 else NMP - 1),
        )

    def begin(self, part):
        self.copy(part, 0, part).start()
        self.copy(1 - part, 1, part).start()

    def step(self, s):
        for fresh in (True, False):
            for d in (0, 1):
                part = 1 - d if fresh else d
                if fresh and s == 1:
                    continue
                self.copy(d, s - 1, part).wait_recv()
                cols = pl.ds(part * HALF, HALF)
                to = self.block(d, s)
                self.parts[to, :, cols] = (
                    self.parts[to, :, cols].astype(F32) + self.came[d, s - 1, :, cols].astype(F32)
                ).astype(BF16)
                self.copy(d, s, part).start()

    def finish(self, result):
        for d in (0, 1):
            for part in (0, 1):
                self.copy(d, 3, part).wait_recv()
        result[...] = (
            self.parts[self.p.m].astype(F32)
            + self.came[0, 3].astype(F32)
            + self.came[1, 3].astype(F32)
        ).astype(BF16)

    def drain(self):
        for d in (0, 1):
            for s in range(4):
                for part in (0, 1):
                    if s > 0 or part == d:
                        self.copy(d, s, part).wait_send()


class GateSum:
    def __init__(self, place, parts, row, total, send_sem, recv_sem):
        self.p = place
        self.parts, self.row, self.total = parts, row, total
        self.ss, self.rs = send_sem, recv_sem
        self.chip = lax.div(place.c, 2)
        view = total.at[place.k]
        self.pair = remote(view, view, send_sem.at[2, 0], recv_sem.at[2, 0], place.other_core())

    def rows(self, chip):
        return pl.ds(pl.multiple_of(chip * 16, 16), 16)

    def copy(self, which, o, arriving):
        owner = lax.rem(self.chip + 16 - o, 16) if arriving else self.chip
        peer = lax.rem(self.chip + o, 16)
        if which == 0:
            src, dst = self.parts.at[:, self.rows(peer), :], self.row.at[owner]
        else:
            src = dst = self.total.at[self.p.k, :, self.rows(owner), :]
        return remote(
            src, dst, self.ss.at[which, o], self.rs.at[which, o], (peer * 2 + self.p.k, self.p.m)
        )

    def each(self, act):
        def one(o, carry):
            act(o)
            return carry

        lax.fori_loop(1, 16, one, 0)

    def start(self, which):
        if which == 2:
            self.pair.start()
            return
        if which == 0:
            self.row[self.chip] = self.parts[:, self.rows(self.chip), :]
        else:
            total = self.row[0].astype(F32)
            for o in range(1, 16):
                total = total + self.row[o].astype(F32)
            self.total[self.p.k, :, self.rows(self.chip), :] = total.astype(BF16)
        self.each(lambda o: self.copy(which, o, False).start())

    def finish(self, which):
        if which == 2:
            view = self.total.at[1 - self.p.k]
            remote(view, view, self.ss.at[2, 0], self.rs.at[2, 0], self.p.other_core()).wait_recv()
        else:
            self.each(lambda o: self.copy(which, o, True).wait_recv())

    def drain(self):
        for which in (0, 1):
            self.each(lambda o: self.copy(which, o, False).wait_send())
        self.pair.wait_send()


def minus_expm1(v):
    series = 1.0 + v * (1.0 / 8.0)
    for n in (7, 6, 5, 4, 3, 2):
        series = 1.0 + v * (1.0 / n) * series
    return jnp.where(v > -0.35, -v * series, 1.0 - jnp.exp(v))


def enter(place, partners):
    barrier = pltpu.get_barrier_semaphore()
    for device in partners:
        pl.semaphore_signal(barrier, inc=1, device_id=device, device_id_type=MESH)
    pl.semaphore_wait(barrier, len(partners))


def first_kernel(
    tokens, branch, out_grad, w_in, conv_w, gate_a_h, gate_a_b, gate_i_h, gate_i_b, decay_param, w_out,
    state_init, conv_history,
    tokens_grad, branch_grad, w_in_t, w_out_grad, small, gate_total,
    tok, og, proj, gated, conv_b, ri, tok_o, og_o, conv_o, ri_o, gate_p, gate_row,
    lhs_g, lhs_p, parts, came, branch_v, gate_a, gate_i,
    w_in_v, w_out_v, acc, px, cv, rg, ig, dk, rem, hs, cp, ep, br, gp, cg, kv, edge_s, edge_r, edge_c,
    all_s, all_b, core_m, row_m, col_m,
    w_sem, ts, tr, gs, gr, fs, fr, bs, brs, es, er, ms, mr, zs, zr, ps, pr, qs, qr,
    *sums,
):
    p = Place()
    loads = [
        pltpu.make_async_copy(src, dst, w_sem.at[n])
        for n, (src, dst) in enumerate(
            (
                (tokens, tok.at[p.m]),
                (out_grad, og.at[p.m]),
                (branch, branch_v),
                (gate_a_h, gate_a),
                (gate_i_h, gate_i),
                (w_in, w_in_v),
                (w_out, w_out_v),
            )
        )
    ]
    for load in loads:
        load.start()
    enter(p, [p.along_z(1), p.along_z(NMP - 1)] + [p.along_ctx(o) for o in range(1, 32)])
    tokens_in = Gather(p, tok, ts, tr)
    grads_in = Gather(p, og, gs, gr)
    loads[0].wait()
    tokens_in.send(0)

    def wide(row):
        return jnp.broadcast_to(row.reshape(1, CH), (8, CH))

    taps = conv_w[...].astype(F32)
    for j in range(4):
        kv[j] = wide(taps[j : j + 1])
    kv[4] = wide(gate_a_b[...])
    kv[5] = wide(gate_i_b[...])
    negative = wide(-decay_param[...])
    small_exp = jnp.exp(-jnp.abs(negative))
    one_more = 1.0 + small_exp
    gap = one_more - 1.0
    log_part = jnp.where(
        gap == 0.0, small_exp, jnp.log(one_more) * (small_exp / jnp.where(gap == 0.0, 1.0, gap))
    )
    kv[6] = jnp.maximum(negative, 0.0) + log_part
    loads[1].wait()
    loads[2].wait()
    br[...] = to_segments(branch_v[...].astype(F32))

    tokens_in.arrive(0)
    grads_in.send(0)
    for load in loads[3:]:
        load.wait()
    tokens_in.arrive(1)
    tokens_in.arrive(2)
    grads_in.arrive(0)
    tokens_in.arrive(3)
    other_tokens = CoreColumns(p, tok, tok_o, ps.at[0], pr.at[0])
    other_grads = CoreColumns(p, og, og_o, ps.at[1], pr.at[1])
    other_conv = CorePair(p, conv_b, conv_o, ps.at[2], pr.at[2])
    other_gated = CorePair(p, lhs_g.at[0], lhs_g.at[1], ps.at[3], pr.at[3])
    other_proj = CorePair(p, lhs_p.at[0], lhs_p.at[1], ps.at[4], pr.at[4])
    other_gate = CorePair(p, ri.at[1 - p.k], ri_o, ps.at[5], pr.at[5])
    pairs = [other_tokens, other_grads, other_conv, other_gated, other_proj, other_gate]
    w_out_sum = WeightSums(
        WeightSum(p, True, lhs_g, og, og_o, sums[:11]),
        WeightSum(p, False, lhs_g, og, og_o, sums[11:22]),
    )
    w_in_sum = WeightSums(
        WeightSum(p, True, lhs_p, tok, tok_o, sums[22:33]),
        WeightSum(p, False, lhs_p, tok, tok_o, sums[33:]),
    )
    row_sum = RowSum(p, parts, came, zs, zr)
    gate_sum = GateSum(p, gate_p, gate_row, gate_total, qs, qr)
    total_sum = Fold(p, core_m, row_m, col_m, ms, mr)
    other_tokens.start()

    acc[...] = jnp.zeros_like(acc)

    def project(n, carry):
        at = pl.ds(pl.multiple_of(n * 512, 512), 512)
        acc[...] += jnp.dot(
            tok[:, :, at].reshape(256, 512), w_in_v[at, :], preferred_element_type=F32
        )
        return carry

    lax.fori_loop(0, 8, project, 0)
    edge_s[...] = acc[pl.ds(240, 16), :].astype(BF16)
    forward_edge = remote(edge_s, edge_r, es.at[0], er.at[0], p.along_ctx(1))
    forward_edge.start()
    px[pl.ds(3, 32)] = to_segments(acc[...].astype(BF16).astype(F32))

    lane8 = lax.broadcasted_iota(jnp.int32, (8, CH), 0)
    forward_edge.wait_recv()
    first = p.c == 0
    before = edge_r[...].astype(F32)[13:16]
    before = jnp.where(first, conv_history[...].astype(F32), before)
    for j in range(3):
        turned = pltpu.roll(px[32 + j], 1, 0)
        px[j] = jnp.where(lane8 == 0, wide(before[j : j + 1]), turned)

    def convolve(n, carry):
        total = kv[0] * px[pl.ds(2 * n + 3, 2)]
        for j in (1, 2, 3):
            total = total + kv[j] * px[pl.ds(2 * n + 3 - j, 2)]
        rounded = total.astype(BF16)
        cv[pl.ds(2 * n, 2)] = rounded.astype(F32)
        conv_b[pl.ds(pl.multiple_of(16 * n, 16), 16), :] = rounded.reshape(16, CH)
        return carry

    lax.fori_loop(0, 16, convolve, 0)
    other_conv.start()
    for b in (0, 1):
        cols = pl.ds(b * 256, 256)
        rg[:, :, cols] = jnp.dot(
            conv_b[:, cols], gate_a[b], preferred_element_type=F32
        ).reshape(32, 8, 256)
        ig[:, :, cols] = jnp.dot(
            conv_b[:, cols], gate_i[b], preferred_element_type=F32
        ).reshape(32, 8, 256)

    def gates(n, carry):
        h, c = carry
        at = pl.ds(2 * n, 2)
        recur = jax.nn.sigmoid(rg[at] + kv[4])
        inp = jax.nn.sigmoid(ig[at] + kv[5])
        log_decay = -8.0 * recur * kv[6]
        decay = jnp.exp(log_decay)
        remain = minus_expm1(2.0 * log_decay)
        rg[at] = recur
        ig[at] = inp
        dk[at] = decay
        rem[at] = remain
        driven = jnp.sqrt(remain) * inp * cv[at]
        for t in (0, 1):
            h = decay[t] * h + driven[t]
            c = decay[t] * c
            hs[2 * n + 1 + t] = h
            cp[2 * n + t] = c
        return h, c

    h, c = lax.fori_loop(0, 16, gates, (jnp.zeros((8, CH), F32), jnp.ones((8, CH), F32)))
    c_seg = c
    for sh in (1, 2, 4):
        ok = lane8 >= sh
        h, c = (
            jnp.where(ok, h + c * pltpu.roll(h, sh, 0), h),
            jnp.where(ok, c * pltpu.roll(c, sh, 0), c),
        )
    c_before = jnp.where(lane8 == 0, 1.0, pltpu.roll(c, 1, 0))
    h_before = jnp.where(lane8 == 0, 0.0, pltpu.roll(h, 1, 0))
    states = Everyone(p, all_s, fs, fr)
    states.start(jnp.concatenate([c[7:8], h[7:8]], 0))
    grads_in.arrive(1)

    def suffix(n, e):
        ep[31 - n] = e
        return e * dk[31 - n]

    lax.fori_loop(0, 32, suffix, jnp.ones((8, CH), F32))
    states.finish()
    state = state_init[...].reshape(1, CH)
    for o in range(32):
        one = all_s[o]
        state = jnp.where(o < p.c, one[0:1] * state + one[1:2], state)
    state = wide(state)
    seg_state = h_before + c_before * state
    hs[0] = seg_state

    def finish_states(n, carry):
        at = pl.ds(2 * n, 2)
        value = hs[pl.ds(2 * n + 1, 2)] + cp[at] * seg_state
        hs[pl.ds(2 * n + 1, 2)] = value
        cp[at] = value * br[at]
        return carry

    lax.fori_loop(0, 16, finish_states, 0)
    gated[...] = from_segments(cp[...]).astype(BF16)
    lhs_g[0] = gated[...].T
    other_gated.start()

    grads_in.arrive(2)
    grads_in.arrive(3)
    other_grads.start()
    acc[...] = jnp.zeros_like(acc)

    def grad_product(n, carry):
        at = pl.ds(pl.multiple_of(n * 512, 512), 512)
        acc[...] += matmul_nt(og[:, :, at].reshape(256, 512), w_out_v[:, at])
        return carry

    lax.fori_loop(0, 8, grad_product, 0)
    gp[...] = to_segments(acc[...])

    def backward(n, b):
        i = 31 - n
        g = gp[i]
        cp[i] = g * hs[i + 1]
        a = g * br[i] + b
        gp[i] = a
        return dk[i] * a

    b = lax.fori_loop(0, 32, backward, jnp.zeros((8, CH), F32))
    c = c_seg
    for sh in (1, 2, 4):
        ok = lane8 < 8 - sh
        b, c = (
            jnp.where(ok, b + c * pltpu.roll(b, 8 - sh, 0), b),
            jnp.where(ok, c * pltpu.roll(c, 8 - sh, 0), c),
        )
    c_after = jnp.where(lane8 == 7, 1.0, pltpu.roll(c, 7, 0))
    b_after = jnp.where(lane8 == 7, 0.0, pltpu.roll(b, 7, 0))
    adjoints = Everyone(p, all_b, bs, brs)
    adjoints.start(b[0:1])
    other_gated.finish()
    other_grads.finish()
    w_out_sum.relay()
    branch_grad[...] = from_segments(cp[...]).astype(BF16)
    w_out_sum.fresh()
    adjoints.finish()
    later = jnp.zeros((1, CH), F32)
    for o in reversed(range(32)):
        later = jnp.where(o > p.c, all_b[o] + all_s[o][0:1] * later, later)
    later = wide(later)
    seg_later = b_after + c_after * later

    def gate_grads(n, carry):
        sum_a, sum_i, sum_r = carry
        at = pl.ds(2 * n, 2)
        adjoint = gp[at] + ep[at] * seg_later
        decay, remain, inp, recur, wide_conv = dk[at], rem[at], ig[at], rg[at], cv[at]
        scaler = jnp.sqrt(remain)
        scaler_grad = adjoint * inp * wide_conv
        log_grad = adjoint * hs[at] * decay - 2.0 * decay * decay * scaler_grad / jnp.sqrt(
            jnp.maximum(4.0 * remain, 1e-06)
        )
        recur_pre = (log_grad * (-8.0 * kv[6]) * recur * (1.0 - recur)).astype(BF16)
        input_pre = (scaler_grad * scaler * (1.0 - inp)).astype(BF16)
        flat = pl.ds(pl.multiple_of(16 * n, 16), 16)
        ri[0, flat, :] = recur_pre.reshape(16, CH)
        ri[1, flat, :] = input_pre.reshape(16, CH)
        cg[at] = adjoint * scaler * inp
        return (
            sum_a + jnp.sum(recur_pre.astype(F32), 0),
            sum_i + jnp.sum(input_pre.astype(F32), 0),
            sum_r + jnp.sum(log_grad * (-8.0 * recur), 0),
        )

    zero = jnp.zeros((8, CH), F32)
    sum_a, sum_i, sum_r = lax.fori_loop(0, 16, gate_grads, (zero, zero, zero))
    other_gate.start()
    for b in (0, 1):
        cols = pl.ds(b * 256, 256)
        cg[pl.ds(0, 32), :, cols] += (
            matmul_nt(ri[0, :, cols], gate_a[b]) + matmul_nt(ri[1, :, cols], gate_i[b])
        ).reshape(32, 8, 256)
    backward_edge = remote(cg.at[pl.ds(0, 3)], edge_c, es.at[1], er.at[1], p.along_ctx(31))
    backward_edge.start()
    w_out_sum.joined()
    w_out_sum.others()
    w_out_sum.keep()
    backward_edge.wait_recv()
    for j in range(3):
        turned = pltpu.roll(cg[j], 7, 0)
        came = jnp.where(p.c == 31, 0.0, wide(edge_c[j][0:1]))
        cg[32 + j] = jnp.where(lane8 == 7, came, turned)

    def proj_grads(n, carry):
        at = pl.ds(2 * n, 2)
        own = cg[at]
        total = kv[0] * own
        for j in (1, 2, 3):
            total = total + kv[j] * cg[pl.ds(2 * n + j, 2)]
        cp[at] = total
        return tuple(
            carry[j] + jnp.sum(own * px[pl.ds(2 * n + 3 - j, 2)], 0) for j in range(4)
        )

    tap_sums = lax.fori_loop(0, 16, proj_grads, (zero, zero, zero, zero))
    proj[...] = from_segments(cp[...]).astype(BF16)
    lhs_p[0] = proj[...].T
    other_proj.start()
    for part in (0, 1):

        def spread(n, carry):
            at = pl.ds(pl.multiple_of(n * 512, 512), 512)
            parts[:, :, at] = matmul_nt(proj[...], w_in_v[at, :]).astype(BF16).reshape(8, 32, 512)
            return carry

        lax.fori_loop(part * 4, part * 4 + 4, spread, 0)
        row_sum.begin(part)
    rows = [jnp.sum(v, 0, keepdims=True) for v in (*tap_sums, sum_r, sum_a, sum_i)]
    total_sum.start(0, jnp.concatenate(rows + [jnp.zeros((1, CH), F32)], 0))
    other_conv.finish()
    other_gate.finish()
    for b in (0, 1):
        cols = pl.ds(b * 256, 256)
        gate_p[b] = (
            matmul_tn(conv_b[:, cols], ri[p.k, :, cols]) + matmul_tn(conv_o[:, cols], ri_o[:, cols])
        ).astype(BF16)
    gate_sum.start(0)
    other_tokens.finish()
    other_proj.finish()
    w_in_sum.relay()
    w_in_sum.fresh()
    row_sum.step(1)
    w_out_sum.turn()
    w_in_sum.joined()
    w_in_sum.others()
    row_sum.step(2)
    w_in_sum.keep()
    gate_sum.finish(0)
    gate_sum.start(1)
    w_out_sum.join()
    total_sum.finish(0)
    total_sum.start(1, core_m[0] + core_m[1])
    w_in_sum.turn()
    row_sum.step(3)
    w_in_sum.join()
    gate_sum.finish(1)
    gate_sum.start(2)
    total_sum.finish(1)
    total_sum.start(2, row_m[0] + row_m[1] + row_m[2] + row_m[3])
    w_out_sum.finish(w_out_grad)
    w_in_sum.finish(w_in_t)
    total_sum.finish(2)
    small[...] = col_m[0] + col_m[1] + col_m[2] + col_m[3]
    row_sum.finish(tokens_grad)
    gate_sum.finish(2)
    for used in (states, adjoints, total_sum, w_out_sum, w_in_sum, row_sum, gate_sum, *pairs):
        used.drain()
    tokens_in.sent()
    grads_in.sent()
    forward_edge.wait_send()
    backward_edge.wait_send()


def call_first(*args):
    def vm(shape, dtype):
        return pltpu.VMEM(shape, dtype)

    seg = (32, 8, CH)
    tile = (8, CH)
    dma = pltpu.SemaphoreType.DMA
    S = jax.ShapeDtypeStruct
    outs = (
        S((32, DM), BF16),
        S((256, CH), BF16),
        S((CH, 128), F32),
        S((CH, 128), F32),
        S((8, CH), F32),
        S((2, 2, 256, 256), BF16),
    )
    weight = [
        vm((3, 4, 256, 128), BF16),
        vm((4, 256, 128), F32),
        vm((4, 256, 128), BF16),
        vm((2, 4, 256, 128), BF16),
        vm((3, 256, 128), BF16),
        vm((2, 128, 128), BF16),
        vm((2, 256, 128), BF16),
        dma((3, 4)),
        dma((3, 4)),
        dma((4,)),
        dma((4,)),
    ]
    big = {0, 1, 2, 3, 5, 7, 10}
    return pl.pallas_call(
        first_kernel,
        out_shape=outs,
        in_specs=[
            pl.BlockSpec(memory_space=pl.ANY if n in big else pltpu.VMEM) for n in range(13)
        ],
        out_specs=tuple(pl.BlockSpec(memory_space=pltpu.VMEM) for _ in outs),
        scratch_shapes=[
            vm((8, 32, DM), BF16),
            vm((8, 32, DM), BF16),
            vm((256, CH), BF16),
            vm((256, CH), BF16),
            vm((256, CH), BF16),
            vm((2, 256, CH), BF16),
            vm((8, 32, HALF), BF16),
            vm((8, 32, HALF), BF16),
            vm((256, CH), BF16),
            vm((256, CH), BF16),
            vm((2, 256, 256), BF16),
            vm((16, 2, 16, 256), BF16),
            vm((2, CH, 256), BF16),
            vm((2, CH, 256), BF16),
            vm((8, 32, DM), BF16),
            vm((2, 4, 32, DM), BF16),
            vm((256, CH), BF16),
            vm((2, 256, 256), BF16),
            vm((2, 256, 256), BF16),
            vm((DM, CH), BF16),
            vm((CH, DM), BF16),
            vm((256, CH), F32),
            vm((35, 8, CH), F32),
            *[vm(seg, F32) for _ in range(5)],
            vm((33, 8, CH), F32),
            *[vm(seg, F32) for _ in range(4)],
            vm((35, 8, CH), F32),
            vm((7, 8, CH), F32),
            vm((16, CH), BF16),
            vm((16, CH), BF16),
            vm((3, 8, CH), F32),
            vm((32, 2, CH), F32),
            vm((32, 1, CH), F32),
            vm((2, *tile), F32),
            vm((4, *tile), F32),
            vm((4, *tile), F32),
            dma((7,)),
            dma((2, 4, 2)),
            dma((2, 4, 2)),
            dma((2, 4, 2)),
            dma((2, 4, 2)),
            dma((32,)),
            dma((32,)),
            dma((32,)),
            dma((32,)),
            dma((2,)),
            dma((2,)),
            dma((7,)),
            dma((7,)),
            dma((2, 4, 2)),
            dma((2, 4, 2)),
            dma((6,)),
            dma((6,)),
            dma((3, 16)),
            dma((3, 16)),
            *weight,
            *weight,
            *weight,
            *weight,
        ],
        compiler_params=pltpu.CompilerParams(
            collective_id=0, has_side_effects=True, vmem_limit_bytes=56 << 20
        ),
    )(*args)


def last_kernel(
    tokens_grad, branch_grad, w_in_t, w_out_grad, small, gates, decay_param,
    o_tokens, o_branch, o_w_in, o_w_out, o_conv, o_ga, o_gab, o_gi, o_gib, o_decay,
):
    o_tokens[...] = tokens_grad[...]
    o_branch[...] = branch_grad[...]
    o_w_in[...] = w_in_t[...].T
    o_w_out[...] = w_out_grad[...]
    o_conv[...] = small[pl.ds(0, 4), :]
    rows = small[...]
    o_gab[...] = rows[5]
    o_gib[...] = rows[6]
    o_decay[...] = rows[4] * -jax.nn.sigmoid(-decay_param[...])
    o_ga[...] = gates[0].astype(F32)
    o_gi[...] = gates[1].astype(F32)


def shards(*args):
    results = call_first(*args)
    S = jax.ShapeDtypeStruct
    outs = (
        S((32, DM), BF16),
        S((256, CH), BF16),
        S((128, CH), F32),
        S((CH, 128), F32),
        S((4, CH), F32),
        S((2, 256, 256), F32),
        S((CH,), F32),
        S((2, 256, 256), F32),
        S((CH,), F32),
        S((CH,), F32),
    )
    return pl.pallas_call(
        last_kernel,
        out_shape=outs,
        in_specs=[pl.BlockSpec(memory_space=pltpu.VMEM)] * 7,
        out_specs=tuple(pl.BlockSpec(memory_space=pltpu.VMEM) for _ in outs),
    )(*results, args[9])


def solution(mesh):
    placed = (
        P(("ctx", "mp"), None),
        P("ctx", "mp"),
        P(("ctx", "mp"), None),
        P(None, "mp"),
        P(None, "mp"),
        P("mp", None, None),
        P("mp"),
        P("mp", None, None),
        P("mp"),
        P("mp"),
        P("mp", None),
        P("mp"),
        P(None, "mp"),
    )
    return jax.shard_map(
        shards,
        mesh=mesh,
        in_specs=placed,
        out_specs=(
            P(("ctx", "mp"), None),
            P("ctx", "mp"),
            P("ctx", "mp"),
            P("mp", "ctx"),
            P(None, "mp"),
            P("mp", None, None),
            P("mp"),
            P("mp", None, None),
            P("mp"),
            P("mp"),
        ),
        check_vma=False,
    )
```

```python
import jax
import jax.numpy as jnp
from jax import lax
from jax.experimental import pallas as pl
from jax.experimental.pallas import tpu as pltpu
from jax.sharding import PartitionSpec as P

MESH = pl.DeviceIdType.MESH
F32 = jnp.float32
BF16 = jnp.bfloat16
NMP = 8
SEG = 32
CH = 512
DM = 4096
HALF = DM // 2


def matmul_tn(left, right):
    return lax.dot_general(left, right, (((0,), (0,)), ((), ())), preferred_element_type=F32)


def matmul_nt(left, right):
    return lax.dot_general(left, right, (((1,), (1,)), ((), ())), preferred_element_type=F32)


def to_segments(value):
    return jnp.transpose(value.reshape(NMP, SEG, CH), (1, 0, 2))


def from_segments(value):
    return jnp.transpose(value, (1, 0, 2)).reshape(NMP * SEG, CH)


def remote(src, dst, send_sem, recv_sem, device):
    return pltpu.make_async_remote_copy(
        src_ref=src,
        dst_ref=dst,
        send_sem=send_sem,
        recv_sem=recv_sem,
        device_id=device,
        device_id_type=MESH,
    )


class Place:
    def __init__(self):
        self.c = lax.axis_index("ctx")
        self.m = lax.axis_index("mp")
        self.k = lax.rem(self.c, 2)
        self.x = lax.rem(lax.div(self.c, 2), 4)
        self.y = lax.div(self.c, 8)

    def chip(self, y, x, k):
        return (y * 8 + x * 2 + k, self.m)

    def other_core(self):
        return self.chip(self.y, self.x, 1 - self.k)

    def along_x(self, step):
        return self.chip(self.y, lax.rem(self.x + step, 4), self.k)

    def along_y(self, step):
        return self.chip(lax.rem(self.y + step, 4), self.x, self.k)

    def along_z(self, step):
        return (self.c, lax.rem(self.m + step, NMP))

    def along_ctx(self, step):
        return (lax.rem(self.c + step, 32), self.m)


class Gather:
    def __init__(self, place, buf, send_sem, recv_sem):
        self.p, self.buf, self.ss, self.rs = place, buf, send_sem, recv_sem

    def view(self, d, s, part):
        step = (NMP - s) if d == 0 else s
        return self.buf.at[lax.rem(self.p.m + step, NMP), :, pl.ds(part * HALF, HALF)]

    def copy(self, d, s, part, at):
        view = self.view(d, at, part)
        to = self.p.along_z(1 if d == 0 else NMP - 1)
        return remote(view, view, self.ss.at[d, s, part], self.rs.at[d, s, part], to)

    def present(self, d, s, part):
        return s < 3 or part == d

    def send(self, s):
        for part in (0, 1):
            for d in (0, 1):
                if self.present(d, s, part):
                    self.copy(d, s, part, s).start()

    def arrive(self, s):
        for part in (0, 1):
            for d in (0, 1):
                if self.present(d, s, part):
                    self.copy(d, s, part, s + 1).wait_recv()
                    if s < 3 and self.present(d, s + 1, part):
                        self.copy(d, s + 1, part, s + 1).start()

    def sent(self):
        for s in range(4):
            for part in (0, 1):
                for d in (0, 1):
                    if self.present(d, s, part):
                        self.copy(d, s, part, s).wait_send()


class Fold:
    def __init__(self, place, core, row, col, send_sem, recv_sem):
        self.p = place
        self.slots = (core, row, col)
        self.ss, self.rs = send_sem, recv_sem

    def copies(self, which, arriving):
        p, slots = self.p, self.slots[which]
        mine = (p.k, p.x, p.y)[which]
        size = 2 if which == 0 else 4
        base = (0, 1, 4)[which]
        found = []
        for o in range(1, size):
            to = p.other_core() if which == 0 else (p.along_x(o) if which == 1 else p.along_y(o))
            slot = slots.at[lax.rem(mine + size - o, size) if arriving else mine]
            sems = self.ss.at[base + o - 1], self.rs.at[base + o - 1]
            found.append(remote(slot, slot, *sems, to))
        return found

    def start(self, which, value):
        self.slots[which][(self.p.k, self.p.x, self.p.y)[which]] = value
        for copy in self.copies(which, False):
            copy.start()

    def finish(self, which):
        for copy in self.copies(which, True):
            copy.wait_recv()

    def drain(self):
        for which in range(3):
            for copy in self.copies(which, False):
                copy.wait_send()


class Everyone:
    def __init__(self, place, slots, send_sem, recv_sem):
        self.p, self.slots, self.ss, self.rs = place, slots, send_sem, recv_sem

    def copy(self, o, owner):
        slot = self.slots.at[owner]
        return remote(slot, slot, self.ss.at[o], self.rs.at[o], self.p.along_ctx(o))

    def start(self, value):
        self.slots[self.p.c] = value

        def one(t, carry):
            self.copy(1 + lax.rem(t + 17, 31), self.p.c).start()
            return carry

        lax.fori_loop(0, 31, one, 0)

    def finish(self):
        def one(o, carry):
            self.copy(o, lax.rem(self.p.c + 32 - o, 32)).wait_recv()
            return carry

        lax.fori_loop(1, 32, one, 0)

    def drain(self):
        def one(o, carry):
            self.copy(o, self.p.c).wait_send()
            return carry

        lax.fori_loop(1, 32, one, 0)


class CorePair:
    def __init__(self, place, src, dst, send_sem, recv_sem):
        self.copy = remote(src, dst, send_sem, recv_sem, place.other_core())
        self.start, self.finish, self.drain = (
            self.copy.start, self.copy.wait_recv, self.copy.wait_send
        )


class CoreColumns:
    def __init__(self, place, own, other, send_sem, recv_sem):
        self.p, self.own, self.other = place, own, other
        self.ss, self.rs = send_sem, recv_sem
        self.whole = remote(other, other, send_sem, recv_sem, place.other_core())

    def start(self):
        def one(j, carry):
            src = pl.ds(pl.multiple_of((2 * j + 1 - self.p.k) * 128, 128), 128)
            dst = pl.ds(pl.multiple_of(j * 128, 128), 128)
            remote(
                self.own.at[:, :, src], self.other.at[:, :, dst], self.ss, self.rs,
                self.p.other_core(),
            ).start()
            return carry

        lax.fori_loop(0, 16, one, 0)

    def finish(self):
        self.whole.wait_recv()

    def drain(self):
        self.whole.wait_send()


class WeightSum:
    def __init__(self, place, first_x, lhs, own, other, refs):
        self.p, self.first_x = place, first_x
        self.lhs, self.own, self.other = lhs, own, other
        (self.out, self.mine, self.relay, self.ring, self.q, self.relay2, self.ring2,
         self.ss, self.rs, self.ss2, self.rs2) = refs
        self.ia, self.ib = (place.x, place.y) if first_x else (place.y, place.x)
        self.rows = pl.ds(0 if first_x else 256, 256)

    def along(self, first, step):
        return self.p.along_x(step) if first == self.first_x else self.p.along_y(step)

    def columns(self, distance, o):
        pa, pb = lax.rem(self.ia + distance, 4), lax.rem(self.ib + o, 4)
        j = pb * 4 + pa if self.first_x else pa * 4 + pb
        here = pl.ds(pl.multiple_of((2 * j + self.p.k) * 128, 128), 128)
        there = pl.ds(pl.multiple_of(j * 128, 128), 128)
        return (
            self.own[:, :, here].reshape(256, 128), self.other[:, :, there].reshape(256, 128)
        )

    def products(self, one, two):
        one, two = self.columns(*one), self.columns(*two)
        both = [
            jnp.dot(
                self.lhs[n, self.rows, :], jnp.concatenate([one[n], two[n]], 1),
                preferred_element_type=F32,
            )
            for n in (0, 1)
        ]
        both = both[0] + both[1]
        return both[:, :128], both[:, 128:]

    def copy(self, kind, o):
        side = lax.rem(o, 2) if kind != 1 else 1 - lax.rem(o, 2)
        target = self.relay.at[o] if kind == 0 else self.ring.at[kind - 1, o]
        return remote(
            self.out.at[kind, o], target, self.ss.at[kind, o], self.rs.at[kind, o],
            self.along(True, 1 + 2 * side),
        )

    def send_relay(self, o):
        for n, value in enumerate(self.products((2, o), (2, o + 1))):
            self.out[0, o + n] = value.astype(BF16)
            self.copy(0, o + n).start()

    def fresh(self, o, value):
        self.out[1, o] = value.astype(BF16)
        self.copy(1, o).start()

    def joined(self, o, value):
        self.copy(0, o).wait_recv()
        self.out[2, o] = (value + self.relay[o].astype(F32)).astype(BF16)
        self.copy(2, o).start()

    def send_fresh(self):
        for o, value in zip((3, 2), self.products((1, 3), (3, 2))):
            self.fresh(o, value)

    def send_joined(self):
        for o, value in zip((2, 3), self.products((1, 2), (3, 3))):
            self.joined(o, value)

    def send_others(self, o):
        far = 2 * lax.rem(o, 2)
        values = self.products((3 - far, o), (1 + far, o))
        self.fresh(o, values[0])
        self.joined(o, values[1])

    def keep(self, o):
        for n, value in enumerate(self.products((0, o), (0, o + 1))):
            self.mine[o + n] = value

    def total(self, o):
        for kind in (1, 2):
            self.copy(kind, o).wait_recv()
        return self.mine[o] + self.ring[0, o].astype(F32) + self.ring[1, o].astype(F32)

    def halves(self, which):
        return remote(
            self.q.at[1, pl.ds(128 * which, 128), :], self.relay2.at[which], self.ss2.at[which],
            self.rs2.at[which], self.along(False, 1 + 2 * which),
        )

    def ends(self, which):
        return remote(
            self.q.at[2 * which], self.ring2.at[which],
            self.ss2.at[2 + which], self.rs2.at[2 + which], self.along(False, 1 + 2 * which),
        )

    def turn(self):
        self.q[1] = self.total(2).astype(BF16)
        for which in (0, 1):
            self.halves(which).start()

    def join(self):
        for which in (0, 1):
            value = self.total(1 + 2 * which)
            self.halves(which).wait_recv()
            met = pl.ds(128 * which, 128)
            rest = slice(128, 256) if which == 0 else slice(0, 128)
            same = slice(0, 128) if which == 0 else slice(128, 256)
            self.q[2 * which, met, :] = (value[same] + self.relay2[which].astype(F32)).astype(BF16)
            self.q[2 * which, pl.ds(128 - 128 * which, 128), :] = value[rest].astype(BF16)
            self.ends(which).start()

    def finish(self, result, turned):
        value = self.total(0)
        for which in (0, 1):
            self.ends(which).wait_recv()
        value = value + self.ring2[0].astype(F32) + self.ring2[1].astype(F32)
        if turned:
            result[:, self.rows] = value.T
        else:
            result[self.rows, :] = value

    def drain(self):
        def one(o, carry):
            for kind in range(3):
                self.copy(kind, o).wait_send()
            return carry

        lax.fori_loop(0, 4, one, 0)
        for which in (0, 1):
            self.halves(which).wait_send()
            self.ends(which).wait_send()


class WeightSums:
    def __init__(self, *sums):
        self.sums = sums

    def twice(self, name, of):
        def one(t, carry):
            for one_sum in self.sums:
                getattr(one_sum, name)(of(t))
            return carry

        lax.fori_loop(0, 2, one, 0)

    def relay(self):
        self.twice("send_relay", lambda t: 2 - 2 * t)

    def fresh(self):
        for one_sum in self.sums:
            one_sum.send_fresh()

    def joined(self):
        for one_sum in self.sums:
            one_sum.send_joined()

    def others(self):
        self.twice("send_others", lambda t: 1 - t)

    def keep(self):
        self.twice("keep", lambda t: 2 * t)

    def turn(self):
        for one_sum in self.sums:
            one_sum.turn()

    def join(self):
        for one_sum in self.sums:
            one_sum.join()

    def finish(self, result, turned):
        for one_sum in self.sums:
            one_sum.finish(result, turned)

    def drain(self):
        for one_sum in self.sums:
            one_sum.drain()


class RowSum:
    def __init__(self, place, parts, came, send_sem, recv_sem):
        self.p, self.parts, self.came = place, parts, came
        self.ss, self.rs = send_sem, recv_sem

    def block(self, d, s):
        return lax.rem(self.p.m + (4 - s if d == 0 else 4 + s), NMP)

    def copy(self, d, s, part):
        cols = pl.ds(part * HALF, HALF)
        return remote(
            self.parts.at[self.block(d, s), :, cols], self.came.at[d, s, :, cols],
            self.ss.at[d, s, part], self.rs.at[d, s, part], self.p.along_z(1 if d == 0 else NMP - 1),
        )

    def begin(self, part):
        self.copy(part, 0, part).start()
        self.copy(1 - part, 1, part).start()

    def step(self, s):
        for fresh in (True, False):
            for d in (0, 1):
                part = 1 - d if fresh else d
                if fresh and s == 1:
                    continue
                self.copy(d, s - 1, part).wait_recv()
                cols = pl.ds(part * HALF, HALF)
                to = self.block(d, s)
                self.parts[to, :, cols] = (
                    self.parts[to, :, cols].astype(F32) + self.came[d, s - 1, :, cols].astype(F32)
                ).astype(BF16)
                self.copy(d, s, part).start()

    def finish(self, result):
        for d in (0, 1):
            for part in (0, 1):
                self.copy(d, 3, part).wait_recv()
        result[...] = (
            self.parts[self.p.m].astype(F32)
            + self.came[0, 3].astype(F32)
            + self.came[1, 3].astype(F32)
        ).astype(BF16)

    def drain(self):
        for d in (0, 1):
            for s in range(4):
                for part in (0, 1):
                    if s > 0 or part == d:
                        self.copy(d, s, part).wait_send()


class GateSum:
    def __init__(self, place, parts, row, total, send_sem, recv_sem):
        self.p = place
        self.parts, self.row, self.total = parts, row, total
        self.ss, self.rs = send_sem, recv_sem
        self.chip = lax.div(place.c, 2)
        view = total.at[place.k]
        self.pair = remote(view, view, send_sem.at[2, 0], recv_sem.at[2, 0], place.other_core())

    def rows(self, chip):
        return pl.ds(pl.multiple_of(chip * 16, 16), 16)

    def copy(self, which, o, arriving):
        owner = lax.rem(self.chip + 16 - o, 16) if arriving else self.chip
        peer = lax.rem(self.chip + o, 16)
        if which == 0:
            src, dst = self.parts.at[:, self.rows(peer), :], self.row.at[owner]
        else:
            src = dst = self.total.at[self.p.k, :, self.rows(owner), :]
        return remote(
            src, dst, self.ss.at[which, o], self.rs.at[which, o], (peer * 2 + self.p.k, self.p.m)
        )

    def each(self, act):
        def one(o, carry):
            act(o)
            return carry

        lax.fori_loop(1, 16, one, 0)

    def start(self, which):
        if which == 2:
            self.pair.start()
            return
        if which == 0:
            self.row[self.chip] = self.parts[:, self.rows(self.chip), :]
        else:
            total = self.row[0].astype(F32)
            for o in range(1, 16):
                total = total + self.row[o].astype(F32)
            self.total[self.p.k, :, self.rows(self.chip), :] = total.astype(BF16)
        self.each(lambda o: self.copy(which, o, False).start())

    def finish(self, which):
        if which == 2:
            view = self.total.at[1 - self.p.k]
            remote(view, view, self.ss.at[2, 0], self.rs.at[2, 0], self.p.other_core()).wait_recv()
        else:
            self.each(lambda o: self.copy(which, o, True).wait_recv())

    def drain(self):
        for which in (0, 1):
            self.each(lambda o: self.copy(which, o, False).wait_send())
        self.pair.wait_send()


def minus_expm1(v):
    series = 1.0 + v * (1.0 / 8.0)
    for n in (7, 6, 5, 4, 3, 2):
        series = 1.0 + v * (1.0 / n) * series
    return jnp.where(v > -0.35, -v * series, 1.0 - jnp.exp(v))


def enter(place, partners):
    barrier = pltpu.get_barrier_semaphore()
    for device in partners:
        pl.semaphore_signal(barrier, inc=1, device_id=device, device_id_type=MESH)
    pl.semaphore_wait(barrier, len(partners))


def first_kernel(
    tokens, branch, out_grad, w_in, conv_w, gate_a_h, gate_a_b, gate_i_h, gate_i_b, decay_param, w_out,
    state_init, conv_history,
    tokens_grad, branch_grad, w_in_grad, w_out_grad, conv_grad, gate_a_grad, bias_a_grad, gate_i_grad,
    bias_i_grad, decay_grad,
    gate_total, w_in_t, w_out_t, pieces,
    tok, og, proj, gated, conv_b, ri, tok_o, og_o, conv_o, ri_o, gate_p, gate_row,
    lhs_g, lhs_p, parts, came, branch_v, gate_a, gate_i,
    w_in_v, w_out_v, acc, px, cv, rg, ig, dk, rem, hs, cp, ep, br, gp, cg, kv, edge_s, edge_r, edge_c,
    all_s, all_b, core_m, row_m, col_m,
    w_sem, ts, tr, gs, gr, fs, fr, bs, brs, es, er, ms, mr, zs, zr, ps, pr, qs, qr,
    *sums,
):
    p = Place()
    loads = [
        pltpu.make_async_copy(src, dst, w_sem.at[n])
        for n, (src, dst) in enumerate(
            (
                (tokens, tok.at[p.m]),
                (out_grad, og.at[p.m]),
                (branch, branch_v),
                (gate_a_h, gate_a),
                (gate_i_h, gate_i),
                (w_in, w_in_v),
                (w_out, w_out_v),
            )
        )
    ]
    for load in loads:
        load.start()
    enter(p, [p.along_z(1), p.along_z(NMP - 1)] + [p.along_ctx(o) for o in range(1, 32)])
    tokens_in = Gather(p, tok, ts, tr)
    grads_in = Gather(p, og, gs, gr)
    loads[0].wait()
    tokens_in.send(0)

    def wide(row):
        return jnp.broadcast_to(row.reshape(1, CH), (8, CH))

    taps = conv_w[...].astype(F32)
    for j in range(4):
        kv[j] = wide(taps[j : j + 1])
    kv[4] = wide(gate_a_b[...])
    kv[5] = wide(gate_i_b[...])
    negative = wide(-decay_param[...])
    small_exp = jnp.exp(-jnp.abs(negative))
    one_more = 1.0 + small_exp
    gap = one_more - 1.0
    log_part = jnp.where(
        gap == 0.0, small_exp, jnp.log(one_more) * (small_exp / jnp.where(gap == 0.0, 1.0, gap))
    )
    kv[6] = jnp.maximum(negative, 0.0) + log_part
    loads[1].wait()
    loads[2].wait()
    br[...] = to_segments(branch_v[...].astype(F32))

    tokens_in.arrive(0)
    grads_in.send(0)
    for load in loads[3:]:
        load.wait()
    tokens_in.arrive(1)

    def turn_weights(n, carry):
        at = pl.ds(pl.multiple_of(n * 512, 512), 512)
        w_out_t[at, :] = w_out_v[:, at].T
        w_in_t[:, at] = w_in_v[at, :].T
        return carry

    lax.fori_loop(0, 4, turn_weights, 0)
    tokens_in.arrive(2)
    lax.fori_loop(4, 8, turn_weights, 0)
    grads_in.arrive(0)
    tokens_in.arrive(3)
    other_tokens = CoreColumns(p, tok, tok_o, ps.at[0], pr.at[0])
    other_grads = CoreColumns(p, og, og_o, ps.at[1], pr.at[1])
    other_conv = CorePair(p, conv_b, conv_o, ps.at[2], pr.at[2])
    other_gated = CorePair(p, lhs_g.at[0], lhs_g.at[1], ps.at[3], pr.at[3])
    other_proj = CorePair(p, lhs_p.at[0], lhs_p.at[1], ps.at[4], pr.at[4])
    other_gate = CorePair(p, ri.at[1 - p.k], ri_o, ps.at[5], pr.at[5])
    pairs = [other_tokens, other_grads, other_conv, other_gated, other_proj, other_gate]
    w_out_sum = WeightSums(
        WeightSum(p, True, lhs_g, og, og_o, sums[:11]),
        WeightSum(p, False, lhs_g, og, og_o, sums[11:22]),
    )
    w_in_sum = WeightSums(
        WeightSum(p, True, lhs_p, tok, tok_o, sums[22:33]),
        WeightSum(p, False, lhs_p, tok, tok_o, sums[33:]),
    )
    row_sum = RowSum(p, parts, came, zs, zr)
    gate_sum = GateSum(p, gate_p, gate_row, gate_total, qs, qr)
    total_sum = Fold(p, core_m, row_m, col_m, ms, mr)
    other_tokens.start()

    acc[...] = jnp.zeros_like(acc)

    def project(n, carry):
        at = pl.ds(pl.multiple_of(n * 1024, 1024), 1024)
        acc[...] += jnp.dot(
            tok[:, :, at].reshape(256, 1024), w_in_v[at, :], preferred_element_type=F32
        )
        return carry

    lax.fori_loop(0, 4, project, 0)
    edge_s[...] = acc[pl.ds(240, 16), :].astype(BF16)
    forward_edge = remote(edge_s, edge_r, es.at[0], er.at[0], p.along_ctx(1))
    forward_edge.start()
    px[pl.ds(3, 32)] = to_segments(acc[...].astype(BF16).astype(F32))

    lane8 = lax.broadcasted_iota(jnp.int32, (8, CH), 0)
    forward_edge.wait_recv()
    first = p.c == 0
    before = edge_r[...].astype(F32)[13:16]
    before = jnp.where(first, conv_history[...].astype(F32), before)
    for j in range(3):
        turned = pltpu.roll(px[32 + j], 1, 0)
        px[j] = jnp.where(lane8 == 0, wide(before[j : j + 1]), turned)

    def convolve(n, carry):
        total = kv[0] * px[pl.ds(2 * n + 3, 2)]
        for j in (1, 2, 3):
            total = total + kv[j] * px[pl.ds(2 * n + 3 - j, 2)]
        rounded = total.astype(BF16)
        cv[pl.ds(2 * n, 2)] = rounded.astype(F32)
        conv_b[pl.ds(pl.multiple_of(16 * n, 16), 16), :] = rounded.reshape(16, CH)
        return carry

    lax.fori_loop(0, 16, convolve, 0)
    other_conv.start()
    for b in (0, 1):
        cols = pl.ds(b * 256, 256)
        rg[:, :, cols] = jnp.dot(
            conv_b[:, cols], gate_a[b], preferred_element_type=F32
        ).reshape(32, 8, 256)
        ig[:, :, cols] = jnp.dot(
            conv_b[:, cols], gate_i[b], preferred_element_type=F32
        ).reshape(32, 8, 256)

    def gates(n, carry):
        h, c = carry
        at = pl.ds(2 * n, 2)
        recur = jax.nn.sigmoid(rg[at] + kv[4])
        inp = jax.nn.sigmoid(ig[at] + kv[5])
        log_decay = -8.0 * recur * kv[6]
        decay = jnp.exp(log_decay)
        remain = minus_expm1(2.0 * log_decay)
        rg[at] = recur
        ig[at] = inp
        dk[at] = decay
        rem[at] = remain
        driven = jnp.sqrt(remain) * inp * cv[at]
        for t in (0, 1):
            h = decay[t] * h + driven[t]
            c = decay[t] * c
            hs[2 * n + 1 + t] = h
            cp[2 * n + t] = c
        return h, c

    h, c = lax.fori_loop(0, 16, gates, (jnp.zeros((8, CH), F32), jnp.ones((8, CH), F32)))
    c_seg = c
    for sh in (1, 2, 4):
        ok = lane8 >= sh
        h, c = (
            jnp.where(ok, h + c * pltpu.roll(h, sh, 0), h),
            jnp.where(ok, c * pltpu.roll(c, sh, 0), c),
        )
    c_before = jnp.where(lane8 == 0, 1.0, pltpu.roll(c, 1, 0))
    h_before = jnp.where(lane8 == 0, 0.0, pltpu.roll(h, 1, 0))
    states = Everyone(p, all_s, fs, fr)
    states.start(jnp.concatenate([c[7:8], h[7:8]], 0))
    grads_in.arrive(1)

    def suffix(n, e):
        ep[31 - n] = e
        return e * dk[31 - n]

    lax.fori_loop(0, 32, suffix, jnp.ones((8, CH), F32))
    states.finish()
    state = state_init[...].reshape(1, CH)
    for o in range(32):
        one = all_s[o]
        state = jnp.where(o < p.c, one[0:1] * state + one[1:2], state)
    state = wide(state)
    seg_state = h_before + c_before * state
    hs[0] = seg_state

    def finish_states(n, carry):
        at = pl.ds(2 * n, 2)
        value = hs[pl.ds(2 * n + 1, 2)] + cp[at] * seg_state
        hs[pl.ds(2 * n + 1, 2)] = value
        cp[at] = value * br[at]
        return carry

    lax.fori_loop(0, 16, finish_states, 0)
    gated[...] = from_segments(cp[...]).astype(BF16)
    lhs_g[0] = gated[...].T
    other_gated.start()

    def coefficients(n, carry):
        at = pl.ds(2 * n, 2)
        decay, remain, inp, recur, wide_conv = dk[at], rem[at], ig[at], rg[at], cv[at]
        scaler = jnp.sqrt(remain)
        inner = inp * wide_conv
        log_part = hs[at] * decay - 2.0 * decay * decay * inner / jnp.sqrt(
            jnp.maximum(4.0 * remain, 1e-06)
        )
        rate_part = -8.0 * recur * log_part
        rem[at] = scaler * inp
        ig[at] = inner * scaler * (1.0 - inp)
        rg[at] = rate_part
        cv[at] = rate_part * kv[6] * (1.0 - recur)
        return carry

    lax.fori_loop(0, 16, coefficients, 0)
    grads_in.arrive(2)
    there = (0, 1, 7, 2, 6, 3, 5)

    def place_of(offset):
        return lax.rem(p.m + offset, NMP)

    def early_product(n, carry):
        at = pl.ds(pl.multiple_of(n * 1024, 1024), 1024)
        rows = jnp.concatenate([og[place_of(o), :, at] for o in there], 0)
        value = jnp.dot(rows, w_out_t[at, :], preferred_element_type=F32).reshape(7, 32, CH)
        pieces[pl.ds(0, 7)] = jnp.where(n == 0, value, pieces[pl.ds(0, 7)] + value)
        return carry

    def late_product(n, carry):
        at = pl.ds(pl.multiple_of(n * 1024, 1024), 1024)
        return carry + jnp.dot(og[place_of(4), :, at], w_out_t[at, :], preferred_element_type=F32)

    pieces[...] = jnp.zeros_like(pieces)
    lax.fori_loop(0, 4, early_product, 0)
    for n, offset in enumerate(there):
        acc[pl.ds(pl.multiple_of(place_of(offset) * 32, 32), 32), :] = pieces[n]
    grads_in.arrive(3)
    other_grads.start()
    acc[pl.ds(pl.multiple_of(place_of(4) * 32, 32), 32), :] = lax.fori_loop(
        0, 4, late_product, jnp.zeros((32, CH), F32)
    )
    gp[...] = to_segments(acc[...])

    def backward(n, b):
        i = 31 - n
        g = gp[i]
        cp[i] = g * hs[i + 1]
        a = g * br[i] + b
        gp[i] = a
        return dk[i] * a

    b = lax.fori_loop(0, 32, backward, jnp.zeros((8, CH), F32))
    c = c_seg
    for sh in (1, 2, 4):
        ok = lane8 < 8 - sh
        b, c = (
            jnp.where(ok, b + c * pltpu.roll(b, 8 - sh, 0), b),
            jnp.where(ok, c * pltpu.roll(c, 8 - sh, 0), c),
        )
    c_after = jnp.where(lane8 == 7, 1.0, pltpu.roll(c, 7, 0))
    b_after = jnp.where(lane8 == 7, 0.0, pltpu.roll(b, 7, 0))
    adjoints = Everyone(p, all_b, bs, brs)
    adjoints.start(b[0:1])
    other_gated.finish()
    other_grads.finish()
    w_out_sum.relay()
    branch_grad[...] = from_segments(cp[...]).astype(BF16)
    w_out_sum.fresh()
    adjoints.finish()
    later = jnp.zeros((1, CH), F32)
    for o in reversed(range(32)):
        later = jnp.where(o > p.c, all_b[o] + all_s[o][0:1] * later, later)
    later = wide(later)
    seg_later = b_after + c_after * later

    def gate_grads(n, carry):
        sum_a, sum_i, sum_r = carry
        at = pl.ds(2 * n, 2)
        adjoint = gp[at] + ep[at] * seg_later
        recur_pre = (adjoint * cv[at]).astype(BF16)
        input_pre = (adjoint * ig[at]).astype(BF16)
        flat = pl.ds(pl.multiple_of(16 * n, 16), 16)
        ri[0, flat, :] = recur_pre.reshape(16, CH)
        ri[1, flat, :] = input_pre.reshape(16, CH)
        cg[at] = adjoint * rem[at]
        return (
            sum_a + jnp.sum(recur_pre.astype(F32), 0),
            sum_i + jnp.sum(input_pre.astype(F32), 0),
            sum_r + jnp.sum(adjoint * rg[at], 0),
        )

    zero = jnp.zeros((8, CH), F32)
    sum_a, sum_i, sum_r = lax.fori_loop(0, 16, gate_grads, (zero, zero, zero))
    other_gate.start()
    for b in (0, 1):
        cols = pl.ds(b * 256, 256)
        cg[pl.ds(0, 32), :, cols] += (
            matmul_nt(ri[0, :, cols], gate_a[b]) + matmul_nt(ri[1, :, cols], gate_i[b])
        ).reshape(32, 8, 256)
    backward_edge = remote(cg.at[pl.ds(0, 3)], edge_c, es.at[1], er.at[1], p.along_ctx(31))
    backward_edge.start()
    w_out_sum.joined()
    w_out_sum.others()
    w_out_sum.keep()
    backward_edge.wait_recv()
    for j in range(3):
        turned = pltpu.roll(cg[j], 7, 0)
        came = jnp.where(p.c == 31, 0.0, wide(edge_c[j][0:1]))
        cg[32 + j] = jnp.where(lane8 == 7, came, turned)

    def proj_grads(n, carry):
        at = pl.ds(2 * n, 2)
        own = cg[at]
        total = kv[0] * own
        for j in (1, 2, 3):
            total = total + kv[j] * cg[pl.ds(2 * n + j, 2)]
        cp[at] = total
        return tuple(
            carry[j] + jnp.sum(own * px[pl.ds(2 * n + 3 - j, 2)], 0) for j in range(4)
        )

    tap_sums = lax.fori_loop(0, 16, proj_grads, (zero, zero, zero, zero))
    proj[...] = from_segments(cp[...]).astype(BF16)
    lhs_p[0] = proj[...].T
    other_proj.start()
    for part in (0, 1):

        def spread(n, carry):
            at = pl.ds(pl.multiple_of(n * 512, 512), 512)
            value = jnp.dot(proj[...], w_in_t[:, at], preferred_element_type=F32)
            parts[:, :, at] = value.astype(BF16).reshape(8, 32, 512)
            return carry

        lax.fori_loop(part * 4, part * 4 + 4, spread, 0)
        row_sum.begin(part)
    rows = [jnp.sum(v, 0, keepdims=True) for v in (*tap_sums, sum_r, sum_a, sum_i)]
    total_sum.start(0, jnp.concatenate(rows + [jnp.zeros((1, CH), F32)], 0))
    other_conv.finish()
    other_gate.finish()
    for b in (0, 1):
        cols = pl.ds(b * 256, 256)
        gate_p[b] = (
            matmul_tn(conv_b[:, cols], ri[p.k, :, cols]) + matmul_tn(conv_o[:, cols], ri_o[:, cols])
        ).astype(BF16)
    gate_sum.start(0)
    other_tokens.finish()
    other_proj.finish()
    w_in_sum.relay()
    w_in_sum.fresh()
    row_sum.step(1)
    w_out_sum.turn()
    w_in_sum.joined()
    w_in_sum.others()
    row_sum.step(2)
    w_in_sum.keep()
    gate_sum.finish(0)
    gate_sum.start(1)
    w_out_sum.join()
    total_sum.finish(0)
    total_sum.start(1, core_m[0] + core_m[1])
    w_in_sum.turn()
    row_sum.step(3)
    w_in_sum.join()
    gate_sum.finish(1)
    gate_sum.start(2)
    total_sum.finish(1)
    total_sum.start(2, row_m[0] + row_m[1] + row_m[2] + row_m[3])
    gates_out = (gate_a_grad, gate_i_grad)
    w_out_sum.finish(w_out_grad, False)
    w_in_sum.finish(w_in_grad, True)
    total_sum.finish(2)
    small = col_m[0] + col_m[1] + col_m[2] + col_m[3]
    conv_grad[...] = small[0:4]
    bias_a_grad[...] = small[5]
    bias_i_grad[...] = small[6]
    decay_grad[...] = small[4] * -jax.nn.sigmoid(-decay_param[...])
    row_sum.finish(tokens_grad)
    gate_sum.finish(2)
    for n in (0, 1):
        gates_out[n][...] = gate_total[n].astype(F32)
    for used in (states, adjoints, total_sum, w_out_sum, w_in_sum, row_sum, gate_sum, *pairs):
        used.drain()
    tokens_in.sent()
    grads_in.sent()
    forward_edge.wait_send()
    backward_edge.wait_send()


def result(shape, dtype):
    return jax.ShapeDtypeStruct(shape, dtype)


OUTS = (
    result((32, DM), BF16),
    result((256, CH), BF16),
    result((128, CH), F32),
    result((CH, 128), F32),
    result((4, CH), F32),
    result((2, 256, 256), F32),
    result((CH,), F32),
    result((2, 256, 256), F32),
    result((CH,), F32),
    result((CH,), F32),
)


def call_first(*args):
    def vm(shape, dtype):
        return pltpu.VMEM(shape, dtype)

    seg = (32, 8, CH)
    tile = (8, CH)
    dma = pltpu.SemaphoreType.DMA
    outs = OUTS
    weight = [
        vm((3, 4, 256, 128), BF16),
        vm((4, 256, 128), F32),
        vm((4, 256, 128), BF16),
        vm((2, 4, 256, 128), BF16),
        vm((3, 256, 128), BF16),
        vm((2, 128, 128), BF16),
        vm((2, 256, 128), BF16),
        dma((3, 4)),
        dma((3, 4)),
        dma((4,)),
        dma((4,)),
    ]
    big = {0, 1, 2, 3, 5, 7, 10}
    return pl.pallas_call(
        first_kernel,
        out_shape=outs,
        in_specs=[
            pl.BlockSpec(memory_space=pl.ANY if n in big else pltpu.VMEM) for n in range(13)
        ],
        out_specs=tuple(pl.BlockSpec(memory_space=pltpu.VMEM) for _ in outs),
        scratch_shapes=[
            vm((2, 2, 256, 256), BF16),
            vm((CH, DM), BF16),
            vm((DM, CH), BF16),
            vm((8, 32, CH), F32),
            vm((8, 32, DM), BF16),
            vm((8, 32, DM), BF16),
            vm((256, CH), BF16),
            vm((256, CH), BF16),
            vm((256, CH), BF16),
            vm((2, 256, CH), BF16),
            vm((8, 32, HALF), BF16),
            vm((8, 32, HALF), BF16),
            vm((256, CH), BF16),
            vm((256, CH), BF16),
            vm((2, 256, 256), BF16),
            vm((16, 2, 16, 256), BF16),
            vm((2, CH, 256), BF16),
            vm((2, CH, 256), BF16),
            vm((8, 32, DM), BF16),
            vm((2, 4, 32, DM), BF16),
            vm((256, CH), BF16),
            vm((2, 256, 256), BF16),
            vm((2, 256, 256), BF16),
            vm((DM, CH), BF16),
            vm((CH, DM), BF16),
            vm((256, CH), F32),
            vm((35, 8, CH), F32),
            *[vm(seg, F32) for _ in range(5)],
            vm((33, 8, CH), F32),
            *[vm(seg, F32) for _ in range(4)],
            vm((35, 8, CH), F32),
            vm((7, 8, CH), F32),
            vm((16, CH), BF16),
            vm((16, CH), BF16),
            vm((3, 8, CH), F32),
            vm((32, 2, CH), F32),
            vm((32, 1, CH), F32),
            vm((2, *tile), F32),
            vm((4, *tile), F32),
            vm((4, *tile), F32),
            dma((7,)),
            dma((2, 4, 2)),
            dma((2, 4, 2)),
            dma((2, 4, 2)),
            dma((2, 4, 2)),
            dma((32,)),
            dma((32,)),
            dma((32,)),
            dma((32,)),
            dma((2,)),
            dma((2,)),
            dma((7,)),
            dma((7,)),
            dma((2, 4, 2)),
            dma((2, 4, 2)),
            dma((6,)),
            dma((6,)),
            dma((3, 16)),
            dma((3, 16)),
            *weight,
            *weight,
            *weight,
            *weight,
        ],
        compiler_params=pltpu.CompilerParams(
            collective_id=0, has_side_effects=True, vmem_limit_bytes=56 << 20
        ),
    )(*args)


def last_kernel(*refs):
    sems = refs[20]
    copies = [pltpu.make_async_copy(refs[n], refs[10 + n], sems.at[n]) for n in range(10)]
    for copy in copies:
        copy.start()
    for copy in copies:
        copy.wait()


def shards(*args):
    return pl.pallas_call(
        last_kernel,
        out_shape=OUTS,
        in_specs=[pl.BlockSpec(memory_space=pl.ANY)] * 10,
        out_specs=tuple(pl.BlockSpec(memory_space=pl.ANY) for _ in OUTS),
        scratch_shapes=[pltpu.SemaphoreType.DMA((10,))],
    )(*call_first(*args))


def solution(mesh):
    placed = (
        P(("ctx", "mp"), None),
        P("ctx", "mp"),
        P(("ctx", "mp"), None),
        P(None, "mp"),
        P(None, "mp"),
        P("mp", None, None),
        P("mp"),
        P("mp", None, None),
        P("mp"),
        P("mp"),
        P("mp", None),
        P("mp"),
        P(None, "mp"),
    )
    return jax.shard_map(
        shards,
        mesh=mesh,
        in_specs=placed,
        out_specs=(
            P(("ctx", "mp"), None),
            P("ctx", "mp"),
            P("ctx", "mp"),
            P("mp", "ctx"),
            P(None, "mp"),
            P("mp", None, None),
            P("mp"),
            P("mp", None, None),
            P("mp"),
            P("mp"),
        ),
        check_vma=False,
    )
```

```python
import jax
import jax.numpy as jnp
from jax import lax
from jax.experimental import pallas as pl
from jax.experimental.pallas import tpu as pltpu
from jax.sharding import PartitionSpec as P

MESH = pl.DeviceIdType.MESH
F32 = jnp.float32
BF16 = jnp.bfloat16
NMP = 8
SEG = 32
CH = 512
DM = 4096
HALF = DM // 2


def matmul_tn(left, right):
    return lax.dot_general(left, right, (((0,), (0,)), ((), ())), preferred_element_type=F32)


def matmul_nt(left, right):
    return lax.dot_general(left, right, (((1,), (1,)), ((), ())), preferred_element_type=F32)


def to_segments(value):
    return jnp.transpose(value.reshape(NMP, SEG, CH), (1, 0, 2))


def from_segments(value):
    return jnp.transpose(value, (1, 0, 2)).reshape(NMP * SEG, CH)


def remote(src, dst, send_sem, recv_sem, device):
    return pltpu.make_async_remote_copy(
        src_ref=src,
        dst_ref=dst,
        send_sem=send_sem,
        recv_sem=recv_sem,
        device_id=device,
        device_id_type=MESH,
    )


class Place:
    def __init__(self):
        self.c = lax.axis_index("ctx")
        self.m = lax.axis_index("mp")
        self.k = lax.rem(self.c, 2)
        self.x = lax.rem(lax.div(self.c, 2), 4)
        self.y = lax.div(self.c, 8)

    def chip(self, y, x, k):
        return (y * 8 + x * 2 + k, self.m)

    def other_core(self):
        return self.chip(self.y, self.x, 1 - self.k)

    def along_x(self, step):
        return self.chip(self.y, lax.rem(self.x + step, 4), self.k)

    def along_y(self, step):
        return self.chip(lax.rem(self.y + step, 4), self.x, self.k)

    def along_z(self, step):
        return (self.c, lax.rem(self.m + step, NMP))

    def along_ctx(self, step):
        return (lax.rem(self.c + step, 32), self.m)


class Gather:
    def __init__(self, place, buf, send_sem, recv_sem):
        self.p, self.buf, self.ss, self.rs = place, buf, send_sem, recv_sem

    def view(self, d, s, part):
        step = (NMP - s) if d == 0 else s
        return self.buf.at[lax.rem(self.p.m + step, NMP), :, pl.ds(part * HALF, HALF)]

    def copy(self, d, s, part, at):
        view = self.view(d, at, part)
        to = self.p.along_z(1 if d == 0 else NMP - 1)
        return remote(view, view, self.ss.at[d, s, part], self.rs.at[d, s, part], to)

    def present(self, d, s, part):
        return s < 3 or part == d

    def send(self, s):
        for part in (0, 1):
            for d in (0, 1):
                if self.present(d, s, part):
                    self.copy(d, s, part, s).start()

    def arrive(self, s):
        for part in (0, 1):
            for d in (0, 1):
                if self.present(d, s, part):
                    self.copy(d, s, part, s + 1).wait_recv()
                    if s < 3 and self.present(d, s + 1, part):
                        self.copy(d, s + 1, part, s + 1).start()

    def sent(self):
        for s in range(4):
            for part in (0, 1):
                for d in (0, 1):
                    if self.present(d, s, part):
                        self.copy(d, s, part, s).wait_send()


class Fold:
    def __init__(self, place, core, row, col, send_sem, recv_sem):
        self.p = place
        self.slots = (core, row, col)
        self.ss, self.rs = send_sem, recv_sem

    def copies(self, which, arriving):
        p, slots = self.p, self.slots[which]
        mine = (p.k, p.x, p.y)[which]
        size = 2 if which == 0 else 4
        base = (0, 1, 4)[which]
        found = []
        for o in range(1, size):
            to = p.other_core() if which == 0 else (p.along_x(o) if which == 1 else p.along_y(o))
            slot = slots.at[lax.rem(mine + size - o, size) if arriving else mine]
            sems = self.ss.at[base + o - 1], self.rs.at[base + o - 1]
            found.append(remote(slot, slot, *sems, to))
        return found

    def start(self, which, value):
        self.slots[which][(self.p.k, self.p.x, self.p.y)[which]] = value
        for copy in self.copies(which, False):
            copy.start()

    def finish(self, which):
        for copy in self.copies(which, True):
            copy.wait_recv()

    def drain(self):
        for which in range(3):
            for copy in self.copies(which, False):
                copy.wait_send()


class Everyone:
    def __init__(self, place, slots, send_sem, recv_sem):
        self.p, self.slots, self.ss, self.rs = place, slots, send_sem, recv_sem

    def copy(self, o, owner):
        slot = self.slots.at[owner]
        return remote(slot, slot, self.ss.at[o], self.rs.at[o], self.p.along_ctx(o))

    def start(self, value):
        self.slots[self.p.c] = value

        def one(t, carry):
            self.copy(1 + lax.rem(t + 17, 31), self.p.c).start()
            return carry

        lax.fori_loop(0, 31, one, 0)

    def finish(self):
        def one(o, carry):
            self.copy(o, lax.rem(self.p.c + 32 - o, 32)).wait_recv()
            return carry

        lax.fori_loop(1, 32, one, 0)

    def drain(self):
        def one(o, carry):
            self.copy(o, self.p.c).wait_send()
            return carry

        lax.fori_loop(1, 32, one, 0)


class CorePair:
    def __init__(self, place, src, dst, send_sem, recv_sem):
        self.copy = remote(src, dst, send_sem, recv_sem, place.other_core())
        self.start, self.finish, self.drain = (
            self.copy.start, self.copy.wait_recv, self.copy.wait_send
        )


class CoreColumns:
    def __init__(self, place, own, other, send_sem, recv_sem):
        self.p, self.own, self.other = place, own, other
        self.ss, self.rs = send_sem, recv_sem
        self.whole = remote(other, other, send_sem, recv_sem, place.other_core())

    def start(self):
        def one(j, carry):
            src = pl.ds(pl.multiple_of((2 * j + 1 - self.p.k) * 128, 128), 128)
            dst = pl.ds(pl.multiple_of(j * 128, 128), 128)
            remote(
                self.own.at[:, :, src], self.other.at[:, :, dst], self.ss, self.rs,
                self.p.other_core(),
            ).start()
            return carry

        lax.fori_loop(0, 16, one, 0)

    def finish(self):
        self.whole.wait_recv()

    def drain(self):
        self.whole.wait_send()


class WeightSum:
    def __init__(self, place, first_x, lhs, own, other, refs):
        self.p, self.first_x = place, first_x
        self.lhs, self.own, self.other = lhs, own, other
        (self.out, self.mine, self.relay, self.ring, self.q, self.relay2, self.ring2,
         self.ss, self.rs, self.ss2, self.rs2) = refs
        self.ia, self.ib = (place.x, place.y) if first_x else (place.y, place.x)
        self.rows = pl.ds(0 if first_x else 256, 256)

    def along(self, first, step):
        return self.p.along_x(step) if first == self.first_x else self.p.along_y(step)

    def columns(self, distance, o):
        pa, pb = lax.rem(self.ia + distance, 4), lax.rem(self.ib + o, 4)
        j = pb * 4 + pa if self.first_x else pa * 4 + pb
        here = pl.ds(pl.multiple_of((2 * j + self.p.k) * 128, 128), 128)
        there = pl.ds(pl.multiple_of(j * 128, 128), 128)
        return (
            self.own[:, :, here].reshape(256, 128), self.other[:, :, there].reshape(256, 128)
        )

    def products(self, one, two):
        one, two = self.columns(*one), self.columns(*two)
        both = [
            jnp.dot(
                self.lhs[n, self.rows, :], jnp.concatenate([one[n], two[n]], 1),
                preferred_element_type=F32,
            )
            for n in (0, 1)
        ]
        both = both[0] + both[1]
        return both[:, :128], both[:, 128:]

    def copy(self, kind, o):
        side = lax.rem(o, 2) if kind != 1 else 1 - lax.rem(o, 2)
        target = self.relay.at[o] if kind == 0 else self.ring.at[kind - 1, o]
        return remote(
            self.out.at[kind, o], target, self.ss.at[kind, o], self.rs.at[kind, o],
            self.along(True, 1 + 2 * side),
        )

    def send_relay(self, o):
        for n, value in enumerate(self.products((2, o), (2, o + 1))):
            self.out[0, o + n] = value.astype(BF16)
            self.copy(0, o + n).start()

    def fresh(self, o, value):
        self.out[1, o] = value.astype(BF16)
        self.copy(1, o).start()

    def joined(self, o, value):
        self.copy(0, o).wait_recv()
        self.out[2, o] = (value + self.relay[o].astype(F32)).astype(BF16)
        self.copy(2, o).start()

    def send_fresh(self):
        for o, value in zip((3, 2), self.products((1, 3), (3, 2))):
            self.fresh(o, value)

    def send_joined(self):
        for o, value in zip((2, 3), self.products((1, 2), (3, 3))):
            self.joined(o, value)

    def send_others(self, o):
        far = 2 * lax.rem(o, 2)
        values = self.products((3 - far, o), (1 + far, o))
        self.fresh(o, values[0])
        self.joined(o, values[1])

    def keep(self, o):
        for n, value in enumerate(self.products((0, o), (0, o + 1))):
            self.mine[o + n] = value

    def total(self, o):
        for kind in (1, 2):
            self.copy(kind, o).wait_recv()
        return self.mine[o] + self.ring[0, o].astype(F32) + self.ring[1, o].astype(F32)

    def halves(self, which):
        return remote(
            self.q.at[1, pl.ds(128 * which, 128), :], self.relay2.at[which], self.ss2.at[which],
            self.rs2.at[which], self.along(False, 1 + 2 * which),
        )

    def ends(self, which):
        return remote(
            self.q.at[2 * which], self.ring2.at[which],
            self.ss2.at[2 + which], self.rs2.at[2 + which], self.along(False, 1 + 2 * which),
        )

    def turn(self):
        self.q[1] = self.total(2).astype(BF16)
        for which in (0, 1):
            self.halves(which).start()

    def join(self):
        for which in (0, 1):
            value = self.total(1 + 2 * which)
            self.halves(which).wait_recv()
            met = pl.ds(128 * which, 128)
            rest = slice(128, 256) if which == 0 else slice(0, 128)
            same = slice(0, 128) if which == 0 else slice(128, 256)
            self.q[2 * which, met, :] = (value[same] + self.relay2[which].astype(F32)).astype(BF16)
            self.q[2 * which, pl.ds(128 - 128 * which, 128), :] = value[rest].astype(BF16)
            self.ends(which).start()

    def finish(self, result, turned):
        value = self.total(0)
        for which in (0, 1):
            self.ends(which).wait_recv()
        value = value + self.ring2[0].astype(F32) + self.ring2[1].astype(F32)
        if turned:
            result[:, self.rows] = value.T
        else:
            result[self.rows, :] = value

    def drain(self):
        def one(o, carry):
            for kind in range(3):
                self.copy(kind, o).wait_send()
            return carry

        lax.fori_loop(0, 4, one, 0)
        for which in (0, 1):
            self.halves(which).wait_send()
            self.ends(which).wait_send()


class WeightSums:
    def __init__(self, *sums):
        self.sums = sums

    def twice(self, name, of):
        def one(t, carry):
            for one_sum in self.sums:
                getattr(one_sum, name)(of(t))
            return carry

        lax.fori_loop(0, 2, one, 0)

    def relay(self):
        self.twice("send_relay", lambda t: 2 - 2 * t)

    def fresh(self):
        for one_sum in self.sums:
            one_sum.send_fresh()

    def joined(self):
        for one_sum in self.sums:
            one_sum.send_joined()

    def others(self):
        self.twice("send_others", lambda t: 1 - t)

    def keep(self):
        self.twice("keep", lambda t: 2 * t)

    def turn(self):
        for one_sum in self.sums:
            one_sum.turn()

    def join(self):
        for one_sum in self.sums:
            one_sum.join()

    def finish(self, result, turned):
        for one_sum in self.sums:
            one_sum.finish(result, turned)

    def drain(self):
        for one_sum in self.sums:
            one_sum.drain()


class RowSum:
    def __init__(self, place, parts, came, send_sem, recv_sem):
        self.p, self.parts, self.came = place, parts, came
        self.ss, self.rs = send_sem, recv_sem

    def block(self, d, s):
        return lax.rem(self.p.m + (4 - s if d == 0 else 4 + s), NMP)

    def copy(self, d, s, part):
        cols = pl.ds(part * HALF, HALF)
        return remote(
            self.parts.at[self.block(d, s), :, cols], self.came.at[d, s, :, cols],
            self.ss.at[d, s, part], self.rs.at[d, s, part], self.p.along_z(1 if d == 0 else NMP - 1),
        )

    def begin(self, part):
        self.copy(part, 0, part).start()
        self.copy(1 - part, 1, part).start()

    def step(self, s):
        for fresh in (True, False):
            for d in (0, 1):
                part = 1 - d if fresh else d
                if fresh and s == 1:
                    continue
                self.copy(d, s - 1, part).wait_recv()
                cols = pl.ds(part * HALF, HALF)
                to = self.block(d, s)
                self.parts[to, :, cols] = (
                    self.parts[to, :, cols].astype(F32) + self.came[d, s - 1, :, cols].astype(F32)
                ).astype(BF16)
                self.copy(d, s, part).start()

    def finish(self, result):
        for d in (0, 1):
            for part in (0, 1):
                self.copy(d, 3, part).wait_recv()
        result[...] = (
            self.parts[self.p.m].astype(F32)
            + self.came[0, 3].astype(F32)
            + self.came[1, 3].astype(F32)
        ).astype(BF16)

    def drain(self):
        for d in (0, 1):
            for s in range(4):
                for part in (0, 1):
                    if s > 0 or part == d:
                        self.copy(d, s, part).wait_send()


class GateSum:
    def __init__(self, place, parts, row, total, send_sem, recv_sem):
        self.p = place
        self.parts, self.row, self.total = parts, row, total
        self.ss, self.rs = send_sem, recv_sem
        self.chip = lax.div(place.c, 2)
        view = total.at[place.k]
        self.pair = remote(view, view, send_sem.at[2, 0], recv_sem.at[2, 0], place.other_core())

    def rows(self, chip):
        return pl.ds(pl.multiple_of(chip * 16, 16), 16)

    def copy(self, which, o, arriving):
        owner = lax.rem(self.chip + 16 - o, 16) if arriving else self.chip
        peer = lax.rem(self.chip + o, 16)
        if which == 0:
            src, dst = self.parts.at[:, self.rows(peer), :], self.row.at[owner]
        else:
            src = dst = self.total.at[self.p.k, :, self.rows(owner), :]
        return remote(
            src, dst, self.ss.at[which, o], self.rs.at[which, o], (peer * 2 + self.p.k, self.p.m)
        )

    def each(self, act):
        def one(o, carry):
            act(o)
            return carry

        lax.fori_loop(1, 16, one, 0)

    def start(self, which):
        if which == 2:
            self.pair.start()
            return
        if which == 0:
            self.row[self.chip] = self.parts[:, self.rows(self.chip), :]
        else:
            total = self.row[0].astype(F32)
            for o in range(1, 16):
                total = total + self.row[o].astype(F32)
            self.total[self.p.k, :, self.rows(self.chip), :] = total.astype(BF16)
        self.each(lambda o: self.copy(which, o, False).start())

    def finish(self, which):
        if which == 2:
            view = self.total.at[1 - self.p.k]
            remote(view, view, self.ss.at[2, 0], self.rs.at[2, 0], self.p.other_core()).wait_recv()
        else:
            self.each(lambda o: self.copy(which, o, True).wait_recv())

    def drain(self):
        for which in (0, 1):
            self.each(lambda o: self.copy(which, o, False).wait_send())
        self.pair.wait_send()


def minus_expm1(v):
    series = 1.0 + v * (1.0 / 8.0)
    for n in (7, 6, 5, 4, 3, 2):
        series = 1.0 + v * (1.0 / n) * series
    return jnp.where(v > -0.35, -v * series, 1.0 - jnp.exp(v))


def enter(place, partners):
    barrier = pltpu.get_barrier_semaphore()
    for device in partners:
        pl.semaphore_signal(barrier, inc=1, device_id=device, device_id_type=MESH)
    pl.semaphore_wait(barrier, len(partners))


def first_kernel(
    tokens, branch, out_grad, w_in, conv_w, gate_a_h, gate_a_b, gate_i_h, gate_i_b, decay_param, w_out,
    state_init, conv_history,
    tokens_grad, branch_grad, w_in_grad, w_out_grad, conv_grad, gate_a_grad, bias_a_grad, gate_i_grad,
    bias_i_grad, decay_grad,
    gate_total, w_in_t, w_out_t, pieces,
    tok, og, proj, gated, conv_b, ri, tok_o, og_o, conv_o, ri_o, gate_p, gate_row,
    lhs_g, lhs_p, parts, came, branch_v, gate_a, gate_i,
    w_in_v, w_out_v, acc, px, cv, rg, ig, dk, rem, hs, cp, ep, br, gp, cg, kv, edge_s, edge_r, edge_c,
    all_s, all_b, core_m, row_m, col_m,
    w_sem, ts, tr, gs, gr, fs, fr, bs, brs, es, er, ms, mr, zs, zr, ps, pr, qs, qr,
    *sums,
):
    p = Place()
    loads = [
        pltpu.make_async_copy(src, dst, w_sem.at[n])
        for n, (src, dst) in enumerate(
            (
                (tokens, tok.at[p.m]),
                (out_grad, og.at[p.m]),
                (branch, branch_v),
                (gate_a_h, gate_a),
                (gate_i_h, gate_i),
                (w_in, w_in_v),
                (w_out, w_out_v),
            )
        )
    ]
    for load in loads:
        load.start()
    enter(p, [p.along_z(1), p.along_z(NMP - 1)] + [p.along_ctx(o) for o in range(1, 32)])
    tokens_in = Gather(p, tok, ts, tr)
    grads_in = Gather(p, og, gs, gr)
    loads[0].wait()
    tokens_in.send(0)

    def wide(row):
        return jnp.broadcast_to(row.reshape(1, CH), (8, CH))

    taps = conv_w[...].astype(F32)
    for j in range(4):
        kv[j] = wide(taps[j : j + 1])
    kv[4] = wide(gate_a_b[...])
    kv[5] = wide(gate_i_b[...])
    negative = wide(-decay_param[...])
    small_exp = jnp.exp(-jnp.abs(negative))
    one_more = 1.0 + small_exp
    gap = one_more - 1.0
    log_part = jnp.where(
        gap == 0.0, small_exp, jnp.log(one_more) * (small_exp / jnp.where(gap == 0.0, 1.0, gap))
    )
    kv[6] = jnp.maximum(negative, 0.0) + log_part
    loads[1].wait()
    loads[2].wait()
    br[...] = to_segments(branch_v[...].astype(F32))

    tokens_in.arrive(0)
    for load in loads[3:]:
        load.wait()
    tokens_in.arrive(1)

    def turn_weights(n, carry):
        at = pl.ds(pl.multiple_of(n * 512, 512), 512)
        w_out_t[at, :] = w_out_v[:, at].T
        w_in_t[:, at] = w_in_v[at, :].T
        return carry

    lax.fori_loop(0, 4, turn_weights, 0)
    tokens_in.arrive(2)
    lax.fori_loop(4, 8, turn_weights, 0)
    grads_in.send(0)
    tokens_in.arrive(3)
    other_tokens = CoreColumns(p, tok, tok_o, ps.at[0], pr.at[0])
    other_grads = CoreColumns(p, og, og_o, ps.at[1], pr.at[1])
    other_conv = CorePair(p, conv_b, conv_o, ps.at[2], pr.at[2])
    other_gated = CorePair(p, lhs_g.at[0], lhs_g.at[1], ps.at[3], pr.at[3])
    other_proj = CorePair(p, lhs_p.at[0], lhs_p.at[1], ps.at[4], pr.at[4])
    other_gate = CorePair(p, ri.at[1 - p.k], ri_o, ps.at[5], pr.at[5])
    pairs = [other_tokens, other_grads, other_conv, other_gated, other_proj, other_gate]
    w_out_sum = WeightSums(
        WeightSum(p, True, lhs_g, og, og_o, sums[:11]),
        WeightSum(p, False, lhs_g, og, og_o, sums[11:22]),
    )
    w_in_sum = WeightSums(
        WeightSum(p, True, lhs_p, tok, tok_o, sums[22:33]),
        WeightSum(p, False, lhs_p, tok, tok_o, sums[33:]),
    )
    row_sum = RowSum(p, parts, came, zs, zr)
    gate_sum = GateSum(p, gate_p, gate_row, gate_total, qs, qr)
    total_sum = Fold(p, core_m, row_m, col_m, ms, mr)
    other_tokens.start()

    acc[...] = jnp.zeros_like(acc)

    def project(n, carry):
        at = pl.ds(pl.multiple_of(n * 1024, 1024), 1024)
        acc[...] += jnp.dot(
            tok[:, :, at].reshape(256, 1024), w_in_v[at, :], preferred_element_type=F32
        )
        return carry

    lax.fori_loop(0, 4, project, 0)
    edge_s[...] = acc[pl.ds(240, 16), :].astype(BF16)
    forward_edge = remote(edge_s, edge_r, es.at[0], er.at[0], p.along_ctx(1))
    forward_edge.start()
    grads_in.arrive(0)
    px[pl.ds(3, 32)] = to_segments(acc[...].astype(BF16).astype(F32))

    lane8 = lax.broadcasted_iota(jnp.int32, (8, CH), 0)
    forward_edge.wait_recv()
    first = p.c == 0
    before = edge_r[...].astype(F32)[13:16]
    before = jnp.where(first, conv_history[...].astype(F32), before)
    for j in range(3):
        turned = pltpu.roll(px[32 + j], 1, 0)
        px[j] = jnp.where(lane8 == 0, wide(before[j : j + 1]), turned)

    grads_in.arrive(1)

    def convolve(n, carry):
        total = kv[0] * px[pl.ds(2 * n + 3, 2)]
        for j in (1, 2, 3):
            total = total + kv[j] * px[pl.ds(2 * n + 3 - j, 2)]
        rounded = total.astype(BF16)
        cv[pl.ds(2 * n, 2)] = rounded.astype(F32)
        conv_b[pl.ds(pl.multiple_of(16 * n, 16), 16), :] = rounded.reshape(16, CH)
        return carry

    lax.fori_loop(0, 16, convolve, 0)
    other_conv.start()
    for b in (0, 1):
        cols = pl.ds(b * 256, 256)
        rg[:, :, cols] = jnp.dot(
            conv_b[:, cols], gate_a[b], preferred_element_type=F32
        ).reshape(32, 8, 256)
        ig[:, :, cols] = jnp.dot(
            conv_b[:, cols], gate_i[b], preferred_element_type=F32
        ).reshape(32, 8, 256)

    def gates(n, carry):
        h, c = carry
        at = pl.ds(2 * n, 2)
        recur = jax.nn.sigmoid(rg[at] + kv[4])
        inp = jax.nn.sigmoid(ig[at] + kv[5])
        log_decay = -8.0 * recur * kv[6]
        decay = jnp.exp(log_decay)
        remain = minus_expm1(2.0 * log_decay)
        rg[at] = recur
        ig[at] = inp
        dk[at] = decay
        rem[at] = remain
        driven = jnp.sqrt(remain) * inp * cv[at]
        for t in (0, 1):
            h = decay[t] * h + driven[t]
            c = decay[t] * c
            hs[2 * n + 1 + t] = h
            cp[2 * n + t] = c
        return h, c

    h, c = lax.fori_loop(0, 16, gates, (jnp.zeros((8, CH), F32), jnp.ones((8, CH), F32)))
    c_seg = c
    for sh in (1, 2, 4):
        ok = lane8 >= sh
        h, c = (
            jnp.where(ok, h + c * pltpu.roll(h, sh, 0), h),
            jnp.where(ok, c * pltpu.roll(c, sh, 0), c),
        )
    c_before = jnp.where(lane8 == 0, 1.0, pltpu.roll(c, 1, 0))
    h_before = jnp.where(lane8 == 0, 0.0, pltpu.roll(h, 1, 0))
    states = Everyone(p, all_s, fs, fr)
    states.start(jnp.concatenate([c[7:8], h[7:8]], 0))

    def suffix(n, e):
        ep[31 - n] = e
        return e * dk[31 - n]

    lax.fori_loop(0, 32, suffix, jnp.ones((8, CH), F32))
    def coefficients(n, carry):
        at = pl.ds(2 * n, 2)
        decay, remain, inp, recur, wide_conv = dk[at], rem[at], ig[at], rg[at], cv[at]
        scaler = jnp.sqrt(remain)
        inner = inp * wide_conv
        cg[at] = 2.0 * decay * decay * inner / jnp.sqrt(jnp.maximum(4.0 * remain, 1e-06))
        rem[at] = scaler * inp
        ig[at] = inner * scaler * (1.0 - inp)
        rg[at] = -8.0 * recur
        cv[at] = kv[6] * (1.0 - recur)
        return carry

    lax.fori_loop(0, 16, coefficients, 0)
    grads_in.arrive(2)
    there = (0, 1, 7, 2, 6, 3, 5)

    def place_of(offset):
        return lax.rem(p.m + offset, NMP)

    def early_product(n, carry):
        at = pl.ds(pl.multiple_of(n * 1024, 1024), 1024)
        rows = jnp.concatenate([og[place_of(o), :, at] for o in there], 0)
        value = jnp.dot(rows, w_out_t[at, :], preferred_element_type=F32).reshape(7, 32, CH)
        pieces[pl.ds(0, 7)] = jnp.where(n == 0, value, pieces[pl.ds(0, 7)] + value)
        return carry

    def late_product(n, carry):
        at = pl.ds(pl.multiple_of(n * 1024, 1024), 1024)
        return carry + jnp.dot(og[place_of(4), :, at], w_out_t[at, :], preferred_element_type=F32)

    pieces[...] = jnp.zeros_like(pieces)
    lax.fori_loop(0, 4, early_product, 0)
    for n, offset in enumerate(there):
        acc[pl.ds(pl.multiple_of(place_of(offset) * 32, 32), 32), :] = pieces[n]
    states.finish()
    state = state_init[...].reshape(1, CH)
    for o in range(32):
        one = all_s[o]
        state = jnp.where(o < p.c, one[0:1] * state + one[1:2], state)
    state = wide(state)
    seg_state = h_before + c_before * state
    hs[0] = seg_state

    def finish_states(n, carry):
        at = pl.ds(2 * n, 2)
        value = hs[pl.ds(2 * n + 1, 2)] + cp[at] * seg_state
        hs[pl.ds(2 * n + 1, 2)] = value
        cp[at] = value * br[at]
        rate_part = rg[at] * (hs[at] * dk[at] - cg[at])
        rg[at] = rate_part
        cv[at] = rate_part * cv[at]
        return carry

    lax.fori_loop(0, 16, finish_states, 0)
    gated[...] = from_segments(cp[...]).astype(BF16)
    lhs_g[0] = gated[...].T
    other_gated.start()

    grads_in.arrive(3)
    other_grads.start()
    acc[pl.ds(pl.multiple_of(place_of(4) * 32, 32), 32), :] = lax.fori_loop(
        0, 4, late_product, jnp.zeros((32, CH), F32)
    )
    gp[...] = to_segments(acc[...])

    def backward(n, b):
        i = 31 - n
        g = gp[i]
        cp[i] = g * hs[i + 1]
        a = g * br[i] + b
        gp[i] = a
        return dk[i] * a

    b = lax.fori_loop(0, 32, backward, jnp.zeros((8, CH), F32))
    c = c_seg
    for sh in (1, 2, 4):
        ok = lane8 < 8 - sh
        b, c = (
            jnp.where(ok, b + c * pltpu.roll(b, 8 - sh, 0), b),
            jnp.where(ok, c * pltpu.roll(c, 8 - sh, 0), c),
        )
    c_after = jnp.where(lane8 == 7, 1.0, pltpu.roll(c, 7, 0))
    b_after = jnp.where(lane8 == 7, 0.0, pltpu.roll(b, 7, 0))
    adjoints = Everyone(p, all_b, bs, brs)
    adjoints.start(b[0:1])
    other_gated.finish()
    other_grads.finish()
    w_out_sum.relay()
    branch_grad[...] = from_segments(cp[...]).astype(BF16)
    w_out_sum.fresh()
    adjoints.finish()
    later = jnp.zeros((1, CH), F32)
    for o in reversed(range(32)):
        later = jnp.where(o > p.c, all_b[o] + all_s[o][0:1] * later, later)
    later = wide(later)
    seg_later = b_after + c_after * later

    def gate_grads(n, carry):
        sum_a, sum_i, sum_r = carry
        at = pl.ds(2 * n, 2)
        adjoint = gp[at] + ep[at] * seg_later
        recur_pre = (adjoint * cv[at]).astype(BF16)
        input_pre = (adjoint * ig[at]).astype(BF16)
        flat = pl.ds(pl.multiple_of(16 * n, 16), 16)
        ri[0, flat, :] = recur_pre.reshape(16, CH)
        ri[1, flat, :] = input_pre.reshape(16, CH)
        cg[at] = adjoint * rem[at]
        return (
            sum_a + jnp.sum(recur_pre.astype(F32), 0),
            sum_i + jnp.sum(input_pre.astype(F32), 0),
            sum_r + jnp.sum(adjoint * rg[at], 0),
        )

    zero = jnp.zeros((8, CH), F32)
    sum_a, sum_i, sum_r = lax.fori_loop(0, 16, gate_grads, (zero, zero, zero))
    other_gate.start()
    for b in (0, 1):
        cols = pl.ds(b * 256, 256)
        cg[pl.ds(0, 32), :, cols] += (
            matmul_nt(ri[0, :, cols], gate_a[b]) + matmul_nt(ri[1, :, cols], gate_i[b])
        ).reshape(32, 8, 256)
    backward_edge = remote(cg.at[pl.ds(0, 3)], edge_c, es.at[1], er.at[1], p.along_ctx(31))
    backward_edge.start()
    w_out_sum.joined()
    w_out_sum.others()
    w_out_sum.keep()
    backward_edge.wait_recv()
    for j in range(3):
        turned = pltpu.roll(cg[j], 7, 0)
        came = jnp.where(p.c == 31, 0.0, wide(edge_c[j][0:1]))
        cg[32 + j] = jnp.where(lane8 == 7, came, turned)

    def proj_grads(n, carry):
        at = pl.ds(2 * n, 2)
        own = cg[at]
        total = kv[0] * own
        for j in (1, 2, 3):
            total = total + kv[j] * cg[pl.ds(2 * n + j, 2)]
        cp[at] = total
        return tuple(
            carry[j] + jnp.sum(own * px[pl.ds(2 * n + 3 - j, 2)], 0) for j in range(4)
        )

    tap_sums = lax.fori_loop(0, 16, proj_grads, (zero, zero, zero, zero))
    proj[...] = from_segments(cp[...]).astype(BF16)
    lhs_p[0] = proj[...].T
    other_proj.start()
    for part in (0, 1):

        def spread(n, carry):
            at = pl.ds(pl.multiple_of(n * 512, 512), 512)
            value = jnp.dot(proj[...], w_in_t[:, at], preferred_element_type=F32)
            parts[:, :, at] = value.astype(BF16).reshape(8, 32, 512)
            return carry

        lax.fori_loop(part * 4, part * 4 + 4, spread, 0)
        row_sum.begin(part)
    rows = [jnp.sum(v, 0, keepdims=True) for v in (*tap_sums, sum_r, sum_a, sum_i)]
    total_sum.start(0, jnp.concatenate(rows + [jnp.zeros((1, CH), F32)], 0))
    other_conv.finish()
    other_gate.finish()
    for b in (0, 1):
        cols = pl.ds(b * 256, 256)
        gate_p[b] = (
            matmul_tn(conv_b[:, cols], ri[p.k, :, cols]) + matmul_tn(conv_o[:, cols], ri_o[:, cols])
        ).astype(BF16)
    gate_sum.start(0)
    other_tokens.finish()
    other_proj.finish()
    w_in_sum.relay()
    w_in_sum.fresh()
    row_sum.step(1)
    w_out_sum.turn()
    w_in_sum.joined()
    w_in_sum.others()
    row_sum.step(2)
    w_in_sum.keep()
    gate_sum.finish(0)
    gate_sum.start(1)
    w_out_sum.join()
    total_sum.finish(0)
    total_sum.start(1, core_m[0] + core_m[1])
    w_in_sum.turn()
    row_sum.step(3)
    w_in_sum.join()
    gate_sum.finish(1)
    gate_sum.start(2)
    total_sum.finish(1)
    total_sum.start(2, row_m[0] + row_m[1] + row_m[2] + row_m[3])
    gates_out = (gate_a_grad, gate_i_grad)
    w_out_sum.finish(w_out_grad, False)
    w_in_sum.finish(w_in_grad, True)
    total_sum.finish(2)
    small = col_m[0] + col_m[1] + col_m[2] + col_m[3]
    conv_grad[...] = small[0:4]
    bias_a_grad[...] = small[5]
    bias_i_grad[...] = small[6]
    decay_grad[...] = small[4] * -jax.nn.sigmoid(-decay_param[...])
    row_sum.finish(tokens_grad)
    gate_sum.finish(2)
    for n in (0, 1):
        gates_out[n][...] = gate_total[n].astype(F32)
    for used in (states, adjoints, total_sum, w_out_sum, w_in_sum, row_sum, gate_sum, *pairs):
        used.drain()
    tokens_in.sent()
    grads_in.sent()
    forward_edge.wait_send()
    backward_edge.wait_send()


def result(shape, dtype):
    return jax.ShapeDtypeStruct(shape, dtype)


OUTS = (
    result((32, DM), BF16),
    result((256, CH), BF16),
    result((128, CH), F32),
    result((CH, 128), F32),
    result((4, CH), F32),
    result((2, 256, 256), F32),
    result((CH,), F32),
    result((2, 256, 256), F32),
    result((CH,), F32),
    result((CH,), F32),
)


def call_first(*args):
    def vm(shape, dtype):
        return pltpu.VMEM(shape, dtype)

    seg = (32, 8, CH)
    tile = (8, CH)
    dma = pltpu.SemaphoreType.DMA
    outs = OUTS
    weight = [
        vm((3, 4, 256, 128), BF16),
        vm((4, 256, 128), F32),
        vm((4, 256, 128), BF16),
        vm((2, 4, 256, 128), BF16),
        vm((3, 256, 128), BF16),
        vm((2, 128, 128), BF16),
        vm((2, 256, 128), BF16),
        dma((3, 4)),
        dma((3, 4)),
        dma((4,)),
        dma((4,)),
    ]
    big = {0, 1, 2, 3, 5, 7, 10}
    return pl.pallas_call(
        first_kernel,
        out_shape=outs,
        in_specs=[
            pl.BlockSpec(memory_space=pl.ANY if n in big else pltpu.VMEM) for n in range(13)
        ],
        out_specs=tuple(pl.BlockSpec(memory_space=pltpu.VMEM) for _ in outs),
        scratch_shapes=[
            vm((2, 2, 256, 256), BF16),
            vm((CH, DM), BF16),
            vm((DM, CH), BF16),
            vm((8, 32, CH), F32),
            vm((8, 32, DM), BF16),
            vm((8, 32, DM), BF16),
            vm((256, CH), BF16),
            vm((256, CH), BF16),
            vm((256, CH), BF16),
            vm((2, 256, CH), BF16),
            vm((8, 32, HALF), BF16),
            vm((8, 32, HALF), BF16),
            vm((256, CH), BF16),
            vm((256, CH), BF16),
            vm((2, 256, 256), BF16),
            vm((16, 2, 16, 256), BF16),
            vm((2, CH, 256), BF16),
            vm((2, CH, 256), BF16),
            vm((8, 32, DM), BF16),
            vm((2, 4, 32, DM), BF16),
            vm((256, CH), BF16),
            vm((2, 256, 256), BF16),
            vm((2, 256, 256), BF16),
            vm((DM, CH), BF16),
            vm((CH, DM), BF16),
            vm((256, CH), F32),
            vm((35, 8, CH), F32),
            *[vm(seg, F32) for _ in range(5)],
            vm((33, 8, CH), F32),
            *[vm(seg, F32) for _ in range(4)],
            vm((35, 8, CH), F32),
            vm((7, 8, CH), F32),
            vm((16, CH), BF16),
            vm((16, CH), BF16),
            vm((3, 8, CH), F32),
            vm((32, 2, CH), F32),
            vm((32, 1, CH), F32),
            vm((2, *tile), F32),
            vm((4, *tile), F32),
            vm((4, *tile), F32),
            dma((7,)),
            dma((2, 4, 2)),
            dma((2, 4, 2)),
            dma((2, 4, 2)),
            dma((2, 4, 2)),
            dma((32,)),
            dma((32,)),
            dma((32,)),
            dma((32,)),
            dma((2,)),
            dma((2,)),
            dma((7,)),
            dma((7,)),
            dma((2, 4, 2)),
            dma((2, 4, 2)),
            dma((6,)),
            dma((6,)),
            dma((3, 16)),
            dma((3, 16)),
            *weight,
            *weight,
            *weight,
            *weight,
        ],
        compiler_params=pltpu.CompilerParams(
            collective_id=0, has_side_effects=True, vmem_limit_bytes=56 << 20
        ),
    )(*args)


def last_kernel(*refs):
    given, results, held, sems = refs[:10], refs[10:20], refs[20:30], refs[30]
    into = [pltpu.make_async_copy(given[n], held[n], sems.at[0, n]) for n in range(10)]
    out = [pltpu.make_async_copy(held[n], results[n], sems.at[1, n]) for n in range(10)]
    for copy in into:
        copy.start()
    for n in range(10):
        into[n].wait()
        out[n].start()
    for copy in out:
        copy.wait()


def shards(*args):
    return pl.pallas_call(
        last_kernel,
        out_shape=OUTS,
        in_specs=[pl.BlockSpec(memory_space=pl.ANY)] * 10,
        out_specs=tuple(pl.BlockSpec(memory_space=pl.ANY) for _ in OUTS),
        scratch_shapes=[pltpu.VMEM(one.shape, one.dtype) for one in OUTS]
        + [pltpu.SemaphoreType.DMA((2, 10))],
    )(*call_first(*args))


def solution(mesh):
    placed = (
        P(("ctx", "mp"), None),
        P("ctx", "mp"),
        P(("ctx", "mp"), None),
        P(None, "mp"),
        P(None, "mp"),
        P("mp", None, None),
        P("mp"),
        P("mp", None, None),
        P("mp"),
        P("mp"),
        P("mp", None),
        P("mp"),
        P(None, "mp"),
    )
    return jax.shard_map(
        shards,
        mesh=mesh,
        in_specs=placed,
        out_specs=(
            P(("ctx", "mp"), None),
            P("ctx", "mp"),
            P("ctx", "mp"),
            P("mp", "ctx"),
            P(None, "mp"),
            P("mp", None, None),
            P("mp"),
            P("mp", None, None),
            P("mp"),
            P("mp"),
        ),
        check_vma=False,
    )
```

```python
import jax
import jax.numpy as jnp
from jax import lax
from jax.experimental import pallas as pl
from jax.experimental.pallas import tpu as pltpu
from jax.sharding import PartitionSpec as P

MESH = pl.DeviceIdType.MESH
F32 = jnp.float32
BF16 = jnp.bfloat16
NMP = 8
SEG = 32
CH = 512
DM = 4096
HALF = DM // 2


def matmul_tn(left, right):
    return lax.dot_general(left, right, (((0,), (0,)), ((), ())), preferred_element_type=F32)


def matmul_nt(left, right):
    return lax.dot_general(left, right, (((1,), (1,)), ((), ())), preferred_element_type=F32)


def to_segments(value):
    return jnp.transpose(value.reshape(NMP, SEG, CH), (1, 0, 2))


def from_segments(value):
    return jnp.transpose(value, (1, 0, 2)).reshape(NMP * SEG, CH)


def remote(src, dst, send_sem, recv_sem, device):
    return pltpu.make_async_remote_copy(
        src_ref=src,
        dst_ref=dst,
        send_sem=send_sem,
        recv_sem=recv_sem,
        device_id=device,
        device_id_type=MESH,
    )


class Place:
    def __init__(self):
        self.c = lax.axis_index("ctx")
        self.m = lax.axis_index("mp")
        self.k = lax.rem(self.c, 2)
        self.x = lax.rem(lax.div(self.c, 2), 4)
        self.y = lax.div(self.c, 8)

    def chip(self, y, x, k):
        return (y * 8 + x * 2 + k, self.m)

    def other_core(self):
        return self.chip(self.y, self.x, 1 - self.k)

    def along_x(self, step):
        return self.chip(self.y, lax.rem(self.x + step, 4), self.k)

    def along_y(self, step):
        return self.chip(lax.rem(self.y + step, 4), self.x, self.k)

    def along_z(self, step):
        return (self.c, lax.rem(self.m + step, NMP))

    def along_ctx(self, step):
        return (lax.rem(self.c + step, 32), self.m)


class Gather:
    def __init__(self, place, buf, send_sem, recv_sem):
        self.p, self.buf, self.ss, self.rs = place, buf, send_sem, recv_sem

    def view(self, d, s, part):
        step = (NMP - s) if d == 0 else s
        return self.buf.at[lax.rem(self.p.m + step, NMP), :, pl.ds(part * HALF, HALF)]

    def copy(self, d, s, part, at):
        view = self.view(d, at, part)
        to = self.p.along_z(1 if d == 0 else NMP - 1)
        return remote(view, view, self.ss.at[d, s, part], self.rs.at[d, s, part], to)

    def present(self, d, s, part):
        return s < 3 or part == d

    def send(self, s):
        for part in (0, 1):
            for d in (0, 1):
                if self.present(d, s, part):
                    self.copy(d, s, part, s).start()

    def arrive(self, s):
        for part in (0, 1):
            for d in (0, 1):
                if self.present(d, s, part):
                    self.copy(d, s, part, s + 1).wait_recv()
                    if s < 3 and self.present(d, s + 1, part):
                        self.copy(d, s + 1, part, s + 1).start()

    def sent(self):
        for s in range(4):
            for part in (0, 1):
                for d in (0, 1):
                    if self.present(d, s, part):
                        self.copy(d, s, part, s).wait_send()


class Fold:
    def __init__(self, place, core, row, col, send_sem, recv_sem):
        self.p = place
        self.slots = (core, row, col)
        self.ss, self.rs = send_sem, recv_sem

    def copies(self, which, arriving):
        p, slots = self.p, self.slots[which]
        mine = (p.k, p.x, p.y)[which]
        size = 2 if which == 0 else 4
        base = (0, 1, 4)[which]
        found = []
        for o in range(1, size):
            to = p.other_core() if which == 0 else (p.along_x(o) if which == 1 else p.along_y(o))
            slot = slots.at[lax.rem(mine + size - o, size) if arriving else mine]
            sems = self.ss.at[base + o - 1], self.rs.at[base + o - 1]
            found.append(remote(slot, slot, *sems, to))
        return found

    def start(self, which, value):
        self.slots[which][(self.p.k, self.p.x, self.p.y)[which]] = value
        for copy in self.copies(which, False):
            copy.start()

    def finish(self, which):
        for copy in self.copies(which, True):
            copy.wait_recv()

    def drain(self):
        for which in range(3):
            for copy in self.copies(which, False):
                copy.wait_send()


class Everyone:
    def __init__(self, place, slots, send_sem, recv_sem):
        self.p, self.slots, self.ss, self.rs = place, slots, send_sem, recv_sem

    def copy(self, o, owner):
        slot = self.slots.at[owner]
        return remote(slot, slot, self.ss.at[o], self.rs.at[o], self.p.along_ctx(o))

    def start(self, value):
        self.slots[self.p.c] = value

        def one(t, carry):
            self.copy(1 + lax.rem(t + 17, 31), self.p.c).start()
            return carry

        lax.fori_loop(0, 31, one, 0)

    def finish(self):
        def one(o, carry):
            self.copy(o, lax.rem(self.p.c + 32 - o, 32)).wait_recv()
            return carry

        lax.fori_loop(1, 32, one, 0)

    def drain(self):
        def one(o, carry):
            self.copy(o, self.p.c).wait_send()
            return carry

        lax.fori_loop(1, 32, one, 0)


class CorePair:
    def __init__(self, place, src, dst, send_sem, recv_sem):
        self.copy = remote(src, dst, send_sem, recv_sem, place.other_core())
        self.start, self.finish, self.drain = (
            self.copy.start, self.copy.wait_recv, self.copy.wait_send
        )


class CoreColumns:
    def __init__(self, place, own, other, send_sem, recv_sem):
        self.p, self.own, self.other = place, own, other
        self.ss, self.rs = send_sem, recv_sem
        self.whole = remote(other, other, send_sem, recv_sem, place.other_core())

    def start(self):
        def one(j, carry):
            src = pl.ds(pl.multiple_of((2 * j + 1 - self.p.k) * 128, 128), 128)
            dst = pl.ds(pl.multiple_of(j * 128, 128), 128)
            remote(
                self.own.at[:, :, src], self.other.at[:, :, dst], self.ss, self.rs,
                self.p.other_core(),
            ).start()
            return carry

        lax.fori_loop(0, 16, one, 0)

    def finish(self):
        self.whole.wait_recv()

    def drain(self):
        self.whole.wait_send()


class WeightSum:
    def __init__(self, place, first_x, lhs, own, other, refs):
        self.p, self.first_x = place, first_x
        self.lhs, self.own, self.other = lhs, own, other
        (self.out, self.mine, self.relay, self.ring, self.q, self.relay2, self.ring2,
         self.ss, self.rs, self.ss2, self.rs2) = refs
        self.ia, self.ib = (place.x, place.y) if first_x else (place.y, place.x)
        self.rows = pl.ds(0 if first_x else 256, 256)

    def along(self, first, step):
        return self.p.along_x(step) if first == self.first_x else self.p.along_y(step)

    def columns(self, distance, o):
        pa, pb = lax.rem(self.ia + distance, 4), lax.rem(self.ib + o, 4)
        j = pb * 4 + pa if self.first_x else pa * 4 + pb
        here = pl.ds(pl.multiple_of((2 * j + self.p.k) * 128, 128), 128)
        there = pl.ds(pl.multiple_of(j * 128, 128), 128)
        return (
            self.own[:, :, here].reshape(256, 128), self.other[:, :, there].reshape(256, 128)
        )

    def products(self, one, two):
        one, two = self.columns(*one), self.columns(*two)
        both = [
            jnp.dot(
                self.lhs[n, self.rows, :], jnp.concatenate([one[n], two[n]], 1),
                preferred_element_type=F32,
            )
            for n in (0, 1)
        ]
        both = both[0] + both[1]
        return both[:, :128], both[:, 128:]

    def copy(self, kind, o):
        side = lax.rem(o, 2) if kind != 1 else 1 - lax.rem(o, 2)
        target = self.relay.at[o] if kind == 0 else self.ring.at[kind - 1, o]
        return remote(
            self.out.at[kind, o], target, self.ss.at[kind, o], self.rs.at[kind, o],
            self.along(True, 1 + 2 * side),
        )

    def send_relay(self, o):
        for n, value in enumerate(self.products((2, o), (2, o + 1))):
            self.out[0, o + n] = value.astype(BF16)
            self.copy(0, o + n).start()

    def fresh(self, o, value):
        self.out[1, o] = value.astype(BF16)
        self.copy(1, o).start()

    def joined(self, o, value):
        self.copy(0, o).wait_recv()
        self.out[2, o] = (value + self.relay[o].astype(F32)).astype(BF16)
        self.copy(2, o).start()

    def send_fresh(self):
        for o, value in zip((3, 2), self.products((1, 3), (3, 2))):
            self.fresh(o, value)

    def send_joined(self):
        for o, value in zip((2, 3), self.products((1, 2), (3, 3))):
            self.joined(o, value)

    def send_others(self, o):
        far = 2 * lax.rem(o, 2)
        values = self.products((3 - far, o), (1 + far, o))
        self.fresh(o, values[0])
        self.joined(o, values[1])

    def keep(self, o):
        for n, value in enumerate(self.products((0, o), (0, o + 1))):
            self.mine[o + n] = value

    def total(self, o):
        for kind in (1, 2):
            self.copy(kind, o).wait_recv()
        return self.mine[o] + self.ring[0, o].astype(F32) + self.ring[1, o].astype(F32)

    def halves(self, which):
        return remote(
            self.q.at[1, pl.ds(128 * which, 128), :], self.relay2.at[which], self.ss2.at[which],
            self.rs2.at[which], self.along(False, 1 + 2 * which),
        )

    def ends(self, which):
        return remote(
            self.q.at[2 * which], self.ring2.at[which],
            self.ss2.at[2 + which], self.rs2.at[2 + which], self.along(False, 1 + 2 * which),
        )

    def turn(self):
        self.q[1] = self.total(2).astype(BF16)
        for which in (0, 1):
            self.halves(which).start()

    def join(self):
        for which in (0, 1):
            value = self.total(1 + 2 * which)
            self.halves(which).wait_recv()
            met = pl.ds(128 * which, 128)
            rest = slice(128, 256) if which == 0 else slice(0, 128)
            same = slice(0, 128) if which == 0 else slice(128, 256)
            self.q[2 * which, met, :] = (value[same] + self.relay2[which].astype(F32)).astype(BF16)
            self.q[2 * which, pl.ds(128 - 128 * which, 128), :] = value[rest].astype(BF16)
            self.ends(which).start()

    def finish(self, result, turned):
        value = self.total(0)
        for which in (0, 1):
            self.ends(which).wait_recv()
        value = value + self.ring2[0].astype(F32) + self.ring2[1].astype(F32)
        if turned:
            result[:, self.rows] = value.T
        else:
            result[self.rows, :] = value

    def drain(self):
        def one(o, carry):
            for kind in range(3):
                self.copy(kind, o).wait_send()
            return carry

        lax.fori_loop(0, 4, one, 0)
        for which in (0, 1):
            self.halves(which).wait_send()
            self.ends(which).wait_send()


class WeightSums:
    def __init__(self, *sums):
        self.sums = sums

    def twice(self, name, of):
        def one(t, carry):
            for one_sum in self.sums:
                getattr(one_sum, name)(of(t))
            return carry

        lax.fori_loop(0, 2, one, 0)

    def relay(self):
        self.twice("send_relay", lambda t: 2 - 2 * t)

    def fresh(self):
        for one_sum in self.sums:
            one_sum.send_fresh()

    def joined(self):
        for one_sum in self.sums:
            one_sum.send_joined()

    def others(self):
        self.twice("send_others", lambda t: 1 - t)

    def keep(self):
        self.twice("keep", lambda t: 2 * t)

    def turn(self):
        for one_sum in self.sums:
            one_sum.turn()

    def join(self):
        for one_sum in self.sums:
            one_sum.join()

    def finish(self, result, turned):
        for one_sum in self.sums:
            one_sum.finish(result, turned)

    def drain(self):
        for one_sum in self.sums:
            one_sum.drain()


class RowSum:
    def __init__(self, place, parts, came, send_sem, recv_sem):
        self.p, self.parts, self.came = place, parts, came
        self.ss, self.rs = send_sem, recv_sem

    def block(self, d, s):
        return lax.rem(self.p.m + (4 - s if d == 0 else 4 + s), NMP)

    def copy(self, d, s, part):
        cols = pl.ds(part * HALF, HALF)
        return remote(
            self.parts.at[self.block(d, s), :, cols], self.came.at[d, s, :, cols],
            self.ss.at[d, s, part], self.rs.at[d, s, part], self.p.along_z(1 if d == 0 else NMP - 1),
        )

    def begin(self, part):
        self.copy(part, 0, part).start()
        self.copy(1 - part, 1, part).start()

    def step(self, s):
        for fresh in (True, False):
            for d in (0, 1):
                part = 1 - d if fresh else d
                if fresh and s == 1:
                    continue
                self.copy(d, s - 1, part).wait_recv()
                cols = pl.ds(part * HALF, HALF)
                to = self.block(d, s)
                self.parts[to, :, cols] = (
                    self.parts[to, :, cols].astype(F32) + self.came[d, s - 1, :, cols].astype(F32)
                ).astype(BF16)
                self.copy(d, s, part).start()

    def finish(self, result):
        for d in (0, 1):
            for part in (0, 1):
                self.copy(d, 3, part).wait_recv()
        result[...] = (
            self.parts[self.p.m].astype(F32)
            + self.came[0, 3].astype(F32)
            + self.came[1, 3].astype(F32)
        ).astype(BF16)

    def drain(self):
        for d in (0, 1):
            for s in range(4):
                for part in (0, 1):
                    if s > 0 or part == d:
                        self.copy(d, s, part).wait_send()


class GateSum:
    def __init__(self, place, parts, row, total, send_sem, recv_sem):
        self.p = place
        self.parts, self.row, self.total = parts, row, total
        self.ss, self.rs = send_sem, recv_sem
        self.chip = lax.div(place.c, 2)
        view = total.at[place.k]
        self.pair = remote(view, view, send_sem.at[2, 0], recv_sem.at[2, 0], place.other_core())

    def rows(self, chip):
        return pl.ds(pl.multiple_of(chip * 16, 16), 16)

    def copy(self, which, o, arriving):
        owner = lax.rem(self.chip + 16 - o, 16) if arriving else self.chip
        peer = lax.rem(self.chip + o, 16)
        if which == 0:
            src, dst = self.parts.at[:, self.rows(peer), :], self.row.at[owner]
        else:
            src = dst = self.total.at[self.p.k, :, self.rows(owner), :]
        return remote(
            src, dst, self.ss.at[which, o], self.rs.at[which, o], (peer * 2 + self.p.k, self.p.m)
        )

    def each(self, act):
        def one(o, carry):
            act(o)
            return carry

        lax.fori_loop(1, 16, one, 0)

    def start(self, which):
        if which == 2:
            self.pair.start()
            return
        if which == 0:
            self.row[self.chip] = self.parts[:, self.rows(self.chip), :]
        else:
            total = self.row[0].astype(F32)
            for o in range(1, 16):
                total = total + self.row[o].astype(F32)
            self.total[self.p.k, :, self.rows(self.chip), :] = total.astype(BF16)
        self.each(lambda o: self.copy(which, o, False).start())

    def finish(self, which):
        if which == 2:
            view = self.total.at[1 - self.p.k]
            remote(view, view, self.ss.at[2, 0], self.rs.at[2, 0], self.p.other_core()).wait_recv()
        else:
            self.each(lambda o: self.copy(which, o, True).wait_recv())

    def drain(self):
        for which in (0, 1):
            self.each(lambda o: self.copy(which, o, False).wait_send())
        self.pair.wait_send()


def minus_expm1(v):
    series = 1.0 + v * (1.0 / 8.0)
    for n in (7, 6, 5, 4, 3, 2):
        series = 1.0 + v * (1.0 / n) * series
    return jnp.where(v > -0.35, -v * series, 1.0 - jnp.exp(v))


def enter(place, partners):
    barrier = pltpu.get_barrier_semaphore()
    for device in partners:
        pl.semaphore_signal(barrier, inc=1, device_id=device, device_id_type=MESH)
    pl.semaphore_wait(barrier, len(partners))


def first_kernel(
    tokens, branch, out_grad, w_in, conv_w, gate_a_h, gate_a_b, gate_i_h, gate_i_b, decay_param, w_out,
    state_init, conv_history,
    tokens_grad, branch_grad, w_in_grad, w_out_grad, conv_grad, gate_a_grad, bias_a_grad, gate_i_grad,
    bias_i_grad, decay_grad,
    gate_total, w_in_t, w_out_t, pieces,
    tok, og, proj, gated, conv_b, ri, tok_o, og_o, conv_o, ri_o, gate_p, gate_row,
    lhs_g, lhs_p, parts, came, branch_v, gate_a, gate_i,
    w_in_v, w_out_v, acc, px, cv, rg, ig, dk, rem, hs, cp, ep, br, gp, cg, kv, edge_s, edge_r, edge_c,
    all_s, all_b, core_m, row_m, col_m,
    w_sem, ts, tr, gs, gr, fs, fr, bs, brs, es, er, ms, mr, zs, zr, ps, pr, qs, qr,
    *sums,
):
    p = Place()
    loads = [
        pltpu.make_async_copy(src, dst, w_sem.at[n])
        for n, (src, dst) in enumerate(
            (
                (tokens, tok.at[p.m]),
                (out_grad, og.at[p.m]),
                (branch, branch_v),
                (gate_a_h, gate_a),
                (gate_i_h, gate_i),
                (w_in, w_in_v),
                (w_out, w_out_v),
            )
        )
    ]
    for load in loads:
        load.start()
    enter(p, [p.along_z(1), p.along_z(NMP - 1)] + [p.along_ctx(o) for o in range(1, 32)])
    tokens_in = Gather(p, tok, ts, tr)
    grads_in = Gather(p, og, gs, gr)
    loads[0].wait()
    tokens_in.send(0)

    def wide(row):
        return jnp.broadcast_to(row.reshape(1, CH), (8, CH))

    taps = conv_w[...].astype(F32)
    for j in range(4):
        kv[j] = wide(taps[j : j + 1])
    kv[4] = wide(gate_a_b[...])
    kv[5] = wide(gate_i_b[...])
    negative = wide(-decay_param[...])
    small_exp = jnp.exp(-jnp.abs(negative))
    one_more = 1.0 + small_exp
    gap = one_more - 1.0
    log_part = jnp.where(
        gap == 0.0, small_exp, jnp.log(one_more) * (small_exp / jnp.where(gap == 0.0, 1.0, gap))
    )
    kv[6] = jnp.maximum(negative, 0.0) + log_part
    loads[1].wait()
    loads[2].wait()
    br[...] = to_segments(branch_v[...].astype(F32))

    tokens_in.arrive(0)
    for load in loads[3:]:
        load.wait()
    tokens_in.arrive(1)

    def turn_weights(n, carry):
        at = pl.ds(pl.multiple_of(n * 512, 512), 512)
        w_out_t[at, :] = w_out_v[:, at].T
        w_in_t[:, at] = w_in_v[at, :].T
        return carry

    lax.fori_loop(0, 4, turn_weights, 0)
    tokens_in.arrive(2)
    grads_in.send(0)
    lax.fori_loop(4, 8, turn_weights, 0)
    tokens_in.arrive(3)
    other_tokens = CoreColumns(p, tok, tok_o, ps.at[0], pr.at[0])
    other_grads = CoreColumns(p, og, og_o, ps.at[1], pr.at[1])
    other_conv = CorePair(p, conv_b, conv_o, ps.at[2], pr.at[2])
    other_gated = CorePair(p, lhs_g.at[0], lhs_g.at[1], ps.at[3], pr.at[3])
    other_proj = CorePair(p, lhs_p.at[0], lhs_p.at[1], ps.at[4], pr.at[4])
    other_gate = CorePair(p, ri.at[1 - p.k], ri_o, ps.at[5], pr.at[5])
    pairs = [other_tokens, other_grads, other_conv, other_gated, other_proj, other_gate]
    w_out_sum = WeightSums(
        WeightSum(p, True, lhs_g, og, og_o, sums[:11]),
        WeightSum(p, False, lhs_g, og, og_o, sums[11:22]),
    )
    w_in_sum = WeightSums(
        WeightSum(p, True, lhs_p, tok, tok_o, sums[22:33]),
        WeightSum(p, False, lhs_p, tok, tok_o, sums[33:]),
    )
    row_sum = RowSum(p, parts, came, zs, zr)
    gate_sum = GateSum(p, gate_p, gate_row, gate_total, qs, qr)
    total_sum = Fold(p, core_m, row_m, col_m, ms, mr)
    other_tokens.start()

    acc[...] = jnp.zeros_like(acc)

    def project(n, carry):
        at = pl.ds(pl.multiple_of(n * 1024, 1024), 1024)
        acc[...] += jnp.dot(
            tok[:, :, at].reshape(256, 1024), w_in_v[at, :], preferred_element_type=F32
        )
        return carry

    lax.fori_loop(0, 4, project, 0)
    edge_s[...] = acc[pl.ds(240, 16), :].astype(BF16)
    forward_edge = remote(edge_s, edge_r, es.at[0], er.at[0], p.along_ctx(1))
    forward_edge.start()
    grads_in.arrive(0)
    px[pl.ds(3, 32)] = to_segments(acc[...].astype(BF16).astype(F32))

    lane8 = lax.broadcasted_iota(jnp.int32, (8, CH), 0)
    forward_edge.wait_recv()
    first = p.c == 0
    before = edge_r[...].astype(F32)[13:16]
    before = jnp.where(first, conv_history[...].astype(F32), before)
    for j in range(3):
        turned = pltpu.roll(px[32 + j], 1, 0)
        px[j] = jnp.where(lane8 == 0, wide(before[j : j + 1]), turned)

    def convolve(n, carry):
        total = kv[0] * px[pl.ds(2 * n + 3, 2)]
        for j in (1, 2, 3):
            total = total + kv[j] * px[pl.ds(2 * n + 3 - j, 2)]
        rounded = total.astype(BF16)
        cv[pl.ds(2 * n, 2)] = rounded.astype(F32)
        conv_b[pl.ds(pl.multiple_of(16 * n, 16), 16), :] = rounded.reshape(16, CH)
        return carry

    lax.fori_loop(0, 16, convolve, 0)
    other_conv.start()
    for b in (0, 1):
        cols = pl.ds(b * 256, 256)
        rg[:, :, cols] = jnp.dot(
            conv_b[:, cols], gate_a[b], preferred_element_type=F32
        ).reshape(32, 8, 256)
        ig[:, :, cols] = jnp.dot(
            conv_b[:, cols], gate_i[b], preferred_element_type=F32
        ).reshape(32, 8, 256)

    def gates(n, carry):
        h, c = carry
        at = pl.ds(2 * n, 2)
        recur = jax.nn.sigmoid(rg[at] + kv[4])
        inp = jax.nn.sigmoid(ig[at] + kv[5])
        log_decay = -8.0 * recur * kv[6]
        decay = jnp.exp(log_decay)
        remain = minus_expm1(2.0 * log_decay)
        rg[at] = recur
        ig[at] = inp
        dk[at] = decay
        rem[at] = remain
        driven = jnp.sqrt(remain) * inp * cv[at]
        for t in (0, 1):
            h = decay[t] * h + driven[t]
            c = decay[t] * c
            hs[2 * n + 1 + t] = h
            cp[2 * n + t] = c
        return h, c

    h, c = lax.fori_loop(0, 16, gates, (jnp.zeros((8, CH), F32), jnp.ones((8, CH), F32)))
    c_seg = c
    for sh in (1, 2, 4):
        ok = lane8 >= sh
        h, c = (
            jnp.where(ok, h + c * pltpu.roll(h, sh, 0), h),
            jnp.where(ok, c * pltpu.roll(c, sh, 0), c),
        )
    c_before = jnp.where(lane8 == 0, 1.0, pltpu.roll(c, 1, 0))
    h_before = jnp.where(lane8 == 0, 0.0, pltpu.roll(h, 1, 0))
    states = Everyone(p, all_s, fs, fr)
    states.start(jnp.concatenate([c[7:8], h[7:8]], 0))

    def suffix(n, e):
        ep[31 - n] = e
        return e * dk[31 - n]

    lax.fori_loop(0, 32, suffix, jnp.ones((8, CH), F32))
    grads_in.arrive(1)

    def coefficients(n, carry):
        at = pl.ds(2 * n, 2)
        decay, remain, inp, recur, wide_conv = dk[at], rem[at], ig[at], rg[at], cv[at]
        scaler = jnp.sqrt(remain)
        inner = inp * wide_conv
        cg[at] = 2.0 * decay * decay * inner / jnp.sqrt(jnp.maximum(4.0 * remain, 1e-06))
        rem[at] = scaler * inp
        ig[at] = inner * scaler * (1.0 - inp)
        rg[at] = -8.0 * recur
        cv[at] = kv[6] * (1.0 - recur)
        return carry

    lax.fori_loop(0, 16, coefficients, 0)
    grads_in.arrive(2)
    there = (0, 1, 7, 2, 6, 3, 5)

    def place_of(offset):
        return lax.rem(p.m + offset, NMP)

    def early_product(n, carry):
        at = pl.ds(pl.multiple_of(n * 1024, 1024), 1024)
        rows = jnp.concatenate([og[place_of(o), :, at] for o in there], 0)
        value = jnp.dot(rows, w_out_t[at, :], preferred_element_type=F32).reshape(7, 32, CH)
        pieces[pl.ds(0, 7)] = jnp.where(n == 0, value, pieces[pl.ds(0, 7)] + value)
        return carry

    def late_product(n, carry):
        at = pl.ds(pl.multiple_of(n * 1024, 1024), 1024)
        return carry + jnp.dot(og[place_of(4), :, at], w_out_t[at, :], preferred_element_type=F32)

    pieces[...] = jnp.zeros_like(pieces)
    lax.fori_loop(0, 4, early_product, 0)
    for n, offset in enumerate(there):
        acc[pl.ds(pl.multiple_of(place_of(offset) * 32, 32), 32), :] = pieces[n]
    states.finish()
    state = state_init[...].reshape(1, CH)
    for o in range(32):
        one = all_s[o]
        state = jnp.where(o < p.c, one[0:1] * state + one[1:2], state)
    state = wide(state)
    seg_state = h_before + c_before * state
    hs[0] = seg_state

    def finish_states(n, carry):
        at = pl.ds(2 * n, 2)
        value = hs[pl.ds(2 * n + 1, 2)] + cp[at] * seg_state
        hs[pl.ds(2 * n + 1, 2)] = value
        cp[at] = value * br[at]
        rate_part = rg[at] * (hs[at] * dk[at] - cg[at])
        rg[at] = rate_part
        cv[at] = rate_part * cv[at]
        return carry

    lax.fori_loop(0, 16, finish_states, 0)
    gated[...] = from_segments(cp[...]).astype(BF16)
    lhs_g[0] = gated[...].T
    other_gated.start()

    grads_in.arrive(3)
    other_grads.start()
    acc[pl.ds(pl.multiple_of(place_of(4) * 32, 32), 32), :] = lax.fori_loop(
        0, 4, late_product, jnp.zeros((32, CH), F32)
    )
    gp[...] = to_segments(acc[...])

    def backward(n, b):
        i = 31 - n
        g = gp[i]
        cp[i] = g * hs[i + 1]
        a = g * br[i] + b
        gp[i] = a
        return dk[i] * a

    b = lax.fori_loop(0, 32, backward, jnp.zeros((8, CH), F32))
    c = c_seg
    for sh in (1, 2, 4):
        ok = lane8 < 8 - sh
        b, c = (
            jnp.where(ok, b + c * pltpu.roll(b, 8 - sh, 0), b),
            jnp.where(ok, c * pltpu.roll(c, 8 - sh, 0), c),
        )
    c_after = jnp.where(lane8 == 7, 1.0, pltpu.roll(c, 7, 0))
    b_after = jnp.where(lane8 == 7, 0.0, pltpu.roll(b, 7, 0))
    adjoints = Everyone(p, all_b, bs, brs)
    adjoints.start(b[0:1])
    other_gated.finish()
    other_grads.finish()
    w_out_sum.relay()
    branch_grad[...] = from_segments(cp[...]).astype(BF16)
    w_out_sum.fresh()
    adjoints.finish()
    later = jnp.zeros((1, CH), F32)
    for o in reversed(range(32)):
        later = jnp.where(o > p.c, all_b[o] + all_s[o][0:1] * later, later)
    later = wide(later)
    seg_later = b_after + c_after * later

    def gate_grads(n, carry):
        sum_a, sum_i, sum_r = carry
        at = pl.ds(2 * n, 2)
        adjoint = gp[at] + ep[at] * seg_later
        recur_pre = (adjoint * cv[at]).astype(BF16)
        input_pre = (adjoint * ig[at]).astype(BF16)
        flat = pl.ds(pl.multiple_of(16 * n, 16), 16)
        ri[0, flat, :] = recur_pre.reshape(16, CH)
        ri[1, flat, :] = input_pre.reshape(16, CH)
        cg[at] = adjoint * rem[at]
        return (
            sum_a + jnp.sum(recur_pre.astype(F32), 0),
            sum_i + jnp.sum(input_pre.astype(F32), 0),
            sum_r + jnp.sum(adjoint * rg[at], 0),
        )

    zero = jnp.zeros((8, CH), F32)
    def through_gates(low, high):
        rows = pl.ds(low * 8, (high - low) * 8)
        for b in (0, 1):
            cols = pl.ds(b * 256, 256)
            cg[pl.ds(low, high - low), :, cols] += (
                matmul_nt(ri[0, rows, cols], gate_a[b]) + matmul_nt(ri[1, rows, cols], gate_i[b])
            ).reshape(high - low, 8, 256)

    first_sums = lax.fori_loop(0, 2, gate_grads, (zero, zero, zero))
    through_gates(0, 4)
    backward_edge = remote(cg.at[pl.ds(0, 3)], edge_c, es.at[1], er.at[1], p.along_ctx(31))
    backward_edge.start()
    sum_a, sum_i, sum_r = lax.fori_loop(2, 16, gate_grads, first_sums)
    other_gate.start()
    through_gates(4, 32)
    w_out_sum.joined()
    w_out_sum.others()
    backward_edge.wait_recv()
    for j in range(3):
        turned = pltpu.roll(cg[j], 7, 0)
        came = jnp.where(p.c == 31, 0.0, wide(edge_c[j][0:1]))
        cg[32 + j] = jnp.where(lane8 == 7, came, turned)

    def proj_grads(n, carry):
        at = pl.ds(2 * n, 2)
        own = cg[at]
        total = kv[0] * own
        for j in (1, 2, 3):
            total = total + kv[j] * cg[pl.ds(2 * n + j, 2)]
        cp[at] = total
        return tuple(
            carry[j] + jnp.sum(own * px[pl.ds(2 * n + 3 - j, 2)], 0) for j in range(4)
        )

    tap_sums = lax.fori_loop(0, 16, proj_grads, (zero, zero, zero, zero))
    proj[...] = from_segments(cp[...]).astype(BF16)
    lhs_p[0] = proj[...].T
    other_proj.start()
    for part in (0, 1):

        def spread(n, carry):
            at = pl.ds(pl.multiple_of(n * 512, 512), 512)
            value = jnp.dot(proj[...], w_in_t[:, at], preferred_element_type=F32)
            parts[:, :, at] = value.astype(BF16).reshape(8, 32, 512)
            return carry

        lax.fori_loop(part * 4, part * 4 + 4, spread, 0)
        row_sum.begin(part)
        if part == 0:
            other_conv.finish()
            other_gate.finish()
            for b in (0, 1):
                cols = pl.ds(b * 256, 256)
                gate_p[b] = (
                    matmul_tn(conv_b[:, cols], ri[p.k, :, cols])
                    + matmul_tn(conv_o[:, cols], ri_o[:, cols])
                ).astype(BF16)
            gate_sum.start(0)
    rows = [jnp.sum(v, 0, keepdims=True) for v in (*tap_sums, sum_r, sum_a, sum_i)]
    total_sum.start(0, jnp.concatenate(rows + [jnp.zeros((1, CH), F32)], 0))
    other_tokens.finish()
    other_proj.finish()
    w_in_sum.relay()
    w_in_sum.fresh()
    row_sum.step(1)
    w_out_sum.keep()
    w_out_sum.turn()
    w_in_sum.joined()
    w_in_sum.others()
    gate_sum.finish(0)
    gate_sum.start(1)
    row_sum.step(2)
    total_sum.finish(0)
    total_sum.start(1, core_m[0] + core_m[1])
    w_in_sum.keep()
    w_in_sum.turn()
    w_out_sum.join()
    row_sum.step(3)
    gate_sum.finish(1)
    gate_sum.start(2)
    w_in_sum.join()
    total_sum.finish(1)
    total_sum.start(2, row_m[0] + row_m[1] + row_m[2] + row_m[3])
    gates_out = (gate_a_grad, gate_i_grad)
    w_out_sum.finish(w_out_grad, False)
    w_in_sum.finish(w_in_grad, True)
    total_sum.finish(2)
    small = col_m[0] + col_m[1] + col_m[2] + col_m[3]
    conv_grad[...] = small[0:4]
    bias_a_grad[...] = small[5]
    bias_i_grad[...] = small[6]
    decay_grad[...] = small[4] * -jax.nn.sigmoid(-decay_param[...])
    gate_sum.finish(2)
    for n in (0, 1):
        gates_out[n][...] = gate_total[n].astype(F32)
    row_sum.finish(tokens_grad)
    for used in (states, adjoints, total_sum, w_out_sum, w_in_sum, row_sum, gate_sum, *pairs):
        used.drain()
    tokens_in.sent()
    grads_in.sent()
    forward_edge.wait_send()
    backward_edge.wait_send()


def result(shape, dtype):
    return jax.ShapeDtypeStruct(shape, dtype)


OUTS = (
    result((32, DM), BF16),
    result((256, CH), BF16),
    result((128, CH), F32),
    result((CH, 128), F32),
    result((4, CH), F32),
    result((2, 256, 256), F32),
    result((CH,), F32),
    result((2, 256, 256), F32),
    result((CH,), F32),
    result((CH,), F32),
)


def call_first(*args):
    def vm(shape, dtype):
        return pltpu.VMEM(shape, dtype)

    seg = (32, 8, CH)
    tile = (8, CH)
    dma = pltpu.SemaphoreType.DMA
    outs = OUTS
    weight = [
        vm((3, 4, 256, 128), BF16),
        vm((4, 256, 128), F32),
        vm((4, 256, 128), BF16),
        vm((2, 4, 256, 128), BF16),
        vm((3, 256, 128), BF16),
        vm((2, 128, 128), BF16),
        vm((2, 256, 128), BF16),
        dma((3, 4)),
        dma((3, 4)),
        dma((4,)),
        dma((4,)),
    ]
    big = {0, 1, 2, 3, 5, 7, 10}
    return pl.pallas_call(
        first_kernel,
        out_shape=outs,
        in_specs=[
            pl.BlockSpec(memory_space=pl.ANY if n in big else pltpu.VMEM) for n in range(13)
        ],
        out_specs=tuple(pl.BlockSpec(memory_space=pltpu.VMEM) for _ in outs),
        scratch_shapes=[
            vm((2, 2, 256, 256), BF16),
            vm((CH, DM), BF16),
            vm((DM, CH), BF16),
            vm((8, 32, CH), F32),
            vm((8, 32, DM), BF16),
            vm((8, 32, DM), BF16),
            vm((256, CH), BF16),
            vm((256, CH), BF16),
            vm((256, CH), BF16),
            vm((2, 256, CH), BF16),
            vm((8, 32, HALF), BF16),
            vm((8, 32, HALF), BF16),
            vm((256, CH), BF16),
            vm((256, CH), BF16),
            vm((2, 256, 256), BF16),
            vm((16, 2, 16, 256), BF16),
            vm((2, CH, 256), BF16),
            vm((2, CH, 256), BF16),
            vm((8, 32, DM), BF16),
            vm((2, 4, 32, DM), BF16),
            vm((256, CH), BF16),
            vm((2, 256, 256), BF16),
            vm((2, 256, 256), BF16),
            vm((DM, CH), BF16),
            vm((CH, DM), BF16),
            vm((256, CH), F32),
            vm((35, 8, CH), F32),
            *[vm(seg, F32) for _ in range(5)],
            vm((33, 8, CH), F32),
            *[vm(seg, F32) for _ in range(4)],
            vm((35, 8, CH), F32),
            vm((7, 8, CH), F32),
            vm((16, CH), BF16),
            vm((16, CH), BF16),
            vm((3, 8, CH), F32),
            vm((32, 2, CH), F32),
            vm((32, 1, CH), F32),
            vm((2, *tile), F32),
            vm((4, *tile), F32),
            vm((4, *tile), F32),
            dma((7,)),
            dma((2, 4, 2)),
            dma((2, 4, 2)),
            dma((2, 4, 2)),
            dma((2, 4, 2)),
            dma((32,)),
            dma((32,)),
            dma((32,)),
            dma((32,)),
            dma((2,)),
            dma((2,)),
            dma((7,)),
            dma((7,)),
            dma((2, 4, 2)),
            dma((2, 4, 2)),
            dma((6,)),
            dma((6,)),
            dma((3, 16)),
            dma((3, 16)),
            *weight,
            *weight,
            *weight,
            *weight,
        ],
        compiler_params=pltpu.CompilerParams(
            collective_id=0, has_side_effects=True, vmem_limit_bytes=56 << 20
        ),
    )(*args)


def last_kernel(*refs):
    given, results, held, sems = refs[:10], refs[10:20], refs[20:30], refs[30]
    into = [pltpu.make_async_copy(given[n], held[n], sems.at[0, n]) for n in range(10)]
    out = [pltpu.make_async_copy(held[n], results[n], sems.at[1, n]) for n in range(10)]
    for copy in into:
        copy.start()
    for n in range(10):
        into[n].wait()
        out[n].start()
    for copy in out:
        copy.wait()


def shards(*args):
    return pl.pallas_call(
        last_kernel,
        out_shape=OUTS,
        in_specs=[pl.BlockSpec(memory_space=pl.ANY)] * 10,
        out_specs=tuple(pl.BlockSpec(memory_space=pl.ANY) for _ in OUTS),
        scratch_shapes=[pltpu.VMEM(one.shape, one.dtype) for one in OUTS]
        + [pltpu.SemaphoreType.DMA((2, 10))],
    )(*call_first(*args))


def solution(mesh):
    placed = (
        P(("ctx", "mp"), None),
        P("ctx", "mp"),
        P(("ctx", "mp"), None),
        P(None, "mp"),
        P(None, "mp"),
        P("mp", None, None),
        P("mp"),
        P("mp", None, None),
        P("mp"),
        P("mp"),
        P("mp", None),
        P("mp"),
        P(None, "mp"),
    )
    return jax.shard_map(
        shards,
        mesh=mesh,
        in_specs=placed,
        out_specs=(
            P(("ctx", "mp"), None),
            P("ctx", "mp"),
            P("ctx", "mp"),
            P("mp", "ctx"),
            P(None, "mp"),
            P("mp", None, None),
            P("mp"),
            P("mp", None, None),
            P("mp"),
            P("mp"),
        ),
        check_vma=False,
    )
```

```python
import jax
import jax.numpy as jnp
from jax import lax
from jax.experimental import pallas as pl
from jax.experimental.pallas import tpu as pltpu
from jax.sharding import PartitionSpec as P

MESH = pl.DeviceIdType.MESH
F32 = jnp.float32
BF16 = jnp.bfloat16
NMP = 8
SEG = 32
CH = 512
DM = 4096
HALF = DM // 2


def matmul_tn(left, right):
    return lax.dot_general(left, right, (((0,), (0,)), ((), ())), preferred_element_type=F32)


def matmul_nt(left, right):
    return lax.dot_general(left, right, (((1,), (1,)), ((), ())), preferred_element_type=F32)


def to_segments(value):
    return jnp.transpose(value.reshape(NMP, SEG, CH), (1, 0, 2))


def from_segments(value):
    return jnp.transpose(value, (1, 0, 2)).reshape(NMP * SEG, CH)


def remote(src, dst, send_sem, recv_sem, device):
    return pltpu.make_async_remote_copy(
        src_ref=src,
        dst_ref=dst,
        send_sem=send_sem,
        recv_sem=recv_sem,
        device_id=device,
        device_id_type=MESH,
    )


class Place:
    def __init__(self):
        self.c = lax.axis_index("ctx")
        self.m = lax.axis_index("mp")
        self.k = lax.rem(self.c, 2)
        self.x = lax.rem(lax.div(self.c, 2), 4)
        self.y = lax.div(self.c, 8)

    def chip(self, y, x, k):
        return (y * 8 + x * 2 + k, self.m)

    def other_core(self):
        return self.chip(self.y, self.x, 1 - self.k)

    def along_x(self, step):
        return self.chip(self.y, lax.rem(self.x + step, 4), self.k)

    def along_y(self, step):
        return self.chip(lax.rem(self.y + step, 4), self.x, self.k)

    def along_z(self, step):
        return (self.c, lax.rem(self.m + step, NMP))

    def along_ctx(self, step):
        return (lax.rem(self.c + step, 32), self.m)


class Gather:
    def __init__(self, place, buf, send_sem, recv_sem):
        self.p, self.buf, self.ss, self.rs = place, buf, send_sem, recv_sem

    def view(self, d, s, part):
        step = (NMP - s) if d == 0 else s
        return self.buf.at[lax.rem(self.p.m + step, NMP), :, pl.ds(part * HALF, HALF)]

    def copy(self, d, s, part, at):
        view = self.view(d, at, part)
        to = self.p.along_z(1 if d == 0 else NMP - 1)
        return remote(view, view, self.ss.at[d, s, part], self.rs.at[d, s, part], to)

    def present(self, d, s, part):
        return s < 3 or part == d

    def send(self, s):
        for part in (0, 1):
            for d in (0, 1):
                if self.present(d, s, part):
                    self.copy(d, s, part, s).start()

    def arrive(self, s):
        for part in (0, 1):
            for d in (0, 1):
                if self.present(d, s, part):
                    self.copy(d, s, part, s + 1).wait_recv()
                    if s < 3 and self.present(d, s + 1, part):
                        self.copy(d, s + 1, part, s + 1).start()

    def sent(self):
        for s in range(4):
            for part in (0, 1):
                for d in (0, 1):
                    if self.present(d, s, part):
                        self.copy(d, s, part, s).wait_send()


class Fold:
    def __init__(self, place, core, row, col, send_sem, recv_sem):
        self.p = place
        self.slots = (core, row, col)
        self.ss, self.rs = send_sem, recv_sem

    def copies(self, which, arriving):
        p, slots = self.p, self.slots[which]
        mine = (p.k, p.x, p.y)[which]
        size = 2 if which == 0 else 4
        base = (0, 1, 4)[which]
        found = []
        for o in range(1, size):
            to = p.other_core() if which == 0 else (p.along_x(o) if which == 1 else p.along_y(o))
            slot = slots.at[lax.rem(mine + size - o, size) if arriving else mine]
            sems = self.ss.at[base + o - 1], self.rs.at[base + o - 1]
            found.append(remote(slot, slot, *sems, to))
        return found

    def start(self, which, value):
        self.slots[which][(self.p.k, self.p.x, self.p.y)[which]] = value
        for copy in self.copies(which, False):
            copy.start()

    def finish(self, which):
        for copy in self.copies(which, True):
            copy.wait_recv()

    def drain(self):
        for which in range(3):
            for copy in self.copies(which, False):
                copy.wait_send()


class Everyone:
    def __init__(self, place, slots, send_sem, recv_sem):
        self.p, self.slots, self.ss, self.rs = place, slots, send_sem, recv_sem

    def copy(self, o, owner):
        slot = self.slots.at[owner]
        return remote(slot, slot, self.ss.at[o], self.rs.at[o], self.p.along_ctx(o))

    def start(self, value):
        self.slots[self.p.c] = value

        def one(t, carry):
            self.copy(1 + lax.rem(t + 17, 31), self.p.c).start()
            return carry

        lax.fori_loop(0, 31, one, 0)

    def finish(self):
        def one(o, carry):
            self.copy(o, lax.rem(self.p.c + 32 - o, 32)).wait_recv()
            return carry

        lax.fori_loop(1, 32, one, 0)

    def drain(self):
        def one(o, carry):
            self.copy(o, self.p.c).wait_send()
            return carry

        lax.fori_loop(1, 32, one, 0)


class CorePair:
    def __init__(self, place, src, dst, send_sem, recv_sem):
        self.copy = remote(src, dst, send_sem, recv_sem, place.other_core())
        self.start, self.finish, self.drain = (
            self.copy.start, self.copy.wait_recv, self.copy.wait_send
        )


class CoreColumns:
    def __init__(self, place, own, other, send_sem, recv_sem):
        self.p, self.own, self.other = place, own, other
        self.ss, self.rs = send_sem, recv_sem
        self.whole = remote(other, other, send_sem, recv_sem, place.other_core())

    def start(self):
        def one(j, carry):
            src = pl.ds(pl.multiple_of((2 * j + 1 - self.p.k) * 128, 128), 128)
            dst = pl.ds(pl.multiple_of(j * 128, 128), 128)
            remote(
                self.own.at[:, :, src], self.other.at[:, :, dst], self.ss, self.rs,
                self.p.other_core(),
            ).start()
            return carry

        lax.fori_loop(0, 16, one, 0)

    def finish(self):
        self.whole.wait_recv()

    def drain(self):
        self.whole.wait_send()


class WeightSum:
    def __init__(self, place, first_x, lhs, own, other, refs):
        self.p, self.first_x = place, first_x
        self.lhs, self.own, self.other = lhs, own, other
        (self.out, self.mine, self.relay, self.ring, self.q, self.relay2, self.ring2,
         self.ss, self.rs, self.ss2, self.rs2) = refs
        self.ia, self.ib = (place.x, place.y) if first_x else (place.y, place.x)
        self.rows = pl.ds(0 if first_x else 256, 256)

    def along(self, first, step):
        return self.p.along_x(step) if first == self.first_x else self.p.along_y(step)

    def columns(self, distance, o):
        pa, pb = lax.rem(self.ia + distance, 4), lax.rem(self.ib + o, 4)
        j = pb * 4 + pa if self.first_x else pa * 4 + pb
        here = pl.ds(pl.multiple_of((2 * j + self.p.k) * 128, 128), 128)
        there = pl.ds(pl.multiple_of(j * 128, 128), 128)
        return (
            self.own[:, :, here].reshape(256, 128), self.other[:, :, there].reshape(256, 128)
        )

    def products(self, one, two):
        one, two = self.columns(*one), self.columns(*two)
        both = [
            jnp.dot(
                self.lhs[n, self.rows, :], jnp.concatenate([one[n], two[n]], 1),
                preferred_element_type=F32,
            )
            for n in (0, 1)
        ]
        both = both[0] + both[1]
        return both[:, :128], both[:, 128:]

    def copy(self, kind, o):
        side = lax.rem(o, 2) if kind != 1 else 1 - lax.rem(o, 2)
        target = self.relay.at[o] if kind == 0 else self.ring.at[kind - 1, o]
        return remote(
            self.out.at[kind, o], target, self.ss.at[kind, o], self.rs.at[kind, o],
            self.along(True, 1 + 2 * side),
        )

    def send_relay(self, o):
        for n, value in enumerate(self.products((2, o), (2, o + 1))):
            self.out[0, o + n] = value.astype(BF16)
            self.copy(0, o + n).start()

    def fresh(self, o, value):
        self.out[1, o] = value.astype(BF16)
        self.copy(1, o).start()

    def joined(self, o, value):
        self.copy(0, o).wait_recv()
        self.out[2, o] = (value + self.relay[o].astype(F32)).astype(BF16)
        self.copy(2, o).start()

    def send_fresh(self):
        for o, value in zip((3, 2), self.products((1, 3), (3, 2))):
            self.fresh(o, value)

    def send_joined(self):
        for o, value in zip((2, 3), self.products((1, 2), (3, 3))):
            self.joined(o, value)

    def send_others(self, o):
        far = 2 * lax.rem(o, 2)
        values = self.products((3 - far, o), (1 + far, o))
        self.fresh(o, values[0])
        self.joined(o, values[1])

    def keep(self, o):
        for n, value in enumerate(self.products((0, o), (0, o + 1))):
            self.mine[o + n] = value

    def total(self, o):
        for kind in (1, 2):
            self.copy(kind, o).wait_recv()
        return self.mine[o] + self.ring[0, o].astype(F32) + self.ring[1, o].astype(F32)

    def halves(self, which):
        return remote(
            self.q.at[1, pl.ds(128 * which, 128), :], self.relay2.at[which], self.ss2.at[which],
            self.rs2.at[which], self.along(False, 1 + 2 * which),
        )

    def ends(self, which):
        return remote(
            self.q.at[2 * which], self.ring2.at[which],
            self.ss2.at[2 + which], self.rs2.at[2 + which], self.along(False, 1 + 2 * which),
        )

    def turn(self):
        self.q[1] = self.total(2).astype(BF16)
        for which in (0, 1):
            self.halves(which).start()

    def join(self):
        for which in (0, 1):
            value = self.total(1 + 2 * which)
            self.halves(which).wait_recv()
            met = pl.ds(128 * which, 128)
            rest = slice(128, 256) if which == 0 else slice(0, 128)
            same = slice(0, 128) if which == 0 else slice(128, 256)
            self.q[2 * which, met, :] = (value[same] + self.relay2[which].astype(F32)).astype(BF16)
            self.q[2 * which, pl.ds(128 - 128 * which, 128), :] = value[rest].astype(BF16)
            self.ends(which).start()

    def finish(self, result, turned):
        value = self.total(0)
        for which in (0, 1):
            self.ends(which).wait_recv()
        value = value + self.ring2[0].astype(F32) + self.ring2[1].astype(F32)
        if turned:
            result[:, self.rows] = value.T
        else:
            result[self.rows, :] = value

    def drain(self):
        def one(o, carry):
            for kind in range(3):
                self.copy(kind, o).wait_send()
            return carry

        lax.fori_loop(0, 4, one, 0)
        for which in (0, 1):
            self.halves(which).wait_send()
            self.ends(which).wait_send()


class WeightSums:
    def __init__(self, *sums):
        self.sums = sums

    def twice(self, name, of):
        def one(t, carry):
            for one_sum in self.sums:
                getattr(one_sum, name)(of(t))
            return carry

        lax.fori_loop(0, 2, one, 0)

    def relay(self):
        self.twice("send_relay", lambda t: 2 - 2 * t)

    def fresh(self):
        for one_sum in self.sums:
            one_sum.send_fresh()

    def joined(self):
        for one_sum in self.sums:
            one_sum.send_joined()

    def others(self):
        self.twice("send_others", lambda t: 1 - t)

    def keep(self):
        self.twice("keep", lambda t: 2 * t)

    def turn(self):
        for one_sum in self.sums:
            one_sum.turn()

    def join(self):
        for one_sum in self.sums:
            one_sum.join()

    def finish(self, result, turned):
        for one_sum in self.sums:
            one_sum.finish(result, turned)

    def drain(self):
        for one_sum in self.sums:
            one_sum.drain()


class RowSum:
    def __init__(self, place, parts, came, send_sem, recv_sem):
        self.p, self.parts, self.came = place, parts, came
        self.ss, self.rs = send_sem, recv_sem

    def block(self, d, s):
        return lax.rem(self.p.m + (4 - s if d == 0 else 4 + s), NMP)

    def copy(self, d, s, part):
        cols = pl.ds(part * HALF, HALF)
        return remote(
            self.parts.at[self.block(d, s), :, cols], self.came.at[d, s, :, cols],
            self.ss.at[d, s, part], self.rs.at[d, s, part], self.p.along_z(1 if d == 0 else NMP - 1),
        )

    def begin(self, part):
        self.copy(part, 0, part).start()
        self.copy(1 - part, 1, part).start()

    def step(self, s):
        for fresh in (True, False):
            for d in (0, 1):
                part = 1 - d if fresh else d
                if fresh and s == 1:
                    continue
                self.copy(d, s - 1, part).wait_recv()
                cols = pl.ds(part * HALF, HALF)
                to = self.block(d, s)
                self.parts[to, :, cols] = (
                    self.parts[to, :, cols].astype(F32) + self.came[d, s - 1, :, cols].astype(F32)
                ).astype(BF16)
                self.copy(d, s, part).start()

    def finish(self, result):
        for d in (0, 1):
            for part in (0, 1):
                self.copy(d, 3, part).wait_recv()
        result[...] = (
            self.parts[self.p.m].astype(F32)
            + self.came[0, 3].astype(F32)
            + self.came[1, 3].astype(F32)
        ).astype(BF16)

    def drain(self):
        for d in (0, 1):
            for s in range(4):
                for part in (0, 1):
                    if s > 0 or part == d:
                        self.copy(d, s, part).wait_send()


class GateSum:
    def __init__(self, place, parts, row, total, send_sem, recv_sem):
        self.p = place
        self.parts, self.row, self.total = parts, row, total
        self.ss, self.rs = send_sem, recv_sem
        self.chip = lax.div(place.c, 2)
        view = total.at[place.k]
        self.pair = remote(view, view, send_sem.at[2, 0], recv_sem.at[2, 0], place.other_core())

    def rows(self, chip):
        return pl.ds(pl.multiple_of(chip * 16, 16), 16)

    def copy(self, which, o, arriving):
        owner = lax.rem(self.chip + 16 - o, 16) if arriving else self.chip
        peer = lax.rem(self.chip + o, 16)
        if which == 0:
            src, dst = self.parts.at[:, self.rows(peer), :], self.row.at[owner]
        else:
            src = dst = self.total.at[self.p.k, :, self.rows(owner), :]
        return remote(
            src, dst, self.ss.at[which, o], self.rs.at[which, o], (peer * 2 + self.p.k, self.p.m)
        )

    def each(self, act):
        def one(o, carry):
            act(o)
            return carry

        lax.fori_loop(1, 16, one, 0)

    def start(self, which):
        if which == 2:
            self.pair.start()
            return
        if which == 0:
            self.row[self.chip] = self.parts[:, self.rows(self.chip), :]
        else:
            total = self.row[0].astype(F32)
            for o in range(1, 16):
                total = total + self.row[o].astype(F32)
            self.total[self.p.k, :, self.rows(self.chip), :] = total.astype(BF16)
        self.each(lambda o: self.copy(which, o, False).start())

    def finish(self, which):
        if which == 2:
            view = self.total.at[1 - self.p.k]
            remote(view, view, self.ss.at[2, 0], self.rs.at[2, 0], self.p.other_core()).wait_recv()
        else:
            self.each(lambda o: self.copy(which, o, True).wait_recv())

    def drain(self):
        for which in (0, 1):
            self.each(lambda o: self.copy(which, o, False).wait_send())
        self.pair.wait_send()


def minus_expm1(v):
    series = 1.0 + v * (1.0 / 8.0)
    for n in (7, 6, 5, 4, 3, 2):
        series = 1.0 + v * (1.0 / n) * series
    return jnp.where(v > -0.35, -v * series, 1.0 - jnp.exp(v))


def enter(place, partners):
    barrier = pltpu.get_barrier_semaphore()
    for device in partners:
        pl.semaphore_signal(barrier, inc=1, device_id=device, device_id_type=MESH)
    pl.semaphore_wait(barrier, len(partners))


def first_kernel(
    tokens, branch, out_grad, w_in, conv_w, gate_a_h, gate_a_b, gate_i_h, gate_i_b, decay_param, w_out,
    state_init, conv_history,
    tokens_grad, branch_grad, w_in_grad, w_out_grad, conv_grad, gate_a_grad, bias_a_grad, gate_i_grad,
    bias_i_grad, decay_grad,
    gate_total, w_in_t, w_out_t, pieces,
    tok, og, proj, gated, conv_b, ri, tok_o, og_o, conv_o, ri_o, gate_p, gate_row,
    lhs_g, lhs_p, parts, came, branch_v, gate_a, gate_i,
    w_in_v, w_out_v, acc, px, cv, rg, ig, dk, rem, hs, cp, ep, br, gp, cg, kv, edge_s, edge_r, edge_c,
    all_s, all_b, core_m, row_m, col_m,
    w_sem, ts, tr, gs, gr, fs, fr, bs, brs, es, er, ms, mr, zs, zr, ps, pr, qs, qr,
    *sums,
):
    p = Place()
    loads = [
        pltpu.make_async_copy(src, dst, w_sem.at[n])
        for n, (src, dst) in enumerate(
            (
                (tokens, tok.at[p.m]),
                (out_grad, og.at[p.m]),
                (branch, branch_v),
                (gate_a_h, gate_a),
                (gate_i_h, gate_i),
                (w_in, w_in_v),
                (w_out, w_out_v),
            )
        )
    ]
    for load in loads:
        load.start()
    enter(p, [p.along_z(1), p.along_z(NMP - 1)] + [p.along_ctx(o) for o in range(1, 32)])
    tokens_in = Gather(p, tok, ts, tr)
    grads_in = Gather(p, og, gs, gr)
    loads[0].wait()
    tokens_in.send(0)

    def wide(row):
        return jnp.broadcast_to(row.reshape(1, CH), (8, CH))

    taps = conv_w[...].astype(F32)
    for j in range(4):
        kv[j] = wide(taps[j : j + 1])
    kv[4] = wide(gate_a_b[...])
    kv[5] = wide(gate_i_b[...])
    negative = wide(-decay_param[...])
    small_exp = jnp.exp(-jnp.abs(negative))
    one_more = 1.0 + small_exp
    gap = one_more - 1.0
    log_part = jnp.where(
        gap == 0.0, small_exp, jnp.log(one_more) * (small_exp / jnp.where(gap == 0.0, 1.0, gap))
    )
    kv[6] = jnp.maximum(negative, 0.0) + log_part
    loads[1].wait()
    loads[2].wait()
    br[...] = to_segments(branch_v[...].astype(F32))

    tokens_in.arrive(0)
    for load in loads[3:]:
        load.wait()
    tokens_in.arrive(1)

    def turn_weights(n, carry):
        at = pl.ds(pl.multiple_of(n * 512, 512), 512)
        w_out_t[at, :] = w_out_v[:, at].T
        w_in_t[:, at] = w_in_v[at, :].T
        return carry

    tokens_in.arrive(2)
    grads_in.send(0)
    lax.fori_loop(0, 8, turn_weights, 0)
    tokens_in.arrive(3)
    other_tokens = CoreColumns(p, tok, tok_o, ps.at[0], pr.at[0])
    other_grads = CoreColumns(p, og, og_o, ps.at[1], pr.at[1])
    other_conv = CorePair(p, conv_b, conv_o, ps.at[2], pr.at[2])
    other_gated = CorePair(p, lhs_g.at[0], lhs_g.at[1], ps.at[3], pr.at[3])
    other_proj = CorePair(p, lhs_p.at[0], lhs_p.at[1], ps.at[4], pr.at[4])
    other_gate = CorePair(p, ri.at[1 - p.k], ri_o, ps.at[5], pr.at[5])
    pairs = [other_tokens, other_grads, other_conv, other_gated, other_proj, other_gate]
    w_out_sum = WeightSums(
        WeightSum(p, True, lhs_g, og, og_o, sums[:11]),
        WeightSum(p, False, lhs_g, og, og_o, sums[11:22]),
    )
    w_in_sum = WeightSums(
        WeightSum(p, True, lhs_p, tok, tok_o, sums[22:33]),
        WeightSum(p, False, lhs_p, tok, tok_o, sums[33:]),
    )
    row_sum = RowSum(p, parts, came, zs, zr)
    gate_sum = GateSum(p, gate_p, gate_row, gate_total, qs, qr)
    total_sum = Fold(p, core_m, row_m, col_m, ms, mr)
    other_tokens.start()

    acc[...] = jnp.zeros_like(acc)

    def project(n, carry):
        at = pl.ds(pl.multiple_of(n * 1024, 1024), 1024)
        acc[...] += jnp.dot(
            tok[:, :, at].reshape(256, 1024), w_in_v[at, :], preferred_element_type=F32
        )
        return carry

    lax.fori_loop(0, 4, project, 0)
    edge_s[...] = acc[pl.ds(240, 16), :].astype(BF16)
    forward_edge = remote(edge_s, edge_r, es.at[0], er.at[0], p.along_ctx(1))
    forward_edge.start()
    grads_in.arrive(0)
    px[pl.ds(3, 32)] = to_segments(acc[...].astype(BF16).astype(F32))

    lane8 = lax.broadcasted_iota(jnp.int32, (8, CH), 0)
    forward_edge.wait_recv()
    first = p.c == 0
    before = edge_r[...].astype(F32)[13:16]
    before = jnp.where(first, conv_history[...].astype(F32), before)
    for j in range(3):
        turned = pltpu.roll(px[32 + j], 1, 0)
        px[j] = jnp.where(lane8 == 0, wide(before[j : j + 1]), turned)

    def convolve(n, carry):
        total = kv[0] * px[pl.ds(2 * n + 3, 2)]
        for j in (1, 2, 3):
            total = total + kv[j] * px[pl.ds(2 * n + 3 - j, 2)]
        rounded = total.astype(BF16)
        cv[pl.ds(2 * n, 2)] = rounded.astype(F32)
        conv_b[pl.ds(pl.multiple_of(16 * n, 16), 16), :] = rounded.reshape(16, CH)
        return carry

    lax.fori_loop(0, 16, convolve, 0)
    other_conv.start()
    for b in (0, 1):
        cols = pl.ds(b * 256, 256)
        rg[:, :, cols] = jnp.dot(
            conv_b[:, cols], gate_a[b], preferred_element_type=F32
        ).reshape(32, 8, 256)
        ig[:, :, cols] = jnp.dot(
            conv_b[:, cols], gate_i[b], preferred_element_type=F32
        ).reshape(32, 8, 256)

    def gates(n, carry):
        h, c = carry
        at = pl.ds(2 * n, 2)
        recur = jax.nn.sigmoid(rg[at] + kv[4])
        inp = jax.nn.sigmoid(ig[at] + kv[5])
        log_decay = -8.0 * recur * kv[6]
        decay = jnp.exp(log_decay)
        remain = minus_expm1(2.0 * log_decay)
        rg[at] = recur
        ig[at] = inp
        dk[at] = decay
        rem[at] = remain
        driven = jnp.sqrt(remain) * inp * cv[at]
        for t in (0, 1):
            h = decay[t] * h + driven[t]
            c = decay[t] * c
            hs[2 * n + 1 + t] = h
            cp[2 * n + t] = c
        return h, c

    h, c = lax.fori_loop(0, 16, gates, (jnp.zeros((8, CH), F32), jnp.ones((8, CH), F32)))
    c_seg = c
    for sh in (1, 2, 4):
        ok = lane8 >= sh
        h, c = (
            jnp.where(ok, h + c * pltpu.roll(h, sh, 0), h),
            jnp.where(ok, c * pltpu.roll(c, sh, 0), c),
        )
    c_before = jnp.where(lane8 == 0, 1.0, pltpu.roll(c, 1, 0))
    h_before = jnp.where(lane8 == 0, 0.0, pltpu.roll(h, 1, 0))
    states = Everyone(p, all_s, fs, fr)
    states.start(jnp.concatenate([c[7:8], h[7:8]], 0))

    def suffix(n, e):
        ep[31 - n] = e
        return e * dk[31 - n]

    lax.fori_loop(0, 32, suffix, jnp.ones((8, CH), F32))
    grads_in.arrive(1)

    def coefficients(n, carry):
        at = pl.ds(2 * n, 2)
        decay, remain, inp, recur, wide_conv = dk[at], rem[at], ig[at], rg[at], cv[at]
        scaler = jnp.sqrt(remain)
        inner = inp * wide_conv
        cg[at] = 2.0 * decay * decay * inner / jnp.sqrt(jnp.maximum(4.0 * remain, 1e-06))
        rem[at] = scaler * inp
        ig[at] = inner * scaler * (1.0 - inp)
        rg[at] = -8.0 * recur
        cv[at] = kv[6] * (1.0 - recur)
        return carry

    lax.fori_loop(0, 16, coefficients, 0)
    grads_in.arrive(2)
    there = (0, 1, 7, 2, 6, 3, 5)

    def place_of(offset):
        return lax.rem(p.m + offset, NMP)

    def early_product(n, carry):
        at = pl.ds(pl.multiple_of(n * 1024, 1024), 1024)
        rows = jnp.concatenate([og[place_of(o), :, at] for o in there], 0)
        value = jnp.dot(rows, w_out_t[at, :], preferred_element_type=F32).reshape(7, 32, CH)
        pieces[pl.ds(0, 7)] = jnp.where(n == 0, value, pieces[pl.ds(0, 7)] + value)
        return carry

    def late_product(n, carry):
        at = pl.ds(pl.multiple_of(n * 1024, 1024), 1024)
        return carry + jnp.dot(og[place_of(4), :, at], w_out_t[at, :], preferred_element_type=F32)

    pieces[...] = jnp.zeros_like(pieces)
    lax.fori_loop(0, 4, early_product, 0)
    for n, offset in enumerate(there):
        acc[pl.ds(pl.multiple_of(place_of(offset) * 32, 32), 32), :] = pieces[n]
    states.finish()
    state = state_init[...].reshape(1, CH)
    for o in range(32):
        one = all_s[o]
        state = jnp.where(o < p.c, one[0:1] * state + one[1:2], state)
    state = wide(state)
    seg_state = h_before + c_before * state
    hs[0] = seg_state

    def finish_states(n, carry):
        at = pl.ds(2 * n, 2)
        value = hs[pl.ds(2 * n + 1, 2)] + cp[at] * seg_state
        hs[pl.ds(2 * n + 1, 2)] = value
        cp[at] = value * br[at]
        rate_part = rg[at] * (hs[at] * dk[at] - cg[at])
        rg[at] = rate_part
        cv[at] = rate_part * cv[at]
        return carry

    lax.fori_loop(0, 16, finish_states, 0)
    gated[...] = from_segments(cp[...]).astype(BF16)
    lhs_g[0] = gated[...].T
    other_gated.start()

    grads_in.arrive(3)
    other_grads.start()
    acc[pl.ds(pl.multiple_of(place_of(4) * 32, 32), 32), :] = lax.fori_loop(
        0, 4, late_product, jnp.zeros((32, CH), F32)
    )
    gp[...] = to_segments(acc[...])

    def backward(n, b):
        i = 31 - n
        g = gp[i]
        cp[i] = g * hs[i + 1]
        a = g * br[i] + b
        gp[i] = a
        return dk[i] * a

    b = lax.fori_loop(0, 32, backward, jnp.zeros((8, CH), F32))
    c = c_seg
    for sh in (1, 2, 4):
        ok = lane8 < 8 - sh
        b, c = (
            jnp.where(ok, b + c * pltpu.roll(b, 8 - sh, 0), b),
            jnp.where(ok, c * pltpu.roll(c, 8 - sh, 0), c),
        )
    c_after = jnp.where(lane8 == 7, 1.0, pltpu.roll(c, 7, 0))
    b_after = jnp.where(lane8 == 7, 0.0, pltpu.roll(b, 7, 0))
    adjoints = Everyone(p, all_b, bs, brs)
    adjoints.start(b[0:1])
    other_gated.finish()
    other_grads.finish()
    w_out_sum.relay()
    branch_grad[...] = from_segments(cp[...]).astype(BF16)
    w_out_sum.fresh()
    adjoints.finish()
    later = jnp.zeros((1, CH), F32)
    for o in reversed(range(32)):
        later = jnp.where(o > p.c, all_b[o] + all_s[o][0:1] * later, later)
    later = wide(later)
    seg_later = b_after + c_after * later

    def gate_grads(n, carry):
        sum_a, sum_i, sum_r = carry
        at = pl.ds(2 * n, 2)
        adjoint = gp[at] + ep[at] * seg_later
        recur_pre = (adjoint * cv[at]).astype(BF16)
        input_pre = (adjoint * ig[at]).astype(BF16)
        flat = pl.ds(pl.multiple_of(16 * n, 16), 16)
        ri[0, flat, :] = recur_pre.reshape(16, CH)
        ri[1, flat, :] = input_pre.reshape(16, CH)
        cg[at] = adjoint * rem[at]
        return (
            sum_a + jnp.sum(recur_pre.astype(F32), 0),
            sum_i + jnp.sum(input_pre.astype(F32), 0),
            sum_r + jnp.sum(adjoint * rg[at], 0),
        )

    zero = jnp.zeros((8, CH), F32)
    def through_gates(low, high):
        rows = pl.ds(low * 8, (high - low) * 8)
        for b in (0, 1):
            cols = pl.ds(b * 256, 256)
            cg[pl.ds(low, high - low), :, cols] += (
                matmul_nt(ri[0, rows, cols], gate_a[b]) + matmul_nt(ri[1, rows, cols], gate_i[b])
            ).reshape(high - low, 8, 256)

    first_sums = lax.fori_loop(0, 2, gate_grads, (zero, zero, zero))
    through_gates(0, 4)
    backward_edge = remote(cg.at[pl.ds(0, 3)], edge_c, es.at[1], er.at[1], p.along_ctx(31))
    backward_edge.start()
    sum_a, sum_i, sum_r = lax.fori_loop(2, 16, gate_grads, first_sums)
    other_gate.start()
    through_gates(4, 32)
    w_out_sum.joined()
    w_out_sum.others()
    backward_edge.wait_recv()
    for j in range(3):
        turned = pltpu.roll(cg[j], 7, 0)
        came = jnp.where(p.c == 31, 0.0, wide(edge_c[j][0:1]))
        cg[32 + j] = jnp.where(lane8 == 7, came, turned)

    def proj_grads(n, carry):
        at = pl.ds(2 * n, 2)
        own = cg[at]
        total = kv[0] * own
        for j in (1, 2, 3):
            total = total + kv[j] * cg[pl.ds(2 * n + j, 2)]
        cp[at] = total
        return tuple(
            carry[j] + jnp.sum(own * px[pl.ds(2 * n + 3 - j, 2)], 0) for j in range(4)
        )

    tap_sums = lax.fori_loop(0, 16, proj_grads, (zero, zero, zero, zero))
    proj[...] = from_segments(cp[...]).astype(BF16)
    lhs_p[0] = proj[...].T
    other_proj.start()
    for part in (0, 1):

        def spread(n, carry):
            at = pl.ds(pl.multiple_of(n * 512, 512), 512)
            value = jnp.dot(proj[...], w_in_t[:, at], preferred_element_type=F32)
            parts[:, :, at] = value.astype(BF16).reshape(8, 32, 512)
            return carry

        lax.fori_loop(part * 4, part * 4 + 4, spread, 0)
        row_sum.begin(part)
        if part == 0:
            other_conv.finish()
            other_gate.finish()
            for b in (0, 1):
                cols = pl.ds(b * 256, 256)
                gate_p[b] = (
                    matmul_tn(conv_b[:, cols], ri[p.k, :, cols])
                    + matmul_tn(conv_o[:, cols], ri_o[:, cols])
                ).astype(BF16)
            gate_sum.start(0)
    rows = [jnp.sum(v, 0, keepdims=True) for v in (*tap_sums, sum_r, sum_a, sum_i)]
    total_sum.start(0, jnp.concatenate(rows + [jnp.zeros((1, CH), F32)], 0))
    other_tokens.finish()
    other_proj.finish()
    w_in_sum.relay()
    w_in_sum.fresh()
    row_sum.step(1)
    w_out_sum.keep()
    w_out_sum.turn()
    w_in_sum.joined()
    w_in_sum.others()
    gate_sum.finish(0)
    gate_sum.start(1)
    row_sum.step(2)
    total_sum.finish(0)
    total_sum.start(1, core_m[0] + core_m[1])
    w_in_sum.keep()
    w_in_sum.turn()
    w_out_sum.join()
    row_sum.step(3)
    gate_sum.finish(1)
    gate_sum.start(2)
    w_in_sum.join()
    total_sum.finish(1)
    total_sum.start(2, row_m[0] + row_m[1] + row_m[2] + row_m[3])
    gates_out = (gate_a_grad, gate_i_grad)
    w_out_sum.finish(w_out_grad, False)
    w_in_sum.finish(w_in_grad, True)
    total_sum.finish(2)
    small = col_m[0] + col_m[1] + col_m[2] + col_m[3]
    conv_grad[...] = small[0:4]
    bias_a_grad[...] = small[5]
    bias_i_grad[...] = small[6]
    decay_grad[...] = small[4] * -jax.nn.sigmoid(-decay_param[...])
    gate_sum.finish(2)
    for n in (0, 1):
        gates_out[n][...] = gate_total[n].astype(F32)
    row_sum.finish(tokens_grad)
    for used in (states, adjoints, total_sum, w_out_sum, w_in_sum, row_sum, gate_sum, *pairs):
        used.drain()
    tokens_in.sent()
    grads_in.sent()
    forward_edge.wait_send()
    backward_edge.wait_send()


def result(shape, dtype):
    return jax.ShapeDtypeStruct(shape, dtype)


OUTS = (
    result((32, DM), BF16),
    result((256, CH), BF16),
    result((128, CH), F32),
    result((CH, 128), F32),
    result((4, CH), F32),
    result((2, 256, 256), F32),
    result((CH,), F32),
    result((2, 256, 256), F32),
    result((CH,), F32),
    result((CH,), F32),
)


def call_first(*args):
    def vm(shape, dtype):
        return pltpu.VMEM(shape, dtype)

    seg = (32, 8, CH)
    tile = (8, CH)
    dma = pltpu.SemaphoreType.DMA
    outs = OUTS
    weight = [
        vm((3, 4, 256, 128), BF16),
        vm((4, 256, 128), F32),
        vm((4, 256, 128), BF16),
        vm((2, 4, 256, 128), BF16),
        vm((3, 256, 128), BF16),
        vm((2, 128, 128), BF16),
        vm((2, 256, 128), BF16),
        dma((3, 4)),
        dma((3, 4)),
        dma((4,)),
        dma((4,)),
    ]
    big = {0, 1, 2, 3, 5, 7, 10}
    return pl.pallas_call(
        first_kernel,
        out_shape=outs,
        in_specs=[
            pl.BlockSpec(memory_space=pl.ANY if n in big else pltpu.VMEM) for n in range(13)
        ],
        out_specs=tuple(pl.BlockSpec(memory_space=pltpu.VMEM) for _ in outs),
        scratch_shapes=[
            vm((2, 2, 256, 256), BF16),
            vm((CH, DM), BF16),
            vm((DM, CH), BF16),
            vm((8, 32, CH), F32),
            vm((8, 32, DM), BF16),
            vm((8, 32, DM), BF16),
            vm((256, CH), BF16),
            vm((256, CH), BF16),
            vm((256, CH), BF16),
            vm((2, 256, CH), BF16),
            vm((8, 32, HALF), BF16),
            vm((8, 32, HALF), BF16),
            vm((256, CH), BF16),
            vm((256, CH), BF16),
            vm((2, 256, 256), BF16),
            vm((16, 2, 16, 256), BF16),
            vm((2, CH, 256), BF16),
            vm((2, CH, 256), BF16),
            vm((8, 32, DM), BF16),
            vm((2, 4, 32, DM), BF16),
            vm((256, CH), BF16),
            vm((2, 256, 256), BF16),
            vm((2, 256, 256), BF16),
            vm((DM, CH), BF16),
            vm((CH, DM), BF16),
            vm((256, CH), F32),
            vm((35, 8, CH), F32),
            *[vm(seg, F32) for _ in range(5)],
            vm((33, 8, CH), F32),
            *[vm(seg, F32) for _ in range(4)],
            vm((35, 8, CH), F32),
            vm((7, 8, CH), F32),
            vm((16, CH), BF16),
            vm((16, CH), BF16),
            vm((3, 8, CH), F32),
            vm((32, 2, CH), F32),
            vm((32, 1, CH), F32),
            vm((2, *tile), F32),
            vm((4, *tile), F32),
            vm((4, *tile), F32),
            dma((7,)),
            dma((2, 4, 2)),
            dma((2, 4, 2)),
            dma((2, 4, 2)),
            dma((2, 4, 2)),
            dma((32,)),
            dma((32,)),
            dma((32,)),
            dma((32,)),
            dma((2,)),
            dma((2,)),
            dma((7,)),
            dma((7,)),
            dma((2, 4, 2)),
            dma((2, 4, 2)),
            dma((6,)),
            dma((6,)),
            dma((3, 16)),
            dma((3, 16)),
            *weight,
            *weight,
            *weight,
            *weight,
        ],
        compiler_params=pltpu.CompilerParams(
            collective_id=0, has_side_effects=True, vmem_limit_bytes=56 << 20
        ),
    )(*args)


def last_kernel(*refs):
    given, results, held, sems = refs[:10], refs[10:20], refs[20:30], refs[30]
    into = [pltpu.make_async_copy(given[n], held[n], sems.at[0, n]) for n in range(10)]
    out = [pltpu.make_async_copy(held[n], results[n], sems.at[1, n]) for n in range(10)]
    for copy in into:
        copy.start()
    for n in range(10):
        into[n].wait()
        out[n].start()
    for copy in out:
        copy.wait()


def shards(*args):
    return pl.pallas_call(
        last_kernel,
        out_shape=OUTS,
        in_specs=[pl.BlockSpec(memory_space=pl.ANY)] * 10,
        out_specs=tuple(pl.BlockSpec(memory_space=pl.ANY) for _ in OUTS),
        scratch_shapes=[pltpu.VMEM(one.shape, one.dtype) for one in OUTS]
        + [pltpu.SemaphoreType.DMA((2, 10))],
    )(*call_first(*args))


def solution(mesh):
    placed = (
        P(("ctx", "mp"), None),
        P("ctx", "mp"),
        P(("ctx", "mp"), None),
        P(None, "mp"),
        P(None, "mp"),
        P("mp", None, None),
        P("mp"),
        P("mp", None, None),
        P("mp"),
        P("mp"),
        P("mp", None),
        P("mp"),
        P(None, "mp"),
    )
    return jax.shard_map(
        shards,
        mesh=mesh,
        in_specs=placed,
        out_specs=(
            P(("ctx", "mp"), None),
            P("ctx", "mp"),
            P("ctx", "mp"),
            P("mp", "ctx"),
            P(None, "mp"),
            P("mp", None, None),
            P("mp"),
            P("mp", None, None),
            P("mp"),
            P("mp"),
        ),
        check_vma=False,
    )
```
